128 devices in a mesh: sfc: 128 (over z, x, y, core).
Axes of the slice: x: 4, y: 4, z: 4, core: 2. Of those that a mesh axis runs over, the one named last changes fastest.
Arguments:
- tracers: float32 [8192, 16, 512], P('sfc'), may hold values from 0 to 2
- velocity: float32 [8192, 16, 128], P('sfc'), may hold values from -4 to 4
- jacobian: float32 [8192, 16], P('sfc'), may hold values from 0.5 to 2
- elem_nodes: int32 [8192, 16], P('sfc'), may hold values from 0 to 624, as said below
Outputs:
- tracers_out: float32 [8192, 16, 512], P('sfc')
The draws below stay inside these ranges and needn't reach their ends.
Inputs may be any that keep to these rules, and one draw needn't show every extreme that they name: `elem_nodes`: the 64 elements of each block of 64 consecutive rows are those of a square of the element grid, listed in some order: the element at column ex and row ey of the square has, at GLL point 4 j + i, the local node (3 ey + j) * 25 + 3 ex + i.
All inputs are finite; a program needn't handle non-finite values.
Results may differ from the reference program's by a relative error of at most 0.0003.
Values sent between devices are 32-bit elements; how exact they have to be, the bound alone decides.
No kernel may reach another device: no remote copies, remote signals or barrier semaphores. Data moves between devices by JAX's collectives and lax.ppermute only.
A program may use at most 128 MiB of HBM per device.

```python
import math
import jax
import jax.numpy as jnp
import numpy as np
from jax import lax

TT = 8
PX = 8
Q = 8
LEV = 64
ELEMS = 8192
NODE_COLS = 192
NODE_ROWS = 384


def draw_elem_nodes(key, part):
    key = jax.random.fold_in(key, 7)
    per_block = TT * TT
    blocks = ELEMS // per_block
    side = 3 * TT + 1
    block_keys = jax.random.split(key, blocks)

    def ordering(subkey):
        return jax.random.permutation(subkey, per_block)
    orders = jax.vmap(ordering)(block_keys).astype(jnp.int32).reshape(-1)
    element_col = orders % TT
    element_row = orders // TT
    corner = 3 * element_row * side + 3 * element_col
    pattern = (jnp.arange(4, dtype=jnp.int32)[:, None] * side + jnp.arange(4, dtype=jnp.int32)[None, :]).reshape(16)
    return (corner[:, None] + pattern[None, :]).astype(jnp.int32)


def shard_levels(own_key, dims, shards, smallest, largest):
    level = 1.0
    for axis_at, shards_of in shards:
        steps = jax.random.uniform(jax.random.fold_in(jax.random.fold_in(own_key, 6), axis_at), (shards_of,), jnp.float32, smallest / len(shards), largest / len(shards))
        level = level * jnp.repeat(jnp.exp(steps), dims[axis_at] // shards_of).reshape((-1,) + (1,) * (len(dims) - 1 - axis_at))
    return level


def gaussian(key, shape, scale, most, pieces=(), held_as=jnp.bfloat16):
    level = shard_levels(key, shape, pieces, -0.22, 0.18) if pieces else 1.0
    values = jax.random.normal(key, shape, jnp.float32) * scale * level
    return jnp.minimum(jnp.maximum(values, -most), most).astype(held_as)


def setup_inputs(seed: int = 0) -> dict:
    streams_of = jax.random.split(jax.random.key(seed), 5)
    tracers = jnp.clip(2.0 * jax.random.uniform(streams_of[0], (ELEMS, 16, Q * LEV), jnp.float32) ** shard_levels(streams_of[0], (ELEMS, 16, Q * LEV), ((0, 128),), -0.2, 0.2), 0.0, 2.0)
    velocity = gaussian(streams_of[1], (ELEMS, 16, 2 * LEV), 1.0, 4.0, ((0, 128),), jnp.float32)
    jacobian = jnp.clip(jnp.exp(math.log(2.0) - 1.3862944 * jax.random.uniform(streams_of[2], (ELEMS, 16), jnp.float32) ** shard_levels(streams_of[2], (ELEMS, 16), ((0, 128),), -0.2, 0.2)), 0.5, 2.0)
    elem_nodes = draw_elem_nodes(jax.random.fold_in(streams_of[4], 71), 0)
    return {"tracers": tracers, "velocity": velocity, "jacobian": jacobian, "elem_nodes": elem_nodes}


HIGHEST = lax.Precision.HIGHEST
STEP_SIZE = 0.04
DIFFUSION = 0.0001

def gll_tables():
    points = np.array([-1.0, -np.sqrt(0.2), np.sqrt(0.2), 1.0])
    weights = np.array([1.0, 5.0, 5.0, 1.0]) / 6.0
    barycentric = np.array([1.0 / np.prod([points[target] - points[partner] for partner in range(4) if partner != target]) for target in range(4)])
    deriv = np.zeros((4, 4))
    for row_index in range(4):
        for col_index in range(4):
            if row_index != col_index:
                deriv[row_index, col_index] = barycentric[col_index] / barycentric[row_index] / (points[row_index] - points[col_index])
        deriv[row_index, row_index] = -np.sum(deriv[row_index])
    return (jnp.asarray(deriv, jnp.float32), jnp.asarray(np.outer(weights, weights).reshape(16), jnp.float32))

def along_xi(deriv, field):
    shaped = field.reshape(field.shape[0], 4, 4, field.shape[2])
    return jnp.einsum('ai,ejiw->ejaw', deriv, shaped, precision=HIGHEST).reshape(field.shape)

def along_eta(deriv, field):
    shaped = field.reshape(field.shape[0], 4, 4, field.shape[2])
    return jnp.einsum('aj,ejiw->eaiw', deriv, shaped, precision=HIGHEST).reshape(field.shape)

def tendency(deriv, field, wind_xi, wind_eta, metric):
    return -(along_xi(deriv, metric * wind_xi * field) + along_eta(deriv, metric * wind_eta * field)) / metric

def laplace(deriv, field, metric):
    return (along_xi(deriv, metric * along_xi(deriv, field)) + along_eta(deriv, metric * along_eta(deriv, field))) / metric

def limit(values, mass):
    weight = mass[:, :, None]
    element_mean = lax.optimization_barrier(jnp.sum(weight * values, axis=1, keepdims=True)) / lax.optimization_barrier(jnp.sum(weight, axis=1, keepdims=True))
    lowest = lax.optimization_barrier(jnp.min(values, axis=1, keepdims=True))
    positive = jnp.maximum(element_mean, 0.0)
    negative = lowest < 0.0
    denominator = jnp.where(negative, positive - lowest, 1.0)
    scaling = jnp.where(negative, positive / denominator, 1.0)
    return element_mean + scaling * (values - element_mean)

def node_ids(elem_nodes):
    side = 3 * TT + 1
    block = jnp.arange(ELEMS, dtype=jnp.int32) // (TT * TT)
    column = 3 * TT * (block % PX)[:, None] + elem_nodes % side
    row_place = 3 * TT * (block // PX)[:, None] + elem_nodes // side
    wrapped = column == NODE_COLS
    column = jnp.where(wrapped, 0, column)
    row_place = jnp.where(wrapped, row_place + 3 * TT, row_place) % NODE_ROWS
    return (row_place * NODE_COLS + column).astype(jnp.int32)

def reference(tracers, velocity, jacobian, elem_nodes):
    deriv, node_weights = gll_tables()
    mass = jacobian * node_weights
    identity_nodes = node_ids(elem_nodes).reshape(-1)
    count_nodes = NODE_COLS * NODE_ROWS
    width = tracers.shape[2]
    total_mass = jax.ops.segment_sum(mass.reshape(-1), identity_nodes, num_segments=count_nodes)

    def average(field):
        sums = jax.ops.segment_sum((mass[:, :, None] * field).reshape(-1, width), identity_nodes, num_segments=count_nodes)
        return (sums / total_mass[:, None])[identity_nodes].reshape(field.shape)
    levels = velocity.shape[2] // 2
    wind_xi = jnp.tile(velocity[:, :, :levels], (1, 1, Q))
    wind_eta = jnp.tile(velocity[:, :, levels:], (1, 1, Q))
    metric = jacobian[:, :, None]
    section_one = average(limit(tracers + STEP_SIZE * tendency(deriv, tracers, wind_xi, wind_eta, metric), mass))
    section_two = average(limit(0.75 * tracers + 0.25 * (section_one + STEP_SIZE * tendency(deriv, section_one, wind_xi, wind_eta, metric)), mass))
    section_three = average(limit(tracers / 3.0 + 2.0 / 3.0 * (section_two + STEP_SIZE * tendency(deriv, section_two, wind_xi, wind_eta, metric)), mass))
    lap_one = average(laplace(deriv, section_three, metric))
    lap_two = average(laplace(deriv, lap_one, metric))
    return section_three - DIFFUSION * lap_two
```

```python
import functools
import jax
import jax.numpy as jnp
import numpy as np
from jax import lax
from jax.experimental import pallas as pl
from jax.experimental.pallas import tpu as pltpu
from jax.sharding import PartitionSpec as P

TT = 8
PX = 8
STEP_SIZE = 0.04
DIFFUSION = 0.0001
F32 = jnp.float32
VMEM_LIMIT = 48 * 1024 * 1024


def gll_derivative():
    points = np.array([-1.0, -np.sqrt(0.2), np.sqrt(0.2), 1.0])
    bary = np.array(
        [1.0 / np.prod([points[t] - points[p] for p in range(4) if p != t]) for t in range(4)]
    )
    deriv = np.zeros((4, 4))
    for a in range(4):
        for i in range(4):
            if a != i:
                deriv[a, i] = bary[i] / bary[a] / (points[a] - points[i])
        deriv[a, a] = -np.sum(deriv[a])
    return deriv


D = gll_derivative()
ODD_00, ODD_01 = (float(0.5 * (D[0, 0] - D[0, 3])), float(0.5 * (D[0, 1] - D[0, 2])))
ODD_10, ODD_11 = (float(0.5 * (D[1, 0] - D[1, 3])), float(0.5 * (D[1, 1] - D[1, 2])))
EVEN_0, EVEN_1 = (float(0.5 * (D[0, 0] + D[0, 3])), float(0.5 * (D[1, 0] + D[1, 3])))


def line(g0, g1, g2, g3):
    o0, o1 = (g0 - g3, g1 - g2)
    ev = (g0 + g3) - (g1 + g2)
    a = ODD_00 * o0 + ODD_01 * o1
    c = ODD_10 * o0 + ODD_11 * o1
    b = EVEN_0 * ev
    e = EVEN_1 * ev
    return a + b, c + e, c - e, a - b


def roll(x, shift):
    return pltpu.roll(x, shift % 8, 0)


def sublane():
    return lax.broadcasted_iota(jnp.int32, (8, 128), 0)


def row8(ref, y):
    return jnp.broadcast_to(ref[pl.ds(y, 1), :], (8, 128))


def tendency_step(f, u, v, rj):
    dx = [None] * 16
    for j in range(4):
        dx[4 * j : 4 * j + 4] = line(*[u(4 * j + i) * f[4 * j + i] for i in range(4)])
    out = [None] * 16
    for i in range(4):
        de = line(*[v(4 * j + i) * f[4 * j + i] for j in range(4)])
        for j in range(4):
            n = 4 * j + i
            out[n] = f[n] - rj(n) * (dx[n] + de[j])
    return out


def weighted(values):
    corner = (values[0] + values[3]) + (values[12] + values[15])
    edge = ((values[1] + values[2]) + (values[4] + values[7])) + (
        (values[8] + values[11]) + (values[13] + values[14])
    )
    inner = (values[5] + values[6]) + (values[9] + values[10])
    return corner + 5.0 * edge + 25.0 * inner


def limited(g, jac, rden):
    mean = weighted([jac[n] * g[n] for n in range(16)]) * rden
    lows = list(g)
    while len(lows) > 1:
        lows = [jnp.minimum(lows[k], lows[k + 1]) for k in range(0, len(lows), 2)]
    low = lows[0]
    positive = jnp.maximum(mean, 0.0)
    negative = low < 0.0
    denominator = jnp.where(negative, positive - low, 1.0)
    scaling = jnp.where(negative, positive / denominator, 1.0)
    return [jac[n] * (mean + scaling * (g[n] - mean)) for n in range(16)]


def add_nodes(sums, edge, ey, c, sub):
    for j in range(4):
        c0, c1, c2, c3 = c[4 * j : 4 * j + 4]
        c0 = c0 + jnp.where(sub == 0, 0.0, roll(c3, 1))
        last = c3[7:8, :]
        y = 3 * ey + j
        if j == 0:
            c0, c1, c2 = (c0 + sums[y, 0], c1 + sums[y, 1], c2 + sums[y, 2])
            last = last + edge[pl.ds(y, 1), :]
        sums[y, 0] = c0
        sums[y, 1] = c1
        sums[y, 2] = c2
        edge[pl.ds(y, 1), :] = last


def clear_first(sums, edge):
    for ii in range(3):
        sums[0, ii] = jnp.zeros((8, 128), F32)
    edge[0:1, :] = jnp.zeros((1, 128), F32)


def thin_messages(sums, edge, west, north, south):
    def copy(y, _):
        west[pl.ds(y, 1), :] = sums[y, 0, 0:1, :]
        return 0

    lax.fori_loop(0, 25, copy, 0, unroll=5)
    for out, y in ((north, 0), (south, 24)):
        for ii in range(3):
            out[8 * ii : 8 * ii + 8, :] = sums[y, ii]
        out[24:32, :] = row8(edge, y)


def spot(nodes, e):
    corner = nodes[e, 0]
    ey = corner // 75
    return ey * 8 + (corner - 75 * ey) // 3


def first_kernel(
    nodes, x, vel, jin, sums, west, east, north, south, t0, u_ref, v_ref, rj_ref, j_ref, rd_ref, gathered, jc
):
    step = pl.program_id(0)
    sub = sublane()
    lane = lax.broadcasted_iota(jnp.int32, (8, 128), 1)

    def gather(src):
        def body(e, _):
            gathered[spot(nodes, e)] = src[e]
            return 0

        lax.fori_loop(0, 64, body, 0, unroll=8)

    @pl.when(step == 0)
    def _():
        gather(vel)
        jc[...] = jnp.zeros_like(jc)

        def jbody(e, _):
            jc[pl.ds(spot(nodes, e), 1), 0:16] = jin[pl.ds(e, 1), :]
            return 0

        lax.fori_loop(0, 64, jbody, 0, unroll=8)
        flat = gathered.reshape(1024, 128)

        def coef(ey, _):
            comp = jc[pl.ds(pl.multiple_of(8 * ey, 8), 8), :]
            js = []
            for n in range(16):
                jv = jnp.broadcast_to(comp[:, n : n + 1], (8, 128))
                w = flat[pl.ds(ey * 128 + n, 8, stride=16), :]
                wr = pltpu.roll(w, 64, 1)
                dj = STEP_SIZE * jv
                u_ref[n, ey] = dj * jnp.where(lane < 64, w, wr)
                v_ref[n, ey] = dj * jnp.where(lane < 64, wr, w)
                j_ref[n, ey] = jv
                rj_ref[n, ey] = 1.0 / jv
                js.append(jv)
            rd_ref[ey] = 1.0 / weighted(js)
            return 0

        lax.fori_loop(0, 8, coef, 0)

    gather(x)
    flat = gathered.reshape(1024, 128)
    clear_first(sums, east)

    def rows(ey, _):
        f = [flat[pl.ds(ey * 128 + n, 8, stride=16), :] for n in range(16)]
        for n in range(16):
            t0[n, ey] = f[n]
        g = tendency_step(
            f, lambda n: u_ref[n, ey], lambda n: v_ref[n, ey], lambda n: rj_ref[n, ey]
        )
        c = limited(g, [j_ref[n, ey] for n in range(16)], rd_ref[ey])
        add_nodes(sums, east, ey, c, sub)
        return 0

    lax.fori_loop(0, 8, rows, 0)
    thin_messages(sums, east, west, north, south)
    for out in (west, east):
        for half in range(2):
            out[32 + 8 * half : 40 + 8 * half, :] = jc[
                pl.ds(pl.multiple_of(8 * (4 * half + step), 8), 8), :
            ]


def geometry_kernel(own, from_e, from_w, from_n, from_s, j_ref, inv):
    sub = sublane()

    def tile(ref, base, t):
        return ref[base : base + 8, 128 * t : 128 * t + 128]

    pending = None
    for r in range(-3, 11):
        if r < 0:
            t = r + 4
            a, b = (tile(from_n, 32, t), tile(from_n, 40, t))
        elif r > 7:
            t = r - 8
            a, b = (tile(from_s, 32, t), tile(from_s, 40, t))
        else:
            base, t = (32 + 8 * (r // 4), r % 4)
            a = tile(own, base, t)
            b = jnp.where(sub < 4, tile(from_e, base, t), tile(from_w, base, t))
        kept = None
        for j in range(4):
            ca = [jnp.broadcast_to(a[:, 4 * j + i : 4 * j + i + 1], (8, 128)) for i in range(4)]
            cb = [jnp.broadcast_to(b[:, 4 * j + i : 4 * j + i + 1], (8, 128)) for i in range(4)]
            if -2 <= r <= 9:
                for i in range(4):
                    j_ref[4 * j + i, r + 2, 0:8] = ca[i]
                    j_ref[4 * j + i, r + 2, 8:16] = cb[i]
            ra, rb = (roll(ca[3], 1), roll(cb[3], 1))
            row = [
                ca[0] + jnp.where(sub == 0, rb, ra),
                cb[0] + jnp.where(sub == 0, ra, rb),
                ca[1],
                cb[1],
                ca[2],
                cb[2],
            ]
            if j == 3:
                kept = row
                continue
            if j == 0 and pending is not None:
                row = [p + q for p, q in zip(row, pending)]
            y = 3 * r + j + 6
            if 0 <= y <= 36:
                for ii in range(3):
                    inv[y, ii, 0:8] = 1.0 / row[2 * ii]
                    inv[y, ii, 8:16] = 1.0 / row[2 * ii + 1]
        pending = kept


def node_values(sums, edge, from_e, from_w, from_n, from_s, inv, whole, side, sub):
    def body(y, _):
        whole[y, 0] = (sums[y, 0] + jnp.where(sub == 0, row8(from_w, y), 0.0)) * inv[y + 6, 0, 0:8]
        whole[y, 1] = sums[y, 1] * inv[y + 6, 1, 0:8]
        whole[y, 2] = sums[y, 2] * inv[y + 6, 2, 0:8]
        side[pl.ds(y, 1), :] = (edge[pl.ds(y, 1), :] + from_e[pl.ds(y, 1), :]) * inv[y + 6, 0, 8:9]
        return 0

    lax.fori_loop(0, 25, body, 0, unroll=5)
    for y, msg in ((0, from_n), (24, from_s)):
        for ii in range(3):
            whole[y, ii] = whole[y, ii] + msg[8 * ii : 8 * ii + 8, :] * inv[y + 6, ii, 0:8]
        side[y : y + 1, :] = side[y : y + 1, :] + msg[24:25, :] * inv[y + 6, 0, 8:9]


def element_values(whole, side, ey, sub):
    f = []
    for j in range(4):
        y = 3 * ey + j
        p0 = whole[y, 0]
        f += [p0, whole[y, 1], whole[y, 2], jnp.where(sub == 7, row8(side, y), roll(p0, 7))]
    return f


def stage_kernel(
    keep, take, wide, sums, edge, from_e, from_w, from_n, from_s, inv, t0, u_ref, v_ref, rj_ref, j_ref, rd_ref,
    out, west, east, third, fourth, whole, side,
):
    sub = sublane()
    node_values(sums, edge, from_e, from_w, from_n, from_s, inv, whole, side, sub)
    column = fourth if wide else east
    clear_first(out, column)

    def rows(ey, _):
        f = element_values(whole, side, ey, sub)
        h = tendency_step(
            f, lambda n: u_ref[n, ey], lambda n: v_ref[n, ey], lambda n: rj_ref[n, ey]
        )
        g = [keep * t0[n, ey] + take * h[n] for n in range(16)]
        c = limited(g, [j_ref[n, ey] for n in range(16)], rd_ref[ey])
        add_nodes(out, column, ey, c, sub)
        return 0

    lax.fori_loop(0, 8, rows, 0)
    if not wide:
        thin_messages(out, column, west, third, fourth)
        return

    def pack(y, _):
        p0, p1, p2 = (out[y, 0], out[y, 1], out[y, 2])
        west[y] = jnp.where(sub < 3, p0, jnp.where(sub < 5, roll(p1, 3), roll(p2, 5)))
        east[y] = jnp.where(
            sub >= 6,
            p0,
            jnp.where(sub >= 4, roll(p1, -2), jnp.where(sub >= 2, roll(p2, -4), row8(column, y))),
        )
        return 0

    lax.fori_loop(0, 25, pack, 0, unroll=5)


def joined_row(sums, edge, from_e, from_w, y, sub):
    me, mw = (from_e[y], from_w[y])
    a0 = sums[y, 0] + jnp.where(sub == 0, mw, 0.0)
    b0 = jnp.where(sub == 0, row8(edge, y) + me, jnp.where(sub < 4, me, mw))
    b1 = jnp.where(sub < 4, roll(me, -3), roll(mw, 2))
    b2 = jnp.where(sub < 4, roll(me, -5), roll(mw, 4))
    return a0, sums[y, 1], sums[y, 2], b0, b1, b2


def rows_kernel(sums, edge, from_e, from_w, north, south):
    sub = sublane()
    for out, first in ((north, 0), (south, 18)):
        for k in range(7):
            a0, a1, a2, b0, b1, b2 = joined_row(sums, edge, from_e, from_w, first + k, sub)
            out[k, 0:8] = a0
            out[k, 8:16] = a1
            out[k, 16:24] = a2
            out[k, 24:32] = b0
            out[k, 32:40] = jnp.where((sub < 2) | (sub >= 6), b1, roll(b2, 4))


def laplace_rows(src, j_ref, inv, dst, first, last, sub):
    for ii in range(3):
        dst[3 * first, ii] = jnp.zeros((16, 128), F32)

    def core(f, jac):
        out = [None] * 16
        for j in range(4):
            d = line(*f[4 * j : 4 * j + 4])
            out[4 * j : 4 * j + 4] = line(*[jac(4 * j + i) * d[i] for i in range(4)])
        for i in range(4):
            d = line(*f[i::4])
            d = line(*[jac(4 * j + i) * d[j] for j in range(4)])
            for j in range(4):
                out[4 * j + i] = out[4 * j + i] + d[j]
        return out

    def rows(r, _):
        fa, fb = ([], [])
        for j in range(4):
            y = 3 * r + j
            pa, pb = (src[y, 0, 0:8], src[y, 0, 8:16])
            ra, rb = (roll(pa, 7), roll(pb, 7))
            fa += [pa, src[y, 1, 0:8], src[y, 2, 0:8], jnp.where(sub == 7, rb, ra)]
            fb += [pb, src[y, 1, 8:16], src[y, 2, 8:16], jnp.where(sub == 7, ra, rb)]
        ca = core(fa, lambda n: j_ref[n, r, 0:8])
        cb = core(fb, lambda n: j_ref[n, r, 8:16])
        for j in range(4):
            y = 3 * r + j
            ra, rb = (roll(ca[4 * j + 3], 1), roll(cb[4 * j + 3], 1))
            row = [
                (ca[4 * j] + jnp.where(sub == 0, rb, ra), cb[4 * j] + jnp.where(sub == 0, ra, rb)),
                (ca[4 * j + 1], cb[4 * j + 1]),
                (ca[4 * j + 2], cb[4 * j + 2]),
            ]
            for ii in range(3):
                a, b = row[ii]
                if j == 0:
                    a, b = (a + dst[y, ii, 0:8], b + dst[y, ii, 8:16])
                if j < 3:
                    a, b = (a * inv[y, ii, 0:8], b * inv[y, ii, 8:16])
                dst[y, ii, 0:8] = a
                dst[y, ii, 8:16] = b
        return 0

    lax.fori_loop(first, last, rows, 0)


def last_kernel(
    nodes, sums, edge, from_e, from_w, from_n, from_s, j_ref, inv, out, field, one, two, spread
):
    sub = sublane()

    def own(y, _):
        a0, a1, a2, b0, b1, b2 = joined_row(sums, edge, from_e, from_w, y, sub)
        for ii, (a, b) in enumerate(((a0, b0), (a1, b1), (a2, b2))):
            field[y + 6, ii, 0:8] = a * inv[y + 6, ii, 0:8]
            field[y + 6, ii, 8:16] = b * inv[y + 6, ii, 8:16]
        return 0

    lax.fori_loop(0, 25, own, 0, unroll=5)
    for msg, first, shared in ((from_n, 0, 6), (from_s, 30, 0)):
        for k in range(7):
            y = first + k
            c = msg[k, 32:40]
            parts = [msg[k, 0:8], msg[k, 24:32], msg[k, 8:16], c, msg[k, 16:24], roll(c, 4)]
            for ii in range(3):
                a, b = (parts[2 * ii] * inv[y, ii, 0:8], parts[2 * ii + 1] * inv[y, ii, 8:16])
                if k == shared:
                    a, b = (a + field[y, ii, 0:8], b + field[y, ii, 8:16])
                field[y, ii, 0:8] = a
                field[y, ii, 8:16] = b
    laplace_rows(field, j_ref, inv, one, 0, 12, sub)
    laplace_rows(one, j_ref, inv, two, 1, 11, sub)
    flat = spread.reshape(1024, 128)

    def finish(ey, _):
        for j in range(4):
            y = 3 * ey + j + 6
            p0 = field[y, 0, 0:8] - DIFFUSION * two[y, 0, 0:8]
            q0 = field[y, 0, 8:16] - DIFFUSION * two[y, 0, 8:16]
            vals = [
                p0,
                field[y, 1, 0:8] - DIFFUSION * two[y, 1, 0:8],
                field[y, 2, 0:8] - DIFFUSION * two[y, 2, 0:8],
                jnp.where(sub == 7, roll(q0, 7), roll(p0, 7)),
            ]
            for i in range(4):
                flat[pl.ds(ey * 128 + 4 * j + i, 8, stride=16), :] = vals[i]
        return 0

    lax.fori_loop(0, 8, finish, 0)

    def scatter(e, _):
        out[e] = spread[spot(nodes, e)]
        return 0

    lax.fori_loop(0, 64, scatter, 0, unroll=8)


def sds(*shape):
    return jax.ShapeDtypeStruct(shape, F32)


def tiled(*shape):
    zeros = (0,) * (len(shape) - 1)
    return pl.BlockSpec(shape, lambda t: zeros + (t,))


def fixed(*shape):
    zeros = (0,) * len(shape)
    return pl.BlockSpec(shape, lambda t: zeros)


PARAMS = pltpu.CompilerParams(vmem_limit_bytes=VMEM_LIMIT, dimension_semantics=("arbitrary",))
SMEM = pl.BlockSpec(memory_space=pltpu.SMEM)


def shifted(value, distance):
    size = lax.axis_size("sfc")
    return lax.ppermute(value, "sfc", [((i - distance) % size, i) for i in range(size)])


def per_device(tracers, velocity, jacobian, elem_nodes):
    coef = [sds(16, 8, 8, 128)] * 4 + [sds(8, 8, 128)]
    coef_specs = [fixed(16, 8, 8, 128)] * 4 + [fixed(8, 8, 128)]
    sums_spec = tiled(27, 3, 8, 128)
    first = pl.pallas_call(
        first_kernel,
        grid=(4,),
        in_specs=[SMEM, tiled(64, 16, 128), fixed(64, 16, 128), fixed(64, 16)],
        out_specs=[sums_spec, tiled(48, 128), tiled(48, 128), tiled(32, 128), tiled(32, 128), tiled(16, 8, 8, 128)]
        + coef_specs,
        out_shape=[sds(27, 3, 8, 512), sds(48, 512), sds(48, 512), sds(32, 512), sds(32, 512), sds(16, 8, 8, 512)]
        + coef,
        scratch_shapes=[pltpu.VMEM((64, 16, 128), F32), pltpu.VMEM((64, 128), F32)],
        compiler_params=PARAMS,
        name="section_one_sums",
    )
    sums, west, east, north, south, t0, *coefs = first(elem_nodes, tracers, velocity, jacobian)

    row = lax.broadcasted_iota(jnp.int32, (32, 1), 0)

    def corrected(own, from_w, from_e, y):
        return own + jnp.where(row == 0, from_w[y : y + 1], 0.0) + jnp.where(row >= 24, from_e[y : y + 1], 0.0)

    from_e, from_w = (shifted(west, -1), shifted(east, 1))
    low = lax.broadcasted_iota(jnp.int32, (8, 1), 0) < 4
    beside = [jnp.where(low, from_e[k : k + 8], from_w[k : k + 8]) for k in (32, 40)]
    msg_n = jnp.concatenate([corrected(north, from_w, from_e, 0), west[32:40], beside[0]])
    msg_s = jnp.concatenate([corrected(south, from_w, from_e, 24), west[40:48], beside[1]])
    from_s, from_n = (shifted(msg_n, -PX), shifted(msg_s, PX))

    whole = pl.BlockSpec(memory_space=pltpu.VMEM)
    jac, inv = pl.pallas_call(
        geometry_kernel,
        in_specs=[whole] * 5,
        out_specs=[whole] * 2,
        out_shape=[sds(16, 12, 16, 128), sds(37, 3, 16, 128)],
        compiler_params=pltpu.CompilerParams(vmem_limit_bytes=VMEM_LIMIT),
        name="geometry",
    )(west, from_e, from_w, from_n, from_s)
    jac_spec, inv_spec = (fixed(16, 12, 16, 128), fixed(37, 3, 16, 128))

    def stage(keep, take, wide, sums, edge, from_e, from_w, from_n, from_s, rows):
        if wide:
            outs = [sds(25, 8, 512), sds(25, 8, 512), sds(8, 512), sds(32, 512)]
            specs = [tiled(25, 8, 128), tiled(25, 8, 128), tiled(8, 128), tiled(32, 128)]
        else:
            outs = [sds(32, 512)] * 4
            specs = [tiled(32, 128)] * 4
        return pl.pallas_call(
            functools.partial(stage_kernel, keep, take, wide),
            grid=(4,),
            in_specs=[sums_spec]
            + [tiled(rows, 128)] * 5
            + [inv_spec, tiled(16, 8, 8, 128)]
            + coef_specs,
            out_specs=[sums_spec] + specs,
            out_shape=[sds(27, 3, 8, 512)] + outs,
            scratch_shapes=[pltpu.VMEM((27, 3, 8, 128), F32), pltpu.VMEM((32, 128), F32)],
            compiler_params=PARAMS,
            name="section_three_sums" if wide else "section_two_sums",
        )(sums, edge, from_e, from_w, from_n, from_s, inv, t0, *coefs)

    sums, west, east, north, south = stage(
        0.75, 0.25, False, sums, east, from_e, from_w, from_n, from_s, 48
    )
    from_e, from_w = (shifted(west, -1), shifted(east, 1))
    msg_n = corrected(north, from_w, from_e, 0)
    msg_s = corrected(south, from_w, from_e, 24)
    from_s, from_n = (shifted(msg_n, -PX), shifted(msg_s, PX))

    sums, west, east, _, edge = stage(
        1.0 / 3.0, 2.0 / 3.0, True, sums, east, from_e, from_w, from_n, from_s, 32
    )
    from_e, from_w = (shifted(west, -1), shifted(east, 1))
    message = tiled(25, 8, 128)
    band = tiled(7, 40, 128)
    msg_n, msg_s = pl.pallas_call(
        rows_kernel,
        grid=(4,),
        in_specs=[sums_spec, tiled(32, 128), message, message],
        out_specs=[band, band],
        out_shape=[sds(7, 40, 512)] * 2,
        compiler_params=PARAMS,
        name="row_bands",
    )(sums, edge, from_e, from_w)
    from_s, from_n = (shifted(msg_n, -PX), shifted(msg_s, PX))
    return pl.pallas_call(
        last_kernel,
        grid=(4,),
        in_specs=[SMEM, sums_spec, tiled(32, 128), message, message, band, band, jac_spec, inv_spec],
        out_specs=tiled(64, 16, 128),
        out_shape=sds(64, 16, 512),
        scratch_shapes=[pltpu.VMEM((37, 3, 16, 128), F32)] * 3 + [pltpu.VMEM((64, 16, 128), F32)],
        compiler_params=PARAMS,
        name="biharmonic",
    )(elem_nodes, sums, edge, from_e, from_w, from_n, from_s, jac, inv)


def solution(mesh):
    in_specs = (P("sfc", None, None), P("sfc", None, None), P("sfc", None), P("sfc", None))
    out_specs = P("sfc", None, None)
    return jax.shard_map(
        per_device, mesh=mesh, in_specs=in_specs, out_specs=out_specs, check_vma=False
    )
```

```python
import functools
import jax
import jax.numpy as jnp
import numpy as np
from jax import lax
from jax.experimental import pallas as pl
from jax.experimental.pallas import tpu as pltpu
from jax.sharding import PartitionSpec as P

TT = 8
PX = 8
STEP_SIZE = 0.04
DIFFUSION = 0.0001
F32 = jnp.float32
VMEM_LIMIT = 48 * 1024 * 1024


def gll_derivative():
    points = np.array([-1.0, -np.sqrt(0.2), np.sqrt(0.2), 1.0])
    bary = np.array(
        [1.0 / np.prod([points[t] - points[p] for p in range(4) if p != t]) for t in range(4)]
    )
    deriv = np.zeros((4, 4))
    for a in range(4):
        for i in range(4):
            if a != i:
                deriv[a, i] = bary[i] / bary[a] / (points[a] - points[i])
        deriv[a, a] = -np.sum(deriv[a])
    return deriv


D = gll_derivative()
ODD_00, ODD_01 = (float(0.5 * (D[0, 0] - D[0, 3])), float(0.5 * (D[0, 1] - D[0, 2])))
ODD_10, ODD_11 = (float(0.5 * (D[1, 0] - D[1, 3])), float(0.5 * (D[1, 1] - D[1, 2])))
EVEN_0, EVEN_1 = (float(0.5 * (D[0, 0] + D[0, 3])), float(0.5 * (D[1, 0] + D[1, 3])))


def line(g0, g1, g2, g3):
    o0, o1 = (g0 - g3, g1 - g2)
    ev = (g0 + g3) - (g1 + g2)
    a = ODD_00 * o0 + ODD_01 * o1
    c = ODD_10 * o0 + ODD_11 * o1
    b = EVEN_0 * ev
    e = EVEN_1 * ev
    return a + b, c + e, c - e, a - b


def roll(x, shift):
    return pltpu.roll(x, shift % 8, 0)


def sublane():
    return lax.broadcasted_iota(jnp.int32, (8, 128), 0)


def row8(ref, y):
    return jnp.broadcast_to(ref[pl.ds(y, 1), :], (8, 128))


def tendency_step(f, u, v, rj):
    dx = [None] * 16
    for j in range(4):
        dx[4 * j : 4 * j + 4] = line(*[u(4 * j + i) * f[4 * j + i] for i in range(4)])
    out = [None] * 16
    for i in range(4):
        de = line(*[v(4 * j + i) * f[4 * j + i] for j in range(4)])
        for j in range(4):
            n = 4 * j + i
            out[n] = f[n] - rj(n) * (dx[n] + de[j])
    return out


def weighted(values):
    corner = (values[0] + values[3]) + (values[12] + values[15])
    edge = ((values[1] + values[2]) + (values[4] + values[7])) + (
        (values[8] + values[11]) + (values[13] + values[14])
    )
    inner = (values[5] + values[6]) + (values[9] + values[10])
    return corner + 5.0 * edge + 25.0 * inner


def limited(g, jac, rden):
    mean = weighted([jac[n] * g[n] for n in range(16)]) * rden
    lows = list(g)
    while len(lows) > 1:
        lows = [jnp.minimum(lows[k], lows[k + 1]) for k in range(0, len(lows), 2)]
    low = lows[0]
    positive = jnp.maximum(mean, 0.0)
    negative = low < 0.0
    denominator = jnp.where(negative, positive - low, 1.0)
    scaling = jnp.where(negative, positive / denominator, 1.0)
    return [jac[n] * (mean + scaling * (g[n] - mean)) for n in range(16)]


def add_nodes(sums, edge, ey, c, sub):
    for j in range(4):
        c0, c1, c2, c3 = c[4 * j : 4 * j + 4]
        c0 = c0 + jnp.where(sub == 0, 0.0, roll(c3, 1))
        last = c3[7:8, :]
        y = 3 * ey + j
        if j == 0:
            c0, c1, c2 = (c0 + sums[y, 0], c1 + sums[y, 1], c2 + sums[y, 2])
            last = last + edge[pl.ds(y, 1), :]
        sums[y, 0] = c0
        sums[y, 1] = c1
        sums[y, 2] = c2
        edge[pl.ds(y, 1), :] = last


def clear_first(sums, edge):
    for ii in range(3):
        sums[0, ii] = jnp.zeros((8, 128), F32)
    edge[0:1, :] = jnp.zeros((1, 128), F32)


def thin_messages(sums, edge, west, north, south):
    def copy(y, _):
        west[pl.ds(y, 1), :] = sums[y, 0, 0:1, :]
        return 0

    lax.fori_loop(0, 25, copy, 0, unroll=5)
    for out, y in ((north, 0), (south, 24)):
        for ii in range(3):
            out[8 * ii : 8 * ii + 8, :] = sums[y, ii]
        out[24:32, :] = row8(edge, y)


def place(corner):
    ey = (corner * 874) >> 16
    return 8 * ey + (((corner - 75 * ey) * 21846) >> 16)


def fill_places(nodes, spots):
    def body(e, _):
        spots[e] = place(nodes[0, e])
        return 0

    lax.fori_loop(0, 64, body, 0, unroll=8)


def first_kernel(
    nodes, x, vel, jin, sums, west, east, north, south, t0, u_ref, v_ref, rj_ref, j_ref, rd_ref,
    gathered, winds, jc, node_rows, j_rows, corners, spots, sem,
):
    step = pl.program_id(0)
    sub = sublane()
    lane = lax.broadcasted_iota(jnp.int32, (8, 128), 1)

    @pl.when(step == 0)
    def _():
        copies = [
            pltpu.make_async_copy(nodes, corners, sem.at[0]),
            pltpu.make_async_copy(nodes, node_rows, sem.at[1]),
            pltpu.make_async_copy(jin, j_rows, sem.at[2]),
            pltpu.make_async_copy(vel, gathered, sem.at[3]),
        ]
        for copy in copies:
            copy.start()
        jc[...] = jnp.zeros_like(jc)
        for copy in copies[:3]:
            copy.wait()
        fill_places(corners, spots)
        to = place(node_rows[0:1, :])
        hit = (lax.broadcasted_iota(jnp.int32, (64, 64), 0) == to).astype(F32)
        jc[:, 0:16] = lax.dot_general(
            hit, j_rows[...], (((1,), (1,)), ((), ())), precision=lax.Precision.HIGHEST, preferred_element_type=F32
        )
        copies[3].wait()

        def order(e, _):
            winds[spots[e]] = gathered[e]
            return 0

        lax.fori_loop(0, 64, order, 0, unroll=8)
        flat = winds.reshape(1024, 128)

        def coef(ey, _):
            comp = jc[pl.ds(pl.multiple_of(8 * ey, 8), 8), :]
            js = []
            for n in range(16):
                jv = jnp.broadcast_to(comp[:, n : n + 1], (8, 128))
                w = flat[pl.ds(ey * 128 + n, 8, stride=16), :]
                wr = pltpu.roll(w, 64, 1)
                dj = STEP_SIZE * jv
                u_ref[n, ey] = dj * jnp.where(lane < 64, w, wr)
                v_ref[n, ey] = dj * jnp.where(lane < 64, wr, w)
                j_ref[n, ey] = jv
                rj_ref[n, ey] = 1.0 / jv
                js.append(jv)
            rd_ref[ey] = 1.0 / weighted(js)
            return 0

        lax.fori_loop(0, 8, coef, 0)

    def gather(e, _):
        gathered[spots[e]] = x[e]
        return 0

    lax.fori_loop(0, 64, gather, 0, unroll=8)
    flat = gathered.reshape(1024, 128)
    clear_first(sums, east)

    def rows(ey, _):
        f = [flat[pl.ds(ey * 128 + n, 8, stride=16), :] for n in range(16)]
        for n in range(16):
            t0[n, ey] = f[n]
        g = tendency_step(
            f, lambda n: u_ref[n, ey], lambda n: v_ref[n, ey], lambda n: rj_ref[n, ey]
        )
        c = limited(g, [j_ref[n, ey] for n in range(16)], rd_ref[ey])
        add_nodes(sums, east, ey, c, sub)
        return 0

    lax.fori_loop(0, 8, rows, 0, unroll=8)
    thin_messages(sums, east, west, north, south)
    for out in (west, east):
        for half in range(2):
            out[32 + 8 * half : 40 + 8 * half, :] = jc[
                pl.ds(pl.multiple_of(8 * (4 * half + step), 8), 8), :
            ]


def geometry_kernel(own, from_e, from_w, from_n, from_s, j_ref, inv):
    sub = sublane()

    def tile(ref, base, t):
        return ref[base : base + 8, 128 * t : 128 * t + 128]

    pending = None
    for r in range(-3, 11):
        if r < 0:
            t = r + 4
            a, b = (tile(from_n, 32, t), tile(from_n, 40, t))
        elif r > 7:
            t = r - 8
            a, b = (tile(from_s, 32, t), tile(from_s, 40, t))
        else:
            base, t = (32 + 8 * (r // 4), r % 4)
            a = tile(own, base, t)
            b = jnp.where(sub < 4, tile(from_e, base, t), tile(from_w, base, t))
        kept = None
        for j in range(4):
            ca = [jnp.broadcast_to(a[:, 4 * j + i : 4 * j + i + 1], (8, 128)) for i in range(4)]
            cb = [jnp.broadcast_to(b[:, 4 * j + i : 4 * j + i + 1], (8, 128)) for i in range(4)]
            if -2 <= r <= 9:
                for i in range(4):
                    j_ref[4 * j + i, r + 2, 0:8] = ca[i]
                    j_ref[4 * j + i, r + 2, 8:16] = cb[i]
            ra, rb = (roll(ca[3], 1), roll(cb[3], 1))
            row = [
                ca[0] + jnp.where(sub == 0, rb, ra),
                cb[0] + jnp.where(sub == 0, ra, rb),
                ca[1],
                cb[1],
                ca[2],
                cb[2],
            ]
            if j == 3:
                kept = row
                continue
            if j == 0 and pending is not None:
                row = [p + q for p, q in zip(row, pending)]
            y = 3 * r + j + 6
            if 0 <= y <= 36:
                for ii in range(3):
                    inv[y, ii, 0:8] = 1.0 / row[2 * ii]
                    inv[y, ii, 8:16] = 1.0 / row[2 * ii + 1]
        pending = kept


def node_values(sums, edge, from_e, from_w, from_n, from_s, inv, whole, side, sub):
    def body(y, _):
        whole[y, 0] = (sums[y, 0] + jnp.where(sub == 0, row8(from_w, y), 0.0)) * inv[y + 6, 0, 0:8]
        whole[y, 1] = sums[y, 1] * inv[y + 6, 1, 0:8]
        whole[y, 2] = sums[y, 2] * inv[y + 6, 2, 0:8]
        side[pl.ds(y, 1), :] = (edge[pl.ds(y, 1), :] + from_e[pl.ds(y, 1), :]) * inv[y + 6, 0, 8:9]
        return 0

    lax.fori_loop(0, 25, body, 0, unroll=5)
    for y, msg in ((0, from_n), (24, from_s)):
        for ii in range(3):
            whole[y, ii] = whole[y, ii] + msg[8 * ii : 8 * ii + 8, :] * inv[y + 6, ii, 0:8]
        side[y : y + 1, :] = side[y : y + 1, :] + msg[24:25, :] * inv[y + 6, 0, 8:9]


def element_values(whole, side, ey, sub):
    f = []
    for j in range(4):
        y = 3 * ey + j
        p0 = whole[y, 0]
        f += [p0, whole[y, 1], whole[y, 2], jnp.where(sub == 7, row8(side, y), roll(p0, 7))]
    return f


def stage_kernel(
    keep, take, wide, sums, edge, from_e, from_w, from_n, from_s, inv, t0, u_ref, v_ref, rj_ref, j_ref, rd_ref,
    out, west, east, third, fourth, whole, side,
):
    sub = sublane()
    node_values(sums, edge, from_e, from_w, from_n, from_s, inv, whole, side, sub)
    column = fourth if wide else east
    clear_first(out, column)

    def rows(ey, _):
        f = element_values(whole, side, ey, sub)
        h = tendency_step(
            f, lambda n: u_ref[n, ey], lambda n: v_ref[n, ey], lambda n: rj_ref[n, ey]
        )
        g = [keep * t0[n, ey] + take * h[n] for n in range(16)]
        c = limited(g, [j_ref[n, ey] for n in range(16)], rd_ref[ey])
        add_nodes(out, column, ey, c, sub)
        return 0

    lax.fori_loop(0, 8, rows, 0, unroll=8)
    if not wide:
        thin_messages(out, column, west, third, fourth)
        return

    def pack(y, _):
        p0, p1, p2 = (out[y, 0], out[y, 1], out[y, 2])
        west[y] = jnp.where(sub < 3, p0, jnp.where(sub < 5, roll(p1, 3), roll(p2, 5)))
        east[y] = jnp.where(
            sub >= 6,
            p0,
            jnp.where(sub >= 4, roll(p1, -2), jnp.where(sub >= 2, roll(p2, -4), row8(column, y))),
        )
        return 0

    lax.fori_loop(0, 25, pack, 0, unroll=5)


def joined_row(sums, edge, from_e, from_w, y, sub):
    me, mw = (from_e[y], from_w[y])
    a0 = sums[y, 0] + jnp.where(sub == 0, mw, 0.0)
    b0 = jnp.where(sub == 0, row8(edge, y) + me, jnp.where(sub < 4, me, mw))
    b1 = jnp.where(sub < 4, roll(me, -3), roll(mw, 2))
    b2 = jnp.where(sub < 4, roll(me, -5), roll(mw, 4))
    return a0, sums[y, 1], sums[y, 2], b0, b1, b2


def rows_kernel(sums, edge, from_e, from_w, north, south):
    sub = sublane()
    for out, first in ((north, 0), (south, 18)):
        for k in range(7):
            a0, a1, a2, b0, b1, b2 = joined_row(sums, edge, from_e, from_w, first + k, sub)
            out[k, 0:8] = a0
            out[k, 8:16] = a1
            out[k, 16:24] = a2
            out[k, 24:32] = b0
            out[k, 32:40] = jnp.where((sub < 2) | (sub >= 6), b1, roll(b2, 4))


def laplace_core(f, jac):
    out = [None] * 16
    for j in range(4):
        d = line(*[f(4 * j + i) for i in range(4)])
        out[4 * j : 4 * j + 4] = line(*[jac(4 * j + i) * d[i] for i in range(4)])
    for i in range(4):
        d = line(*[f(4 * j + i) for j in range(4)])
        d = line(*[jac(4 * j + i) * d[j] for j in range(4)])
        for j in range(4):
            out[4 * j + i] = out[4 * j + i] + d[j]
    return out


FIRST, JOIN, SKIP = range(3)


def laplace_row(src, j_ref, inv, dst, r, top, bottom, sub):
    fa, fb = ([], [])
    for j in range(4):
        y = 3 * r + j
        pa, pb = (src[y, 0, 0:8], src[y, 0, 8:16])
        ra, rb = (roll(pa, 7), roll(pb, 7))
        fa += [pa, src[y, 1, 0:8], src[y, 2, 0:8], jnp.where(sub == 7, rb, ra)]
        fb += [pb, src[y, 1, 8:16], src[y, 2, 8:16], jnp.where(sub == 7, ra, rb)]
    ca = laplace_core(lambda n: fa[n], lambda n: j_ref[n, r, 0:8])
    cb = laplace_core(lambda n: fb[n], lambda n: j_ref[n, r, 8:16])
    for j in range(4):
        what = {0: top, 3: bottom}.get(j)
        if what == SKIP:
            continue
        y = 3 * r + j
        ra, rb = (roll(ca[4 * j + 3], 1), roll(cb[4 * j + 3], 1))
        row = [
            (ca[4 * j] + jnp.where(sub == 0, rb, ra), cb[4 * j] + jnp.where(sub == 0, ra, rb)),
            (ca[4 * j + 1], cb[4 * j + 1]),
            (ca[4 * j + 2], cb[4 * j + 2]),
        ]
        for ii in range(3):
            a, b = row[ii]
            if what == JOIN:
                a, b = (a + dst[y, ii, 0:8], b + dst[y, ii, 8:16])
            if what != FIRST:
                a, b = (a * inv[y, ii, 0:8], b * inv[y, ii, 8:16])
            dst[y, ii, 0:8] = a
            dst[y, ii, 8:16] = b


def own_rows(sums, edge, from_e, from_w, inv, field, first, last, sub):
    def body(y, _):
        a0, a1, a2, b0, b1, b2 = joined_row(sums, edge, from_e, from_w, y, sub)
        for ii, (a, b) in enumerate(((a0, b0), (a1, b1), (a2, b2))):
            field[y + 6, ii, 0:8] = a * inv[y + 6, ii, 0:8]
            field[y + 6, ii, 8:16] = b * inv[y + 6, ii, 8:16]
        return 0

    lax.fori_loop(first, last, body, 0)


def inner_kernel(sums, edge, from_e, from_w, j_ref, inv, field, one, two):
    sub = sublane()
    own_rows(sums, edge, from_e, from_w, inv, field, 0, 25, sub)
    laplace_row(field, j_ref, inv, one, 3, FIRST, FIRST, sub)

    def rows_one(r, _):
        laplace_row(field, j_ref, inv, one, r, JOIN, FIRST, sub)
        return 0

    lax.fori_loop(4, 9, rows_one, 0, unroll=5)
    laplace_row(one, j_ref, inv, two, 4, FIRST, FIRST, sub)

    def rows_two(r, _):
        laplace_row(one, j_ref, inv, two, r, JOIN, FIRST, sub)
        return 0

    lax.fori_loop(5, 8, rows_two, 0, unroll=3)


def last_kernel(
    nodes, from_n, from_s, j_ref, inv, field_in, one_in, two_in, out, field, one, two, spread, spots
):
    sub = sublane()

    @pl.when(pl.program_id(0) == 0)
    def _():
        fill_places(nodes, spots)

    def copy_rows(src, dst, first, last):
        def body(y, _):
            for ii in range(3):
                dst[y, ii] = src[y, ii]
            return 0

        lax.fori_loop(first, last, body, 0)

    copy_rows(field_in, field, 6, 31)
    for msg, first, shared in ((from_n, 0, 6), (from_s, 30, 0)):
        for k in range(7):
            y = first + k
            c = msg[k, 32:40]
            parts = [msg[k, 0:8], msg[k, 24:32], msg[k, 8:16], c, msg[k, 16:24], roll(c, 4)]
            for ii in range(3):
                a, b = (parts[2 * ii] * inv[y, ii, 0:8], parts[2 * ii + 1] * inv[y, ii, 8:16])
                if k == shared:
                    a, b = (a + field[y, ii, 0:8], b + field[y, ii, 8:16])
                field[y, ii, 0:8] = a
                field[y, ii, 8:16] = b
    copy_rows(one_in, one, 9, 28)
    laplace_row(field, j_ref, inv, one, 0, SKIP, FIRST, sub)
    laplace_row(field, j_ref, inv, one, 1, JOIN, FIRST, sub)
    laplace_row(field, j_ref, inv, one, 2, JOIN, JOIN, sub)
    laplace_row(field, j_ref, inv, one, 9, JOIN, FIRST, sub)
    laplace_row(field, j_ref, inv, one, 10, JOIN, FIRST, sub)
    laplace_row(field, j_ref, inv, one, 11, JOIN, SKIP, sub)
    copy_rows(two_in, two, 12, 25)
    laplace_row(one, j_ref, inv, two, 1, SKIP, FIRST, sub)
    laplace_row(one, j_ref, inv, two, 2, JOIN, FIRST, sub)
    laplace_row(one, j_ref, inv, two, 3, JOIN, JOIN, sub)
    laplace_row(one, j_ref, inv, two, 8, JOIN, FIRST, sub)
    laplace_row(one, j_ref, inv, two, 9, JOIN, FIRST, sub)
    laplace_row(one, j_ref, inv, two, 10, JOIN, SKIP, sub)
    flat = spread.reshape(1024, 128)

    def finish(ey, _):
        for j in range(4):
            y = 3 * ey + j + 6
            p0 = field[y, 0, 0:8] - DIFFUSION * two[y, 0, 0:8]
            q0 = field[y, 0, 8:16] - DIFFUSION * two[y, 0, 8:16]
            vals = [
                p0,
                field[y, 1, 0:8] - DIFFUSION * two[y, 1, 0:8],
                field[y, 2, 0:8] - DIFFUSION * two[y, 2, 0:8],
                jnp.where(sub == 7, roll(q0, 7), roll(p0, 7)),
            ]
            for i in range(4):
                flat[pl.ds(ey * 128 + 4 * j + i, 8, stride=16), :] = vals[i]
        return 0

    lax.fori_loop(0, 8, finish, 0)

    def scatter(e, _):
        out[e] = spread[spots[e]]
        return 0

    lax.fori_loop(0, 64, scatter, 0, unroll=8)


def sds(*shape):
    return jax.ShapeDtypeStruct(shape, F32)


def tiled(*shape):
    zeros = (0,) * (len(shape) - 1)
    return pl.BlockSpec(shape, lambda t: zeros + (t,))


def fixed(*shape):
    zeros = (0,) * len(shape)
    return pl.BlockSpec(shape, lambda t: zeros)


PARAMS = pltpu.CompilerParams(vmem_limit_bytes=VMEM_LIMIT, dimension_semantics=("arbitrary",))
SMEM = pl.BlockSpec(memory_space=pltpu.SMEM)
HBM = pl.BlockSpec(memory_space=pltpu.HBM)


def swapped(before, after, distance):
    size = lax.axis_size("sfc")
    even = (lax.axis_index("sfc") // distance) % 2 == 0
    up = [(i, (i + distance) % size) for i in range(size) if (i // distance) % 2 == 0]
    over = [(i, (i + distance) % size) for i in range(size) if (i // distance) % 2 == 1]
    one = lax.ppermute(jnp.where(even, after, before), "sfc", up + [(j, i) for i, j in up])
    two = lax.ppermute(jnp.where(even, before, after), "sfc", over + [(j, i) for i, j in over])
    return jnp.where(even, two, one), jnp.where(even, one, two)


def per_device(tracers, velocity, jacobian, elem_nodes):
    nodes = elem_nodes.T
    coef = [sds(16, 8, 8, 128)] * 4 + [sds(8, 8, 128)]
    coef_specs = [fixed(16, 8, 8, 128)] * 4 + [fixed(8, 8, 128)]
    sums_spec = tiled(27, 3, 8, 128)
    first = pl.pallas_call(
        first_kernel,
        grid=(4,),
        in_specs=[HBM, tiled(64, 16, 128), HBM, HBM],
        out_specs=[sums_spec, tiled(48, 128), tiled(48, 128), tiled(32, 128), tiled(32, 128), tiled(16, 8, 8, 128)]
        + coef_specs,
        out_shape=[sds(27, 3, 8, 512), sds(48, 512), sds(48, 512), sds(32, 512), sds(32, 512), sds(16, 8, 8, 512)]
        + coef,
        scratch_shapes=[
            pltpu.VMEM((64, 16, 128), F32),
            pltpu.VMEM((64, 16, 128), F32),
            pltpu.VMEM((64, 128), F32),
            pltpu.VMEM((16, 64), jnp.int32),
            pltpu.VMEM((16, 64), F32),
            pltpu.SMEM((16, 64), jnp.int32),
            pltpu.SMEM((64,), jnp.int32),
            pltpu.SemaphoreType.DMA((4,)),
        ],
        compiler_params=PARAMS,
        name="section_one_sums",
    )
    sums, west, east, north, south, t0, *coefs = first(nodes, tracers, velocity, jacobian.T)

    row = lax.broadcasted_iota(jnp.int32, (32, 1), 0)

    def corrected(own, from_w, from_e, y):
        return own + jnp.where(row == 0, from_w[y : y + 1], 0.0) + jnp.where(row >= 24, from_e[y : y + 1], 0.0)

    from_w, from_e = swapped(west, east, 1)
    low = lax.broadcasted_iota(jnp.int32, (8, 1), 0) < 4
    beside = [jnp.where(low, from_e[k : k + 8], from_w[k : k + 8]) for k in (32, 40)]
    msg_n = jnp.concatenate([corrected(north, from_w, from_e, 0), west[32:40], beside[0]])
    msg_s = jnp.concatenate([corrected(south, from_w, from_e, 24), west[40:48], beside[1]])
    from_n, from_s = swapped(msg_n, msg_s, PX)

    whole = pl.BlockSpec(memory_space=pltpu.VMEM)
    jac, inv = pl.pallas_call(
        geometry_kernel,
        in_specs=[whole] * 5,
        out_specs=[whole] * 2,
        out_shape=[sds(16, 12, 16, 128), sds(37, 3, 16, 128)],
        compiler_params=pltpu.CompilerParams(vmem_limit_bytes=VMEM_LIMIT),
        name="geometry",
    )(west, from_e, from_w, from_n, from_s)
    jac_spec, inv_spec = (fixed(16, 12, 16, 128), fixed(37, 3, 16, 128))

    def stage(keep, take, wide, sums, edge, from_e, from_w, from_n, from_s, rows):
        if wide:
            outs = [sds(25, 8, 512), sds(25, 8, 512), sds(8, 512), sds(32, 512)]
            specs = [tiled(25, 8, 128), tiled(25, 8, 128), tiled(8, 128), tiled(32, 128)]
        else:
            outs = [sds(32, 512)] * 4
            specs = [tiled(32, 128)] * 4
        return pl.pallas_call(
            functools.partial(stage_kernel, keep, take, wide),
            grid=(4,),
            in_specs=[sums_spec]
            + [tiled(rows, 128)] * 5
            + [inv_spec, tiled(16, 8, 8, 128)]
            + coef_specs,
            out_specs=[sums_spec] + specs,
            out_shape=[sds(27, 3, 8, 512)] + outs,
            scratch_shapes=[pltpu.VMEM((27, 3, 8, 128), F32), pltpu.VMEM((32, 128), F32)],
            compiler_params=PARAMS,
            name="section_three_sums" if wide else "section_two_sums",
        )(sums, edge, from_e, from_w, from_n, from_s, inv, t0, *coefs)

    sums, west, east, north, south = stage(
        0.75, 0.25, False, sums, east, from_e, from_w, from_n, from_s, 48
    )
    from_w, from_e = swapped(west, east, 1)
    msg_n = corrected(north, from_w, from_e, 0)
    msg_s = corrected(south, from_w, from_e, 24)
    from_n, from_s = swapped(msg_n, msg_s, PX)

    sums, west, east, _, edge = stage(
        1.0 / 3.0, 2.0 / 3.0, True, sums, east, from_e, from_w, from_n, from_s, 32
    )
    from_w, from_e = swapped(west, east, 1)
    message = tiled(25, 8, 128)
    band = tiled(7, 40, 128)
    msg_n, msg_s = pl.pallas_call(
        rows_kernel,
        grid=(4,),
        in_specs=[sums_spec, tiled(32, 128), message, message],
        out_specs=[band, band],
        out_shape=[sds(7, 40, 512)] * 2,
        compiler_params=PARAMS,
        name="row_bands",
    )(sums, edge, from_e, from_w)
    from_n, from_s = swapped(msg_n, msg_s, PX)
    grown = tiled(37, 3, 16, 128)
    flops = 64 * 16 * 512 * 60
    field, one, two = pl.pallas_call(
        inner_kernel,
        grid=(4,),
        in_specs=[sums_spec, tiled(32, 128), message, message, jac_spec, inv_spec],
        out_specs=[grown] * 3,
        out_shape=[sds(37, 3, 16, 512)] * 3,
        compiler_params=PARAMS,
        cost_estimate=pl.CostEstimate(flops=flops, bytes_accessed=16 * 1024 * 1024, transcendentals=0),
        name="biharmonic_inner_rows",
    )(sums, edge, from_e, from_w, jac, inv)
    return pl.pallas_call(
        last_kernel,
        grid=(4,),
        in_specs=[SMEM, band, band, jac_spec, inv_spec] + [grown] * 3,
        out_specs=tiled(64, 16, 128),
        out_shape=sds(64, 16, 512),
        scratch_shapes=[pltpu.VMEM((37, 3, 16, 128), F32)] * 3
        + [pltpu.VMEM((64, 16, 128), F32), pltpu.SMEM((64,), jnp.int32)],
        compiler_params=PARAMS,
        name="biharmonic_outer_rows",
    )(nodes, from_n, from_s, jac, inv, field, one, two)


def solution(mesh):
    in_specs = (P("sfc", None, None), P("sfc", None, None), P("sfc", None), P("sfc", None))
    out_specs = P("sfc", None, None)
    return jax.shard_map(
        per_device, mesh=mesh, in_specs=in_specs, out_specs=out_specs, check_vma=False
    )
```

```python
import functools
import jax
import jax.numpy as jnp
import numpy as np
from jax import lax
from jax.experimental import pallas as pl
from jax.experimental.pallas import tpu as pltpu
from jax.sharding import PartitionSpec as P

TT = 8
PX = 8
STEP_SIZE = 0.04
DIFFUSION = 0.0001
F32 = jnp.float32
VMEM_LIMIT = 36 * 1024 * 1024
FIRST_LIMIT = 52 * 1024 * 1024


def gll_derivative():
    points = np.array([-1.0, -np.sqrt(0.2), np.sqrt(0.2), 1.0])
    bary = np.array(
        [1.0 / np.prod([points[t] - points[p] for p in range(4) if p != t]) for t in range(4)]
    )
    deriv = np.zeros((4, 4))
    for a in range(4):
        for i in range(4):
            if a != i:
                deriv[a, i] = bary[i] / bary[a] / (points[a] - points[i])
        deriv[a, a] = -np.sum(deriv[a])
    return deriv


D = gll_derivative()
ODD_00, ODD_01 = (float(0.5 * (D[0, 0] - D[0, 3])), float(0.5 * (D[0, 1] - D[0, 2])))
ODD_10, ODD_11 = (float(0.5 * (D[1, 0] - D[1, 3])), float(0.5 * (D[1, 1] - D[1, 2])))
EVEN_0, EVEN_1 = (float(0.5 * (D[0, 0] + D[0, 3])), float(0.5 * (D[1, 0] + D[1, 3])))


def line(g0, g1, g2, g3):
    o0, o1 = (g0 - g3, g1 - g2)
    ev = (g0 + g3) - (g1 + g2)
    a = ODD_00 * o0 + ODD_01 * o1
    c = ODD_10 * o0 + ODD_11 * o1
    b = EVEN_0 * ev
    e = EVEN_1 * ev
    return a + b, c + e, c - e, a - b


def roll(x, shift):
    return pltpu.roll(x, shift % 8, 0)


def sublane():
    return lax.broadcasted_iota(jnp.int32, (8, 128), 0)


def row8(ref, y):
    return jnp.broadcast_to(ref[pl.ds(y, 1), :], (8, 128))


def tendency_step(f, u, v, rj):
    dx = [None] * 16
    for j in range(4):
        dx[4 * j : 4 * j + 4] = line(*[u(4 * j + i) * f[4 * j + i] for i in range(4)])
    out = [None] * 16
    for i in range(4):
        de = line(*[v(4 * j + i) * f[4 * j + i] for j in range(4)])
        for j in range(4):
            n = 4 * j + i
            out[n] = f[n] - rj(n) * (dx[n] + de[j])
    return out


def weighted(values):
    corner = (values[0] + values[3]) + (values[12] + values[15])
    edge = ((values[1] + values[2]) + (values[4] + values[7])) + (
        (values[8] + values[11]) + (values[13] + values[14])
    )
    inner = (values[5] + values[6]) + (values[9] + values[10])
    return corner + 5.0 * edge + 25.0 * inner


def limited(g, jac, rden):
    mean = weighted([jac[n] * g[n] for n in range(16)]) * rden
    lows = list(g)
    while len(lows) > 1:
        lows = [jnp.minimum(lows[k], lows[k + 1]) for k in range(0, len(lows), 2)]
    low = lows[0]
    positive = jnp.maximum(mean, 0.0)
    negative = low < 0.0
    denominator = jnp.where(negative, positive - low, 1.0)
    scaling = jnp.where(negative, positive / denominator, 1.0)
    return [jac[n] * (mean + scaling * (g[n] - mean)) for n in range(16)]


def add_nodes(sums, edge, ey, c, sub, joins=(0,)):
    for j in range(4):
        c0, c1, c2, c3 = c[4 * j : 4 * j + 4]
        c0 = c0 + jnp.where(sub == 0, 0.0, roll(c3, 1))
        last = c3[7:8, :]
        y = 3 * ey + j
        if j in joins:
            c0, c1, c2 = (c0 + sums[y, 0], c1 + sums[y, 1], c2 + sums[y, 2])
            last = last + edge[pl.ds(y, 1), :]
        sums[y, 0] = c0
        sums[y, 1] = c1
        sums[y, 2] = c2
        edge[pl.ds(y, 1), :] = last


def clear_first(sums, edge, y=0):
    for ii in range(3):
        sums[y, ii] = jnp.zeros((8, 128), F32)
    edge[y : y + 1, :] = jnp.zeros((1, 128), F32)


def thin_messages(sums, edge, west, north, south):
    def copy(y, _):
        west[pl.ds(y, 1), :] = sums[y, 0, 0:1, :]
        return 0

    lax.fori_loop(0, 25, copy, 0, unroll=5)
    for out, y in ((north, 0), (south, 24)):
        for ii in range(3):
            out[8 * ii : 8 * ii + 8, :] = sums[y, ii]
        out[24:32, :] = row8(edge, y)


def place(corner):
    ey = (corner * 874) >> 16
    return 8 * ey + (((corner - 75 * ey) * 21846) >> 16)


def fill_places(nodes, spots):
    def body(e, _):
        spots[e] = place(nodes[0, e])
        return 0

    lax.fori_loop(0, 64, body, 0, unroll=8)


def first_kernel(
    nodes, x, vel, jin, sums, west, east, north, south, t0, u_ref, v_ref, rj_ref, j_ref, rd_ref,
    gathered, winds, jc, node_rows, j_rows, corners, spots, sem,
):
    step = pl.program_id(0)
    sub = sublane()
    lane = lax.broadcasted_iota(jnp.int32, (8, 128), 1)

    @pl.when(step == 0)
    def _():
        copies = [
            pltpu.make_async_copy(nodes, corners, sem.at[0]),
            pltpu.make_async_copy(nodes, node_rows, sem.at[1]),
            pltpu.make_async_copy(jin, j_rows, sem.at[2]),
            pltpu.make_async_copy(vel, gathered, sem.at[3]),
        ]
        for copy in copies:
            copy.start()
        jc[...] = jnp.zeros_like(jc)
        for copy in copies[:3]:
            copy.wait()
        fill_places(corners, spots)
        to = place(node_rows[0:1, :])
        hit = (lax.broadcasted_iota(jnp.int32, (64, 64), 0) == to).astype(F32)
        jc[:, 0:16] = lax.dot_general(
            hit, j_rows[...], (((1,), (1,)), ((), ())), precision=lax.Precision.HIGHEST, preferred_element_type=F32
        )
        copies[3].wait()

        def order(e, _):
            winds[spots[e]] = gathered[e]
            return 0

        lax.fori_loop(0, 64, order, 0, unroll=8)
        flat = winds.reshape(1024, 128)

        def coef(ey, _):
            comp = jc[pl.ds(pl.multiple_of(8 * ey, 8), 8), :]
            js = []
            for n in range(16):
                jv = jnp.broadcast_to(comp[:, n : n + 1], (8, 128))
                w = flat[pl.ds(ey * 128 + n, 8, stride=16), :]
                wr = pltpu.roll(w, 64, 1)
                dj = STEP_SIZE * jv
                u_ref[n, ey] = dj * jnp.where(lane < 64, w, wr)
                v_ref[n, ey] = dj * jnp.where(lane < 64, wr, w)
                j_ref[n, ey] = jv
                rj_ref[n, ey] = 1.0 / jv
                js.append(jv)
            rd_ref[ey] = 1.0 / weighted(js)
            return 0

        lax.fori_loop(0, 8, coef, 0)

    def gather(e, _):
        gathered[spots[e]] = x[e]
        return 0

    lax.fori_loop(0, 64, gather, 0, unroll=8)
    flat = gathered.reshape(1024, 128)
    clear_first(sums, east)

    def rows(ey, _):
        f = [flat[pl.ds(ey * 128 + n, 8, stride=16), :] for n in range(16)]
        for n in range(16):
            t0[n, ey] = f[n]
        g = tendency_step(
            f, lambda n: u_ref[n, ey], lambda n: v_ref[n, ey], lambda n: rj_ref[n, ey]
        )
        c = limited(g, [j_ref[n, ey] for n in range(16)], rd_ref[ey])
        add_nodes(sums, east, ey, c, sub)
        return 0

    lax.fori_loop(0, 8, rows, 0, unroll=8)
    thin_messages(sums, east, west, north, south)
    for out in (west, east):
        for half in range(2):
            out[32 + 8 * half : 40 + 8 * half, :] = jc[
                pl.ds(pl.multiple_of(8 * (4 * half + step), 8), 8), :
            ]


def own_geometry_kernel(own, from_e, from_w, inv):
    geometry_rows(own, from_e, from_w, None, None, None, inv, 0, 8)


def geometry_kernel(own, from_e, from_w, from_n, from_s, j_ref, inv):
    geometry_rows(own, from_e, from_w, from_n, from_s, j_ref, inv, -3, 11)


def geometry_rows(own, from_e, from_w, from_n, from_s, j_ref, inv, first, last):
    sub = sublane()

    def tile(ref, base, t):
        return ref[base : base + 8, 128 * t : 128 * t + 128]

    pending = None
    for r in range(first, last):
        if r < 0:
            t = r + 4
            a, b = (tile(from_n, 32, t), tile(from_n, 40, t))
        elif r > 7:
            t = r - 8
            a, b = (tile(from_s, 32, t), tile(from_s, 40, t))
        else:
            base, t = (32 + 8 * (r // 4), r % 4)
            a = tile(own, base, t)
            b = jnp.where(sub < 4, tile(from_e, base, t), tile(from_w, base, t))
        kept = None
        for j in range(4):
            ca = [jnp.broadcast_to(a[:, 4 * j + i : 4 * j + i + 1], (8, 128)) for i in range(4)]
            cb = [jnp.broadcast_to(b[:, 4 * j + i : 4 * j + i + 1], (8, 128)) for i in range(4)]
            if j_ref is not None and -2 <= r <= 9:
                for i in range(4):
                    j_ref[4 * j + i, r + 2, 0:8] = ca[i]
                    j_ref[4 * j + i, r + 2, 8:16] = cb[i]
            ra, rb = (roll(ca[3], 1), roll(cb[3], 1))
            row = [
                ca[0] + jnp.where(sub == 0, rb, ra),
                cb[0] + jnp.where(sub == 0, ra, rb),
                ca[1],
                cb[1],
                ca[2],
                cb[2],
            ]
            if j == 3:
                kept = row
                continue
            if j == 0 and pending is not None:
                row = [p + q for p, q in zip(row, pending)]
            y = 3 * r + j + 6
            if 0 <= y <= 36:
                for ii in range(3):
                    inv[y, ii, 0:8] = 1.0 / row[2 * ii]
                    inv[y, ii, 8:16] = 1.0 / row[2 * ii + 1]
        pending = kept


def node_values(sums, edge, from_e, from_w, inv, whole, side, first, last, sub):
    def body(y, _):
        whole[y, 0] = (sums[y, 0] + jnp.where(sub == 0, row8(from_w, y), 0.0)) * inv[y + 6, 0, 0:8]
        whole[y, 1] = sums[y, 1] * inv[y + 6, 1, 0:8]
        whole[y, 2] = sums[y, 2] * inv[y + 6, 2, 0:8]
        side[pl.ds(y, 1), :] = (edge[pl.ds(y, 1), :] + from_e[pl.ds(y, 1), :]) * inv[y + 6, 0, 8:9]
        return 0

    lax.fori_loop(first, last, body, 0, unroll=4)


def add_row(whole, side, msg, inv, y):
    for ii in range(3):
        whole[y, ii] = whole[y, ii] + msg[8 * ii : 8 * ii + 8, :] * inv[y + 6, ii, 0:8]
    side[y : y + 1, :] = side[y : y + 1, :] + msg[24:25, :] * inv[y + 6, 0, 8:9]


def element_values(whole, side, ey, sub):
    f = []
    for j in range(4):
        y = 3 * ey + j
        p0 = whole[y, 0]
        f += [p0, whole[y, 1], whole[y, 2], jnp.where(sub == 7, row8(side, y), roll(p0, 7))]
    return f


def stage_row(keep, take, whole, side, t0, u_ref, v_ref, rj_ref, j_ref, rd_ref, ey, sub):
    f = element_values(whole, side, ey, sub)
    h = tendency_step(f, lambda n: u_ref[n, ey], lambda n: v_ref[n, ey], lambda n: rj_ref[n, ey])
    g = [keep * t0[n, ey] + take * h[n] for n in range(16)]
    return limited(g, [j_ref[n, ey] for n in range(16)], rd_ref[ey])


def stage_inner_kernel(
    keep, take, sums, edge, from_e, from_w, inv, t0, u_ref, v_ref, rj_ref, j_ref, rd_ref, out, column, whole, side
):
    sub = sublane()
    node_values(sums, edge, from_e, from_w, inv, whole, side, 3, 22, sub)
    clear_first(out, column, 3)

    def rows(ey, _):
        c = stage_row(keep, take, whole, side, t0, u_ref, v_ref, rj_ref, j_ref, rd_ref, ey, sub)
        add_nodes(out, column, ey, c, sub)
        return 0

    lax.fori_loop(1, 7, rows, 0, unroll=6)


def stage_kernel(
    keep, take, wide, sums, edge, from_e, from_w, from_n, from_s, inv, t0, u_ref, v_ref, rj_ref, j_ref, rd_ref,
    inner, inner_column, out, west, east, third, fourth, whole, side,
):
    sub = sublane()
    node_values(sums, edge, from_e, from_w, inv, whole, side, 0, 4, sub)
    node_values(sums, edge, from_e, from_w, inv, whole, side, 21, 25, sub)
    add_row(whole, side, from_n, inv, 0)
    add_row(whole, side, from_s, inv, 24)
    column = fourth if wide else east

    def copy(y, _):
        for ii in range(3):
            out[y, ii] = inner[y, ii]
        column[pl.ds(y, 1), :] = inner_column[pl.ds(y, 1), :]
        return 0

    lax.fori_loop(3, 22, copy, 0, unroll=19)
    for ey, joins in ((0, (3,)), (7, (0,))):
        c = stage_row(keep, take, whole, side, t0, u_ref, v_ref, rj_ref, j_ref, rd_ref, ey, sub)
        add_nodes(out, column, ey, c, sub, joins)
    if not wide:
        thin_messages(out, column, west, third, fourth)
        return

    def pack(y, _):
        p0, p1, p2 = (out[y, 0], out[y, 1], out[y, 2])
        west[y] = jnp.where(sub < 3, p0, jnp.where(sub < 5, roll(p1, 3), roll(p2, 5)))
        east[y] = jnp.where(
            sub >= 6,
            p0,
            jnp.where(sub >= 4, roll(p1, -2), jnp.where(sub >= 2, roll(p2, -4), row8(column, y))),
        )
        return 0

    lax.fori_loop(0, 25, pack, 0, unroll=5)


def joined_row(sums, edge, from_e, from_w, y, sub):
    me, mw = (from_e[y], from_w[y])
    a0 = sums[y, 0] + jnp.where(sub == 0, mw, 0.0)
    b0 = jnp.where(sub == 0, row8(edge, y) + me, jnp.where(sub < 4, me, mw))
    b1 = jnp.where(sub < 4, roll(me, -3), roll(mw, 2))
    b2 = jnp.where(sub < 4, roll(me, -5), roll(mw, 4))
    return a0, sums[y, 1], sums[y, 2], b0, b1, b2


def rows_kernel(sums, edge, from_e, from_w, north, south):
    sub = sublane()
    for out, first in ((north, 0), (south, 18)):
        for k in range(7):
            a0, a1, a2, b0, b1, b2 = joined_row(sums, edge, from_e, from_w, first + k, sub)
            out[k, 0:8] = a0
            out[k, 8:16] = a1
            out[k, 16:24] = a2
            out[k, 24:32] = b0
            out[k, 32:40] = jnp.where((sub < 2) | (sub >= 6), b1, roll(b2, 4))


def laplace_core(f, jac):
    out = [None] * 16
    for j in range(4):
        d = line(*[f(4 * j + i) for i in range(4)])
        out[4 * j : 4 * j + 4] = line(*[jac(4 * j + i) * d[i] for i in range(4)])
    for i in range(4):
        d = line(*[f(4 * j + i) for j in range(4)])
        d = line(*[jac(4 * j + i) * d[j] for j in range(4)])
        for j in range(4):
            out[4 * j + i] = out[4 * j + i] + d[j]
    return out


FIRST, JOIN, SKIP = range(3)


def laplace_row(src, j_ref, inv, dst, r, top, bottom, sub, at=(0, 0), narrow=False):
    fa, fb = ([], [])
    for j in range(4):
        y = 3 * r + j - at[0]
        pa, pb = (src[y, 0, 0:8], src[y, 0, 8:16])
        ra, rb = (roll(pa, 7), roll(pb, 7))
        fa += [pa, src[y, 1, 0:8], src[y, 2, 0:8], jnp.where(sub == 7, rb, ra)]
        fb += [pb, src[y, 1, 8:16], src[y, 2, 8:16], jnp.where(sub == 7, ra, rb)]
    ca = laplace_core(lambda n: fa[n], lambda n: j_ref[n, r, 0:8])
    cb = laplace_core(lambda n: fb[n], lambda n: j_ref[n, r, 8:16])
    for j in range(4):
        what = {0: top, 3: bottom}.get(j)
        if what == SKIP:
            continue
        y = 3 * r + j
        ra, rb = (roll(ca[4 * j + 3], 1), roll(cb[4 * j + 3], 1))
        row = [
            (ca[4 * j] + jnp.where(sub == 0, rb, ra), cb[4 * j] + jnp.where(sub == 0, ra, rb)),
            (ca[4 * j + 1], cb[4 * j + 1]),
            (ca[4 * j + 2], cb[4 * j + 2]),
        ]
        z = y - at[1]
        for ii in range(3):
            for part, rows in zip(row[ii], (slice(0, 8), slice(8, 16))):
                if narrow and ii and rows.start:
                    continue
                if what == JOIN:
                    part = part + dst[z, ii, rows]
                if what != FIRST:
                    part = part * inv[y, ii, rows]
                dst[z, ii, rows] = part


def own_rows(sums, edge, from_e, from_w, inv, field, first, last, sub):
    def body(y, _):
        a0, a1, a2, b0, b1, b2 = joined_row(sums, edge, from_e, from_w, y, sub)
        for ii, (a, b) in enumerate(((a0, b0), (a1, b1), (a2, b2))):
            field[y, ii, 0:8] = a * inv[y + 6, ii, 0:8]
            field[y, ii, 8:16] = b * inv[y + 6, ii, 8:16]
        return 0

    lax.fori_loop(first, last, body, 0)


def inner_kernel(sums, edge, from_e, from_w, j_ref, inv, field, one, two):
    sub = sublane()
    own_rows(sums, edge, from_e, from_w, inv, field, 0, 25, sub)
    laplace_row(field, j_ref, inv, one, 3, FIRST, FIRST, sub, (6, 9))

    def rows_one(r, _):
        laplace_row(field, j_ref, inv, one, r, JOIN, FIRST, sub, (6, 9))
        return 0

    lax.fori_loop(4, 9, rows_one, 0, unroll=5)
    laplace_row(one, j_ref, inv, two, 4, FIRST, FIRST, sub, (9, 12), True)

    def rows_two(r, _):
        laplace_row(one, j_ref, inv, two, r, JOIN, FIRST, sub, (9, 12), True)
        return 0

    lax.fori_loop(5, 8, rows_two, 0, unroll=3)


def last_kernel(
    nodes, from_n, from_s, j_ref, inv, field_in, one_in, two_in, out, field, one, two, spread, spots
):
    sub = sublane()

    @pl.when(pl.program_id(0) == 0)
    def _():
        fill_places(nodes, spots)

    def copy_rows(src, dst, first, last):
        def body(y, _):
            for ii in range(3):
                dst[y, ii] = src[y - first, ii]
            return 0

        lax.fori_loop(first, last, body, 0, unroll=4)

    copy_rows(field_in, field, 6, 31)
    for msg, first, shared in ((from_n, 0, 6), (from_s, 30, 0)):
        for k in range(7):
            y = first + k
            c = msg[k, 32:40]
            parts = [msg[k, 0:8], msg[k, 24:32], msg[k, 8:16], c, msg[k, 16:24], roll(c, 4)]
            for ii in range(3):
                a, b = (parts[2 * ii] * inv[y, ii, 0:8], parts[2 * ii + 1] * inv[y, ii, 8:16])
                if k == shared:
                    a, b = (a + field[y, ii, 0:8], b + field[y, ii, 8:16])
                field[y, ii, 0:8] = a
                field[y, ii, 8:16] = b
    copy_rows(one_in, one, 9, 28)
    laplace_row(field, j_ref, inv, one, 0, SKIP, FIRST, sub)
    laplace_row(field, j_ref, inv, one, 1, JOIN, FIRST, sub)
    laplace_row(field, j_ref, inv, one, 2, JOIN, JOIN, sub)
    laplace_row(field, j_ref, inv, one, 9, JOIN, FIRST, sub)
    laplace_row(field, j_ref, inv, one, 10, JOIN, FIRST, sub)
    laplace_row(field, j_ref, inv, one, 11, JOIN, SKIP, sub)
    copy_rows(two_in, two, 12, 25)
    laplace_row(one, j_ref, inv, two, 1, SKIP, FIRST, sub, narrow=True)
    laplace_row(one, j_ref, inv, two, 2, JOIN, FIRST, sub, narrow=True)
    laplace_row(one, j_ref, inv, two, 3, JOIN, JOIN, sub, narrow=True)
    laplace_row(one, j_ref, inv, two, 8, JOIN, FIRST, sub, narrow=True)
    laplace_row(one, j_ref, inv, two, 9, JOIN, FIRST, sub, narrow=True)
    laplace_row(one, j_ref, inv, two, 10, JOIN, SKIP, sub, narrow=True)
    flat = spread.reshape(1024, 128)

    def finish(ey, _):
        for j in range(4):
            y = 3 * ey + j + 6
            p0 = field[y, 0, 0:8] - DIFFUSION * two[y, 0, 0:8]
            q0 = field[y, 0, 8:16] - DIFFUSION * two[y, 0, 8:16]
            vals = [
                p0,
                field[y, 1, 0:8] - DIFFUSION * two[y, 1, 0:8],
                field[y, 2, 0:8] - DIFFUSION * two[y, 2, 0:8],
                jnp.where(sub == 7, roll(q0, 7), roll(p0, 7)),
            ]
            for i in range(4):
                flat[pl.ds(ey * 128 + 4 * j + i, 8, stride=16), :] = vals[i]
        return 0

    lax.fori_loop(0, 8, finish, 0)

    def scatter(e, _):
        out[e] = spread[spots[e]]
        return 0

    lax.fori_loop(0, 64, scatter, 0, unroll=8)


def sds(*shape):
    return jax.ShapeDtypeStruct(shape, F32)


def tiled(*shape):
    zeros = (0,) * (len(shape) - 1)
    return pl.BlockSpec(shape, lambda t: zeros + (t,))


def fixed(*shape):
    zeros = (0,) * len(shape)
    return pl.BlockSpec(shape, lambda t: zeros)


PARAMS = pltpu.CompilerParams(vmem_limit_bytes=VMEM_LIMIT, dimension_semantics=("arbitrary",))
SMEM = pl.BlockSpec(memory_space=pltpu.SMEM)
HBM = pl.BlockSpec(memory_space=pltpu.HBM)


def swapped(before, after, distance):
    size = lax.axis_size("sfc")
    even = (lax.axis_index("sfc") // distance) % 2 == 0
    up = [(i, (i + distance) % size) for i in range(size) if (i // distance) % 2 == 0]
    over = [(i, (i + distance) % size) for i in range(size) if (i // distance) % 2 == 1]
    one = lax.ppermute(jnp.where(even, after, before), "sfc", up + [(j, i) for i, j in up])
    two = lax.ppermute(jnp.where(even, before, after), "sfc", over + [(j, i) for i, j in over])
    return jnp.where(even, two, one), jnp.where(even, one, two)


def per_device(tracers, velocity, jacobian, elem_nodes):
    nodes = elem_nodes.T
    coef = [sds(16, 8, 8, 128)] * 4 + [sds(8, 8, 128)]
    coef_specs = [fixed(16, 8, 8, 128)] * 4 + [fixed(8, 8, 128)]
    sums_spec = tiled(27, 3, 8, 128)
    first = pl.pallas_call(
        first_kernel,
        grid=(4,),
        in_specs=[HBM, tiled(64, 16, 128), HBM, HBM],
        out_specs=[sums_spec, tiled(48, 128), tiled(48, 128), tiled(32, 128), tiled(32, 128), tiled(16, 8, 8, 128)]
        + coef_specs,
        out_shape=[sds(27, 3, 8, 512), sds(48, 512), sds(48, 512), sds(32, 512), sds(32, 512), sds(16, 8, 8, 512)]
        + coef,
        scratch_shapes=[
            pltpu.VMEM((64, 16, 128), F32),
            pltpu.VMEM((64, 16, 128), F32),
            pltpu.VMEM((64, 128), F32),
            pltpu.VMEM((16, 64), jnp.int32),
            pltpu.VMEM((16, 64), F32),
            pltpu.SMEM((16, 64), jnp.int32),
            pltpu.SMEM((64,), jnp.int32),
            pltpu.SemaphoreType.DMA((4,)),
        ],
        compiler_params=pltpu.CompilerParams(vmem_limit_bytes=FIRST_LIMIT, dimension_semantics=("arbitrary",)),
        name="section_one_sums",
    )
    sums, west, east, north, south, t0, *coefs = first(nodes, tracers, velocity, jacobian.T)

    row = lax.broadcasted_iota(jnp.int32, (32, 1), 0)

    def corrected(own, from_w, from_e, y):
        return own + jnp.where(row == 0, from_w[y : y + 1], 0.0) + jnp.where(row >= 24, from_e[y : y + 1], 0.0)

    from_w, from_e = swapped(west, east, 1)
    low = lax.broadcasted_iota(jnp.int32, (8, 1), 0) < 4
    beside = [jnp.where(low, from_e[k : k + 8], from_w[k : k + 8]) for k in (32, 40)]
    msg_n = jnp.concatenate([corrected(north, from_w, from_e, 0), west[32:40], beside[0]])
    msg_s = jnp.concatenate([corrected(south, from_w, from_e, 24), west[40:48], beside[1]])
    from_n, from_s = swapped(msg_n, msg_s, PX)

    whole = pl.BlockSpec(memory_space=pltpu.VMEM)
    inv_inner = pl.pallas_call(
        own_geometry_kernel,
        in_specs=[whole] * 3,
        out_specs=whole,
        out_shape=sds(37, 3, 16, 128),
        compiler_params=pltpu.CompilerParams(vmem_limit_bytes=VMEM_LIMIT),
        name="inner_geometry",
    )(west, from_e, from_w)
    jac, inv = pl.pallas_call(
        geometry_kernel,
        in_specs=[whole] * 5,
        out_specs=[whole] * 2,
        out_shape=[sds(16, 12, 16, 128), sds(37, 3, 16, 128)],
        compiler_params=pltpu.CompilerParams(vmem_limit_bytes=VMEM_LIMIT),
        name="geometry",
    )(west, from_e, from_w, from_n, from_s)
    jac_spec, inv_spec = (fixed(16, 12, 16, 128), fixed(37, 3, 16, 128))

    def inner_stage(keep, take, sums, edge, from_e, from_w, inv, rows):
        return pl.pallas_call(
            functools.partial(stage_inner_kernel, keep, take),
            grid=(4,),
            in_specs=[sums_spec] + [tiled(rows, 128)] * 3 + [inv_spec, tiled(16, 8, 8, 128)] + coef_specs,
            out_specs=[sums_spec, tiled(32, 128)],
            out_shape=[sds(27, 3, 8, 512), sds(32, 512)],
            scratch_shapes=[pltpu.VMEM((27, 3, 8, 128), F32), pltpu.VMEM((32, 128), F32)],
            compiler_params=PARAMS,
            cost_estimate=pl.CostEstimate(
                flops=64 * 16 * 512 * 60, bytes_accessed=8 * 1024 * 1024, transcendentals=0
            ),
            name="inner_rows",
        )(sums, edge, from_e, from_w, inv, t0, *coefs)

    def stage(keep, take, wide, sums, edge, from_e, from_w, from_n, from_s, rows, inner):
        if wide:
            outs = [sds(25, 8, 512), sds(25, 8, 512), sds(8, 512), sds(32, 512)]
            specs = [tiled(25, 8, 128), tiled(25, 8, 128), tiled(8, 128), tiled(32, 128)]
        else:
            outs = [sds(32, 512)] * 4
            specs = [tiled(32, 128)] * 4
        return pl.pallas_call(
            functools.partial(stage_kernel, keep, take, wide),
            grid=(4,),
            in_specs=[sums_spec]
            + [tiled(rows, 128)] * 5
            + [inv_spec, tiled(16, 8, 8, 128)]
            + coef_specs
            + [sums_spec, tiled(32, 128)],
            out_specs=[sums_spec] + specs,
            out_shape=[sds(27, 3, 8, 512)] + outs,
            scratch_shapes=[pltpu.VMEM((27, 3, 8, 128), F32), pltpu.VMEM((32, 128), F32)],
            compiler_params=PARAMS,
            name="section_three_sums" if wide else "section_two_sums",
        )(sums, edge, from_e, from_w, from_n, from_s, inv, t0, *coefs, *inner)

    inner = inner_stage(0.75, 0.25, sums, east, from_e, from_w, inv_inner, 48)
    sums, west, east, north, south = stage(
        0.75, 0.25, False, sums, east, from_e, from_w, from_n, from_s, 48, inner
    )
    from_w, from_e = swapped(west, east, 1)
    msg_n = corrected(north, from_w, from_e, 0)
    msg_s = corrected(south, from_w, from_e, 24)
    from_n, from_s = swapped(msg_n, msg_s, PX)

    inner = inner_stage(1.0 / 3.0, 2.0 / 3.0, sums, east, from_e, from_w, inv, 32)
    sums, west, east, _, edge = stage(
        1.0 / 3.0, 2.0 / 3.0, True, sums, east, from_e, from_w, from_n, from_s, 32, inner
    )
    from_w, from_e = swapped(west, east, 1)
    message = tiled(25, 8, 128)
    band = tiled(7, 40, 128)
    msg_n, msg_s = pl.pallas_call(
        rows_kernel,
        grid=(4,),
        in_specs=[sums_spec, tiled(32, 128), message, message],
        out_specs=[band, band],
        out_shape=[sds(7, 40, 512)] * 2,
        compiler_params=PARAMS,
        name="row_bands",
    )(sums, edge, from_e, from_w)
    from_n, from_s = swapped(msg_n, msg_s, PX)
    grown = [(25, 3, 16), (19, 3, 16), (13, 3, 16)]
    flops = 64 * 16 * 512 * 60
    field, one, two = pl.pallas_call(
        inner_kernel,
        grid=(4,),
        in_specs=[sums_spec, tiled(32, 128), message, message, jac_spec, inv_spec],
        out_specs=[tiled(*g, 128) for g in grown],
        out_shape=[sds(*g, 512) for g in grown],
        compiler_params=PARAMS,
        cost_estimate=pl.CostEstimate(flops=flops, bytes_accessed=16 * 1024 * 1024, transcendentals=0),
        name="biharmonic_inner_rows",
    )(sums, edge, from_e, from_w, jac, inv)
    return pl.pallas_call(
        last_kernel,
        grid=(4,),
        in_specs=[SMEM, band, band, jac_spec, inv_spec] + [tiled(*g, 128) for g in grown],
        out_specs=tiled(64, 16, 128),
        out_shape=sds(64, 16, 512),
        scratch_shapes=[pltpu.VMEM((37, 3, 16, 128), F32)] * 3
        + [pltpu.VMEM((64, 16, 128), F32), pltpu.SMEM((64,), jnp.int32)],
        compiler_params=PARAMS,
        name="biharmonic_outer_rows",
    )(nodes, from_n, from_s, jac, inv, field, one, two)


def solution(mesh):
    in_specs = (P("sfc", None, None), P("sfc", None, None), P("sfc", None), P("sfc", None))
    out_specs = P("sfc", None, None)
    return jax.shard_map(
        per_device, mesh=mesh, in_specs=in_specs, out_specs=out_specs, check_vma=False
    )
```

```python
import functools
import jax
import jax.numpy as jnp
import numpy as np
from jax import lax
from jax.experimental import pallas as pl
from jax.experimental.pallas import tpu as pltpu
from jax.sharding import PartitionSpec as P

TT = 8
PX = 8
STEP_SIZE = 0.04
DIFFUSION = 0.0001
F32 = jnp.float32
VMEM_LIMIT = 36 * 1024 * 1024
FIRST_LIMIT = 52 * 1024 * 1024


def gll_derivative():
    points = np.array([-1.0, -np.sqrt(0.2), np.sqrt(0.2), 1.0])
    bary = np.array(
        [1.0 / np.prod([points[t] - points[p] for p in range(4) if p != t]) for t in range(4)]
    )
    deriv = np.zeros((4, 4))
    for a in range(4):
        for i in range(4):
            if a != i:
                deriv[a, i] = bary[i] / bary[a] / (points[a] - points[i])
        deriv[a, a] = -np.sum(deriv[a])
    return deriv


D = gll_derivative()
ODD_00, ODD_01 = (float(0.5 * (D[0, 0] - D[0, 3])), float(0.5 * (D[0, 1] - D[0, 2])))
ODD_10, ODD_11 = (float(0.5 * (D[1, 0] - D[1, 3])), float(0.5 * (D[1, 1] - D[1, 2])))
EVEN_0, EVEN_1 = (float(0.5 * (D[0, 0] + D[0, 3])), float(0.5 * (D[1, 0] + D[1, 3])))


def line(g0, g1, g2, g3):
    o0, o1 = (g0 - g3, g1 - g2)
    ev = (g0 + g3) - (g1 + g2)
    a = ODD_00 * o0 + ODD_01 * o1
    c = ODD_10 * o0 + ODD_11 * o1
    b = EVEN_0 * ev
    e = EVEN_1 * ev
    return a + b, c + e, c - e, a - b


def roll(x, shift):
    return pltpu.roll(x, shift % 8, 0)


def sublane():
    return lax.broadcasted_iota(jnp.int32, (8, 128), 0)


def row8(ref, y):
    return jnp.broadcast_to(ref[pl.ds(y, 1), :], (8, 128))


def tendency_step(f, u, v, rj):
    dx = [None] * 16
    for j in range(4):
        dx[4 * j : 4 * j + 4] = line(*[u(4 * j + i) * f[4 * j + i] for i in range(4)])
    out = [None] * 16
    for i in range(4):
        de = line(*[v(4 * j + i) * f[4 * j + i] for j in range(4)])
        for j in range(4):
            n = 4 * j + i
            out[n] = f[n] - rj(n) * (dx[n] + de[j])
    return out


def weighted(values):
    corner = (values[0] + values[3]) + (values[12] + values[15])
    edge = ((values[1] + values[2]) + (values[4] + values[7])) + (
        (values[8] + values[11]) + (values[13] + values[14])
    )
    inner = (values[5] + values[6]) + (values[9] + values[10])
    return corner + 5.0 * edge + 25.0 * inner


def limited(g, jac, rden):
    mean = weighted([jac[n] * g[n] for n in range(16)]) * rden
    lows = list(g)
    while len(lows) > 1:
        lows = [jnp.minimum(lows[k], lows[k + 1]) for k in range(0, len(lows), 2)]
    low = lows[0]
    positive = jnp.maximum(mean, 0.0)
    negative = low < 0.0
    denominator = jnp.where(negative, positive - low, 1.0)
    scaling = jnp.where(negative, positive / denominator, 1.0)
    return [jac[n] * (mean + scaling * (g[n] - mean)) for n in range(16)]


def add_nodes(sums, edge, ey, c, sub, joins=(0,)):
    for j in range(4):
        c0, c1, c2, c3 = c[4 * j : 4 * j + 4]
        c0 = c0 + jnp.where(sub == 0, 0.0, roll(c3, 1))
        last = c3[7:8, :]
        y = 3 * ey + j
        if j in joins:
            c0, c1, c2 = (c0 + sums[y, 0], c1 + sums[y, 1], c2 + sums[y, 2])
            last = last + edge[pl.ds(y, 1), :]
        sums[y, 0] = c0
        sums[y, 1] = c1
        sums[y, 2] = c2
        edge[pl.ds(y, 1), :] = last


def clear_first(sums, edge, y=0):
    for ii in range(3):
        sums[y, ii] = jnp.zeros((8, 128), F32)
    edge[y : y + 1, :] = jnp.zeros((1, 128), F32)


def thin_messages(sums, edge, west, north, south):
    def copy(y, _):
        west[pl.ds(y, 1), :] = sums[y, 0, 0:1, :]
        return 0

    lax.fori_loop(0, 25, copy, 0, unroll=5)
    for out, y in ((north, 0), (south, 24)):
        for ii in range(3):
            out[8 * ii : 8 * ii + 8, :] = sums[y, ii]
        out[24:32, :] = row8(edge, y)


def place(corner):
    ey = (corner * 874) >> 16
    return 8 * ey + (((corner - 75 * ey) * 21846) >> 16)


def fill_places(nodes, spots):
    def body(e, _):
        spots[e] = place(nodes[0, e])
        return 0

    lax.fori_loop(0, 64, body, 0, unroll=8)


def first_kernel(
    corners, node_rows, x, vel, j_rows, sums, west, east, north, south, t0, u_ref, v_ref, rj_ref, j_ref, rd_ref,
    gathered, winds, jc, spots,
):
    step = pl.program_id(0)
    sub = sublane()
    lane = lax.broadcasted_iota(jnp.int32, (8, 128), 1)

    @pl.when(step == 0)
    def _():
        jc[...] = jnp.zeros_like(jc)
        fill_places(corners, spots)
        to = place(node_rows[0:1, :])
        hit = (lax.broadcasted_iota(jnp.int32, (64, 64), 0) == to).astype(F32)
        jc[:, 0:16] = lax.dot_general(
            hit, j_rows[...], (((1,), (1,)), ((), ())), precision=lax.Precision.HIGHEST, preferred_element_type=F32
        )

        def order(e, _):
            winds[spots[e]] = vel[e]
            return 0

        lax.fori_loop(0, 64, order, 0, unroll=8)
        flat = winds.reshape(1024, 128)

        def coef(ey, _):
            comp = jc[pl.ds(pl.multiple_of(8 * ey, 8), 8), :]
            js = []
            for n in range(16):
                jv = jnp.broadcast_to(comp[:, n : n + 1], (8, 128))
                w = flat[pl.ds(ey * 128 + n, 8, stride=16), :]
                wr = pltpu.roll(w, 64, 1)
                dj = STEP_SIZE * jv
                u_ref[n, ey] = dj * jnp.where(lane < 64, w, wr)
                v_ref[n, ey] = dj * jnp.where(lane < 64, wr, w)
                j_ref[n, ey] = jv
                rj_ref[n, ey] = 1.0 / jv
                js.append(jv)
            rd_ref[ey] = 1.0 / weighted(js)
            return 0

        lax.fori_loop(0, 8, coef, 0)

    def gather(e, _):
        gathered[spots[e]] = x[e]
        return 0

    lax.fori_loop(0, 64, gather, 0, unroll=8)
    flat = gathered.reshape(1024, 128)
    clear_first(sums, east)

    def rows(ey, _):
        f = [flat[pl.ds(ey * 128 + n, 8, stride=16), :] for n in range(16)]
        for n in range(16):
            t0[n, ey] = f[n]
        g = tendency_step(
            f, lambda n: u_ref[n, ey], lambda n: v_ref[n, ey], lambda n: rj_ref[n, ey]
        )
        c = limited(g, [j_ref[n, ey] for n in range(16)], rd_ref[ey])
        add_nodes(sums, east, ey, c, sub)
        return 0

    lax.fori_loop(0, 8, rows, 0, unroll=8)
    thin_messages(sums, east, west, north, south)
    for out in (west, east):
        for half in range(2):
            out[32 + 8 * half : 40 + 8 * half, :] = jc[
                pl.ds(pl.multiple_of(8 * (4 * half + step), 8), 8), :
            ]


def own_geometry_kernel(own, from_e, from_w, inv):
    geometry_rows(own, from_e, from_w, None, None, None, inv, 0, 8)


def geometry_kernel(own, from_e, from_w, from_n, from_s, j_ref, inv):
    geometry_rows(own, from_e, from_w, from_n, from_s, j_ref, inv, -3, 11)


def geometry_rows(own, from_e, from_w, from_n, from_s, j_ref, inv, first, last):
    sub = sublane()

    def tile(ref, base, t):
        return ref[base : base + 8, 128 * t : 128 * t + 128]

    pending = None
    for r in range(first, last):
        if r < 0:
            t = r + 4
            a, b = (tile(from_n, 32, t), tile(from_n, 40, t))
        elif r > 7:
            t = r - 8
            a, b = (tile(from_s, 32, t), tile(from_s, 40, t))
        else:
            base, t = (32 + 8 * (r // 4), r % 4)
            a = tile(own, base, t)
            b = jnp.where(sub < 4, tile(from_e, base, t), tile(from_w, base, t))
        kept = None
        for j in range(4):
            ca = [jnp.broadcast_to(a[:, 4 * j + i : 4 * j + i + 1], (8, 128)) for i in range(4)]
            cb = [jnp.broadcast_to(b[:, 4 * j + i : 4 * j + i + 1], (8, 128)) for i in range(4)]
            if j_ref is not None and -2 <= r <= 9:
                for i in range(4):
                    j_ref[4 * j + i, r + 2, 0:8] = ca[i]
                    j_ref[4 * j + i, r + 2, 8:16] = cb[i]
            ra, rb = (roll(ca[3], 1), roll(cb[3], 1))
            row = [
                ca[0] + jnp.where(sub == 0, rb, ra),
                cb[0] + jnp.where(sub == 0, ra, rb),
                ca[1],
                cb[1],
                ca[2],
                cb[2],
            ]
            if j == 3:
                kept = row
                continue
            if j == 0 and pending is not None:
                row = [p + q for p, q in zip(row, pending)]
            y = 3 * r + j + 6
            if 0 <= y <= 36:
                for ii in range(3):
                    inv[y, ii, 0:8] = 1.0 / row[2 * ii]
                    inv[y, ii, 8:16] = 1.0 / row[2 * ii + 1]
        pending = kept


def node_values(sums, edge, from_e, from_w, inv, whole, side, first, last, sub):
    def body(y, _):
        whole[y, 0] = (sums[y, 0] + jnp.where(sub == 0, row8(from_w, y), 0.0)) * inv[y + 6, 0, 0:8]
        whole[y, 1] = sums[y, 1] * inv[y + 6, 1, 0:8]
        whole[y, 2] = sums[y, 2] * inv[y + 6, 2, 0:8]
        side[pl.ds(y, 1), :] = (edge[pl.ds(y, 1), :] + from_e[pl.ds(y, 1), :]) * inv[y + 6, 0, 8:9]
        return 0

    lax.fori_loop(first, last, body, 0, unroll=4)


def add_row(whole, side, msg, inv, y):
    for ii in range(3):
        whole[y, ii] = whole[y, ii] + msg[8 * ii : 8 * ii + 8, :] * inv[y + 6, ii, 0:8]
    side[y : y + 1, :] = side[y : y + 1, :] + msg[24:25, :] * inv[y + 6, 0, 8:9]


def element_values(whole, side, ey, sub):
    f = []
    for j in range(4):
        y = 3 * ey + j
        p0 = whole[y, 0]
        f += [p0, whole[y, 1], whole[y, 2], jnp.where(sub == 7, row8(side, y), roll(p0, 7))]
    return f


def stage_row(keep, take, whole, side, t0, u_ref, v_ref, rj_ref, j_ref, rd_ref, ey, sub):
    f = element_values(whole, side, ey, sub)
    h = tendency_step(f, lambda n: u_ref[n, ey], lambda n: v_ref[n, ey], lambda n: rj_ref[n, ey])
    g = [keep * t0[n, ey] + take * h[n] for n in range(16)]
    return limited(g, [j_ref[n, ey] for n in range(16)], rd_ref[ey])


def stage_inner_kernel(
    keep, take, sums, edge, from_e, from_w, inv, t0, u_ref, v_ref, rj_ref, j_ref, rd_ref, out, column, whole, side
):
    sub = sublane()
    node_values(sums, edge, from_e, from_w, inv, whole, side, 3, 22, sub)
    clear_first(out, column, 3)

    def rows(ey, _):
        c = stage_row(keep, take, whole, side, t0, u_ref, v_ref, rj_ref, j_ref, rd_ref, ey, sub)
        add_nodes(out, column, ey, c, sub)
        return 0

    lax.fori_loop(1, 7, rows, 0, unroll=6)


def stage_kernel(
    keep, take, wide, sums, edge, from_e, from_w, from_n, from_s, inv, t0, u_ref, v_ref, rj_ref, j_ref, rd_ref,
    inner, inner_column, out, west, east, third, fourth, whole, side,
):
    sub = sublane()
    node_values(sums, edge, from_e, from_w, inv, whole, side, 0, 4, sub)
    node_values(sums, edge, from_e, from_w, inv, whole, side, 21, 25, sub)
    add_row(whole, side, from_n, inv, 0)
    add_row(whole, side, from_s, inv, 24)
    column = fourth if wide else east

    def copy(y, _):
        for ii in range(3):
            out[y, ii] = inner[y, ii]
        column[pl.ds(y, 1), :] = inner_column[pl.ds(y, 1), :]
        return 0

    lax.fori_loop(3, 22, copy, 0, unroll=19)
    for ey, joins in ((0, (3,)), (7, (0,))):
        c = stage_row(keep, take, whole, side, t0, u_ref, v_ref, rj_ref, j_ref, rd_ref, ey, sub)
        add_nodes(out, column, ey, c, sub, joins)
    if not wide:
        thin_messages(out, column, west, third, fourth)
        return

    def pack(y, _):
        p0, p1, p2 = (out[y, 0], out[y, 1], out[y, 2])
        west[y] = jnp.where(sub < 3, p0, jnp.where(sub < 5, roll(p1, 3), roll(p2, 5)))
        east[y] = jnp.where(
            sub >= 6,
            p0,
            jnp.where(sub >= 4, roll(p1, -2), jnp.where(sub >= 2, roll(p2, -4), row8(column, y))),
        )
        return 0

    lax.fori_loop(0, 25, pack, 0, unroll=5)


def joined_row(sums, edge, from_e, from_w, y, sub):
    me, mw = (from_e[y], from_w[y])
    a0 = sums[y, 0] + jnp.where(sub == 0, mw, 0.0)
    b0 = jnp.where(sub == 0, row8(edge, y) + me, jnp.where(sub < 4, me, mw))
    b1 = jnp.where(sub < 4, roll(me, -3), roll(mw, 2))
    b2 = jnp.where(sub < 4, roll(me, -5), roll(mw, 4))
    return a0, sums[y, 1], sums[y, 2], b0, b1, b2


def rows_kernel(sums, edge, from_e, from_w, north, south):
    sub = sublane()
    for out, first in ((north, 0), (south, 18)):
        for k in range(7):
            a0, a1, a2, b0, b1, b2 = joined_row(sums, edge, from_e, from_w, first + k, sub)
            out[k, 0:8] = a0
            out[k, 8:16] = a1
            out[k, 16:24] = a2
            out[k, 24:32] = b0
            out[k, 32:40] = jnp.where((sub < 2) | (sub >= 6), b1, roll(b2, 4))


def laplace_core(f, jac):
    out = [None] * 16
    for j in range(4):
        d = line(*[f(4 * j + i) for i in range(4)])
        out[4 * j : 4 * j + 4] = line(*[jac(4 * j + i) * d[i] for i in range(4)])
    for i in range(4):
        d = line(*[f(4 * j + i) for j in range(4)])
        d = line(*[jac(4 * j + i) * d[j] for j in range(4)])
        for j in range(4):
            out[4 * j + i] = out[4 * j + i] + d[j]
    return out


FIRST, JOIN, SKIP = range(3)


def laplace_row(src, j_ref, inv, dst, r, top, bottom, sub, at=(0, 0), narrow=False, only=range(4)):
    fa, fb = ([], [])
    for j in range(4):
        y = 3 * r + j - at[0]
        pa, pb = (src[y, 0, 0:8], src[y, 0, 8:16])
        ra, rb = (roll(pa, 7), roll(pb, 7))
        fa += [pa, src[y, 1, 0:8], src[y, 2, 0:8], jnp.where(sub == 7, rb, ra)]
        fb += [pb, src[y, 1, 8:16], src[y, 2, 8:16], jnp.where(sub == 7, ra, rb)]
    ca = laplace_core(lambda n: fa[n], lambda n: j_ref[n, r, 0:8])
    cb = laplace_core(lambda n: fb[n], lambda n: j_ref[n, r, 8:16])
    for j in range(4):
        what = {0: top, 3: bottom}.get(j)
        if what == SKIP or j not in only:
            continue
        y = 3 * r + j
        ra, rb = (roll(ca[4 * j + 3], 1), roll(cb[4 * j + 3], 1))
        row = [
            (ca[4 * j] + jnp.where(sub == 0, rb, ra), cb[4 * j] + jnp.where(sub == 0, ra, rb)),
            (ca[4 * j + 1], cb[4 * j + 1]),
            (ca[4 * j + 2], cb[4 * j + 2]),
        ]
        z = y - at[1]
        for ii in range(3):
            for part, rows in zip(row[ii], (slice(0, 8), slice(8, 16))):
                if narrow and ii and rows.start:
                    continue
                if what == JOIN:
                    part = part + dst[z, ii, rows]
                if what != FIRST:
                    part = part * inv[y, ii, rows]
                dst[z, ii, rows] = part


def own_rows(sums, edge, from_e, from_w, inv, field, first, last, sub):
    def body(y, _):
        a0, a1, a2, b0, b1, b2 = joined_row(sums, edge, from_e, from_w, y, sub)
        for ii, (a, b) in enumerate(((a0, b0), (a1, b1), (a2, b2))):
            field[y, ii, 0:8] = a * inv[y + 6, ii, 0:8]
            field[y, ii, 8:16] = b * inv[y + 6, ii, 8:16]
        return 0

    lax.fori_loop(first, last, body, 0)


def inner_kernel(sums, edge, from_e, from_w, j_ref, inv, field, one, two):
    sub = sublane()
    own_rows(sums, edge, from_e, from_w, inv, field, 0, 25, sub)
    laplace_row(field, j_ref, inv, one, 3, FIRST, FIRST, sub, (6, 9))

    def rows_one(r, _):
        laplace_row(field, j_ref, inv, one, r, JOIN, FIRST, sub, (6, 9))
        return 0

    lax.fori_loop(4, 9, rows_one, 0, unroll=5)
    laplace_row(one, j_ref, inv, two, 4, FIRST, FIRST, sub, (9, 12), True)

    def rows_two(r, _):
        laplace_row(one, j_ref, inv, two, r, JOIN, FIRST, sub, (9, 12), True)
        return 0

    lax.fori_loop(5, 8, rows_two, 0, unroll=3)


def last_kernel(
    nodes, from_n, from_s, j_ref, inv, field_in, one_in, two_in, out, field, one, two, spread, spots
):
    sub = sublane()

    @pl.when(pl.program_id(0) == 0)
    def _():
        fill_places(nodes, spots)

    def copy_rows(src, dst, first, last):
        def body(y, _):
            for ii in range(3):
                dst[y, ii] = src[y - first, ii]
            return 0

        lax.fori_loop(first, last, body, 0, unroll=4)

    copy_rows(field_in, field, 6, 31)
    for msg, first, shared in ((from_n, 0, 6), (from_s, 30, 0)):
        for k in range(7):
            y = first + k
            c = msg[k, 32:40]
            parts = [msg[k, 0:8], msg[k, 24:32], msg[k, 8:16], c, msg[k, 16:24], roll(c, 4)]
            for ii in range(3):
                a, b = (parts[2 * ii] * inv[y, ii, 0:8], parts[2 * ii + 1] * inv[y, ii, 8:16])
                if k == shared:
                    a, b = (a + field[y, ii, 0:8], b + field[y, ii, 8:16])
                field[y, ii, 0:8] = a
                field[y, ii, 8:16] = b
    copy_rows(one_in, one, 9, 28)
    laplace_row(field, j_ref, inv, one, 0, SKIP, FIRST, sub, only=(3,))
    laplace_row(field, j_ref, inv, one, 1, JOIN, FIRST, sub)
    laplace_row(field, j_ref, inv, one, 2, JOIN, JOIN, sub)
    laplace_row(field, j_ref, inv, one, 9, JOIN, FIRST, sub)
    laplace_row(field, j_ref, inv, one, 10, JOIN, FIRST, sub)
    laplace_row(field, j_ref, inv, one, 11, JOIN, SKIP, sub, only=(0,))
    copy_rows(two_in, two, 12, 25)
    laplace_row(one, j_ref, inv, two, 1, SKIP, FIRST, sub, narrow=True, only=(3,))
    laplace_row(one, j_ref, inv, two, 2, JOIN, FIRST, sub, narrow=True)
    laplace_row(one, j_ref, inv, two, 3, JOIN, JOIN, sub, narrow=True)
    laplace_row(one, j_ref, inv, two, 8, JOIN, FIRST, sub, narrow=True)
    laplace_row(one, j_ref, inv, two, 9, JOIN, FIRST, sub, narrow=True)
    laplace_row(one, j_ref, inv, two, 10, JOIN, SKIP, sub, narrow=True, only=(0,))
    flat = spread.reshape(1024, 128)

    def finish(ey, _):
        for j in range(4):
            y = 3 * ey + j + 6
            p0 = field[y, 0, 0:8] - DIFFUSION * two[y, 0, 0:8]
            q0 = field[y, 0, 8:16] - DIFFUSION * two[y, 0, 8:16]
            vals = [
                p0,
                field[y, 1, 0:8] - DIFFUSION * two[y, 1, 0:8],
                field[y, 2, 0:8] - DIFFUSION * two[y, 2, 0:8],
                jnp.where(sub == 7, roll(q0, 7), roll(p0, 7)),
            ]
            for i in range(4):
                flat[pl.ds(ey * 128 + 4 * j + i, 8, stride=16), :] = vals[i]
        return 0

    lax.fori_loop(0, 8, finish, 0)

    def scatter(e, _):
        out[e] = spread[spots[e]]
        return 0

    lax.fori_loop(0, 64, scatter, 0, unroll=8)


def sds(*shape):
    return jax.ShapeDtypeStruct(shape, F32)


def tiled(*shape):
    zeros = (0,) * (len(shape) - 1)
    return pl.BlockSpec(shape, lambda t: zeros + (t,))


def fixed(*shape):
    zeros = (0,) * len(shape)
    return pl.BlockSpec(shape, lambda t: zeros)


PARAMS = pltpu.CompilerParams(vmem_limit_bytes=VMEM_LIMIT, dimension_semantics=("arbitrary",))
SMEM = pl.BlockSpec(memory_space=pltpu.SMEM)


def swapped(before, after, distance):
    size = lax.axis_size("sfc")
    even = (lax.axis_index("sfc") // distance) % 2 == 0
    up = [(i, (i + distance) % size) for i in range(size) if (i // distance) % 2 == 0]
    over = [(i, (i + distance) % size) for i in range(size) if (i // distance) % 2 == 1]
    one = lax.ppermute(jnp.where(even, after, before), "sfc", up + [(j, i) for i, j in up])
    two = lax.ppermute(jnp.where(even, before, after), "sfc", over + [(j, i) for i, j in over])
    return jnp.where(even, two, one), jnp.where(even, one, two)


def per_device(tracers, velocity, jacobian, elem_nodes):
    nodes = elem_nodes.T
    coef = [sds(16, 8, 8, 128)] * 4 + [sds(8, 8, 128)]
    coef_specs = [fixed(16, 8, 8, 128)] * 4 + [fixed(8, 8, 128)]
    sums_spec = tiled(27, 3, 8, 128)
    first = pl.pallas_call(
        first_kernel,
        grid=(4,),
        in_specs=[SMEM, fixed(16, 64), tiled(64, 16, 128), fixed(64, 16, 128), fixed(16, 64)],
        out_specs=[sums_spec, tiled(48, 128), tiled(48, 128), tiled(32, 128), tiled(32, 128), tiled(16, 8, 8, 128)]
        + coef_specs,
        out_shape=[sds(27, 3, 8, 512), sds(48, 512), sds(48, 512), sds(32, 512), sds(32, 512), sds(16, 8, 8, 512)]
        + coef,
        scratch_shapes=[
            pltpu.VMEM((64, 16, 128), F32),
            pltpu.VMEM((64, 16, 128), F32),
            pltpu.VMEM((64, 128), F32),
            pltpu.SMEM((64,), jnp.int32),
        ],
        compiler_params=pltpu.CompilerParams(vmem_limit_bytes=FIRST_LIMIT, dimension_semantics=("arbitrary",)),
        name="section_one_sums",
    )
    sums, west, east, north, south, t0, *coefs = first(nodes, nodes, tracers, velocity, jacobian.T)

    row = lax.broadcasted_iota(jnp.int32, (32, 1), 0)

    def corrected(own, from_w, from_e, y):
        return own + jnp.where(row == 0, from_w[y : y + 1], 0.0) + jnp.where(row >= 24, from_e[y : y + 1], 0.0)

    from_w, from_e = swapped(west, east, 1)
    low = lax.broadcasted_iota(jnp.int32, (8, 1), 0) < 4
    beside = [jnp.where(low, from_e[k : k + 8], from_w[k : k + 8]) for k in (32, 40)]
    msg_n = jnp.concatenate([corrected(north, from_w, from_e, 0), west[32:40], beside[0]])
    msg_s = jnp.concatenate([corrected(south, from_w, from_e, 24), west[40:48], beside[1]])
    from_n, from_s = swapped(msg_n, msg_s, PX)

    whole = pl.BlockSpec(memory_space=pltpu.VMEM)
    inv_inner = pl.pallas_call(
        own_geometry_kernel,
        in_specs=[whole] * 3,
        out_specs=whole,
        out_shape=sds(37, 3, 16, 128),
        compiler_params=pltpu.CompilerParams(vmem_limit_bytes=VMEM_LIMIT),
        name="inner_geometry",
    )(west, from_e, from_w)
    jac, inv = pl.pallas_call(
        geometry_kernel,
        in_specs=[whole] * 5,
        out_specs=[whole] * 2,
        out_shape=[sds(16, 12, 16, 128), sds(37, 3, 16, 128)],
        compiler_params=pltpu.CompilerParams(vmem_limit_bytes=VMEM_LIMIT),
        name="geometry",
    )(west, from_e, from_w, from_n, from_s)
    jac_spec, inv_spec = (fixed(16, 12, 16, 128), fixed(37, 3, 16, 128))

    def inner_stage(keep, take, sums, edge, from_e, from_w, inv, rows):
        return pl.pallas_call(
            functools.partial(stage_inner_kernel, keep, take),
            grid=(4,),
            in_specs=[sums_spec] + [tiled(rows, 128)] * 3 + [inv_spec, tiled(16, 8, 8, 128)] + coef_specs,
            out_specs=[sums_spec, tiled(32, 128)],
            out_shape=[sds(27, 3, 8, 512), sds(32, 512)],
            scratch_shapes=[pltpu.VMEM((27, 3, 8, 128), F32), pltpu.VMEM((32, 128), F32)],
            compiler_params=PARAMS,
            cost_estimate=pl.CostEstimate(
                flops=64 * 16 * 512 * 60, bytes_accessed=8 * 1024 * 1024, transcendentals=0
            ),
            name="inner_rows",
        )(sums, edge, from_e, from_w, inv, t0, *coefs)

    def stage(keep, take, wide, sums, edge, from_e, from_w, from_n, from_s, rows, inner):
        if wide:
            outs = [sds(25, 8, 512), sds(25, 8, 512), sds(8, 512), sds(32, 512)]
            specs = [tiled(25, 8, 128), tiled(25, 8, 128), tiled(8, 128), tiled(32, 128)]
        else:
            outs = [sds(32, 512)] * 4
            specs = [tiled(32, 128)] * 4
        return pl.pallas_call(
            functools.partial(stage_kernel, keep, take, wide),
            grid=(4,),
            in_specs=[sums_spec]
            + [tiled(rows, 128)] * 5
            + [inv_spec, tiled(16, 8, 8, 128)]
            + coef_specs
            + [sums_spec, tiled(32, 128)],
            out_specs=[sums_spec] + specs,
            out_shape=[sds(27, 3, 8, 512)] + outs,
            scratch_shapes=[pltpu.VMEM((27, 3, 8, 128), F32), pltpu.VMEM((32, 128), F32)],
            compiler_params=PARAMS,
            name="section_three_sums" if wide else "section_two_sums",
        )(sums, edge, from_e, from_w, from_n, from_s, inv, t0, *coefs, *inner)

    inner = inner_stage(0.75, 0.25, sums, east, from_e, from_w, inv_inner, 48)
    sums, west, east, north, south = stage(
        0.75, 0.25, False, sums, east, from_e, from_w, from_n, from_s, 48, inner
    )
    from_w, from_e = swapped(west, east, 1)
    msg_n = corrected(north, from_w, from_e, 0)
    msg_s = corrected(south, from_w, from_e, 24)
    from_n, from_s = swapped(msg_n, msg_s, PX)

    inner = inner_stage(1.0 / 3.0, 2.0 / 3.0, sums, east, from_e, from_w, inv, 32)
    sums, west, east, _, edge = stage(
        1.0 / 3.0, 2.0 / 3.0, True, sums, east, from_e, from_w, from_n, from_s, 32, inner
    )
    from_w, from_e = swapped(west, east, 1)
    message = tiled(25, 8, 128)
    band = tiled(7, 40, 128)
    msg_n, msg_s = pl.pallas_call(
        rows_kernel,
        grid=(4,),
        in_specs=[sums_spec, tiled(32, 128), message, message],
        out_specs=[band, band],
        out_shape=[sds(7, 40, 512)] * 2,
        compiler_params=PARAMS,
        name="row_bands",
    )(sums, edge, from_e, from_w)
    from_n, from_s = swapped(msg_n, msg_s, PX)
    grown = [(25, 3, 16), (19, 3, 16), (13, 3, 16)]
    flops = 64 * 16 * 512 * 60
    field, one, two = pl.pallas_call(
        inner_kernel,
        grid=(4,),
        in_specs=[sums_spec, tiled(32, 128), message, message, jac_spec, inv_spec],
        out_specs=[tiled(*g, 128) for g in grown],
        out_shape=[sds(*g, 512) for g in grown],
        compiler_params=PARAMS,
        cost_estimate=pl.CostEstimate(flops=flops, bytes_accessed=16 * 1024 * 1024, transcendentals=0),
        name="biharmonic_inner_rows",
    )(sums, edge, from_e, from_w, jac, inv)
    return pl.pallas_call(
        last_kernel,
        grid=(4,),
        in_specs=[SMEM, band, band, jac_spec, inv_spec] + [tiled(*g, 128) for g in grown],
        out_specs=tiled(64, 16, 128),
        out_shape=sds(64, 16, 512),
        scratch_shapes=[pltpu.VMEM((37, 3, 16, 128), F32)] * 3
        + [pltpu.VMEM((64, 16, 128), F32), pltpu.SMEM((64,), jnp.int32)],
        compiler_params=PARAMS,
        name="biharmonic_outer_rows",
    )(nodes, from_n, from_s, jac, inv, field, one, two)


def solution(mesh):
    in_specs = (P("sfc", None, None), P("sfc", None, None), P("sfc", None), P("sfc", None))
    out_specs = P("sfc", None, None)
    return jax.shard_map(
        per_device, mesh=mesh, in_specs=in_specs, out_specs=out_specs, check_vma=False
    )
```

```python
import functools
import jax
import jax.numpy as jnp
import numpy as np
from jax import lax
from jax.experimental import pallas as pl
from jax.experimental.pallas import tpu as pltpu
from jax.sharding import PartitionSpec as P

TT = 8
PX = 8
STEP_SIZE = 0.04
DIFFUSION = 0.0001
F32 = jnp.float32
VMEM_LIMIT = 36 * 1024 * 1024
FIRST_LIMIT = 52 * 1024 * 1024


def gll_derivative():
    points = np.array([-1.0, -np.sqrt(0.2), np.sqrt(0.2), 1.0])
    bary = np.array(
        [1.0 / np.prod([points[t] - points[p] for p in range(4) if p != t]) for t in range(4)]
    )
    deriv = np.zeros((4, 4))
    for a in range(4):
        for i in range(4):
            if a != i:
                deriv[a, i] = bary[i] / bary[a] / (points[a] - points[i])
        deriv[a, a] = -np.sum(deriv[a])
    return deriv


D = gll_derivative()
ODD_00, ODD_01 = (float(0.5 * (D[0, 0] - D[0, 3])), float(0.5 * (D[0, 1] - D[0, 2])))
ODD_10, ODD_11 = (float(0.5 * (D[1, 0] - D[1, 3])), float(0.5 * (D[1, 1] - D[1, 2])))
EVEN_0, EVEN_1 = (float(0.5 * (D[0, 0] + D[0, 3])), float(0.5 * (D[1, 0] + D[1, 3])))


def line(g0, g1, g2, g3):
    o0, o1 = (g0 - g3, g1 - g2)
    ev = (g0 + g3) - (g1 + g2)
    a = ODD_00 * o0 + ODD_01 * o1
    c = ODD_10 * o0 + ODD_11 * o1
    b = EVEN_0 * ev
    e = EVEN_1 * ev
    return a + b, c + e, c - e, a - b


def roll(x, shift):
    return pltpu.roll(x, shift % 8, 0)


def sublane():
    return lax.broadcasted_iota(jnp.int32, (8, 128), 0)


def row8(ref, y):
    return jnp.broadcast_to(ref[pl.ds(y, 1), :], (8, 128))


def tendency_step(f, u, v, rj):
    dx = [None] * 16
    for j in range(4):
        dx[4 * j : 4 * j + 4] = line(*[u(4 * j + i) * f[4 * j + i] for i in range(4)])
    out = [None] * 16
    for i in range(4):
        de = line(*[v(4 * j + i) * f[4 * j + i] for j in range(4)])
        for j in range(4):
            n = 4 * j + i
            out[n] = f[n] - rj(n) * (dx[n] + de[j])
    return out


def weighted(values):
    corner = (values[0] + values[3]) + (values[12] + values[15])
    edge = ((values[1] + values[2]) + (values[4] + values[7])) + (
        (values[8] + values[11]) + (values[13] + values[14])
    )
    inner = (values[5] + values[6]) + (values[9] + values[10])
    return corner + 5.0 * edge + 25.0 * inner


def limited(g, jac, rden):
    mean = weighted([jac[n] * g[n] for n in range(16)]) * rden
    lows = list(g)
    while len(lows) > 1:
        lows = [jnp.minimum(lows[k], lows[k + 1]) for k in range(0, len(lows), 2)]
    low = lows[0]
    positive = jnp.maximum(mean, 0.0)
    negative = low < 0.0
    denominator = jnp.where(negative, positive - low, 1.0)
    scaling = jnp.where(negative, positive / denominator, 1.0)
    return [jac[n] * (mean + scaling * (g[n] - mean)) for n in range(16)]


def add_nodes(sums, edge, ey, c, sub, joins=(0,)):
    for j in range(4):
        c0, c1, c2, c3 = c[4 * j : 4 * j + 4]
        c0 = c0 + jnp.where(sub == 0, 0.0, roll(c3, 1))
        last = c3[7:8, :]
        y = 3 * ey + j
        if j in joins:
            c0, c1, c2 = (c0 + sums[y, 0], c1 + sums[y, 1], c2 + sums[y, 2])
            last = last + edge[pl.ds(y, 1), :]
        sums[y, 0] = c0
        sums[y, 1] = c1
        sums[y, 2] = c2
        edge[pl.ds(y, 1), :] = last


def clear_first(sums, edge, y=0):
    for ii in range(3):
        sums[y, ii] = jnp.zeros((8, 128), F32)
    edge[y : y + 1, :] = jnp.zeros((1, 128), F32)


def thin_messages(sums, edge, west, north, south):
    def copy(y, _):
        west[pl.ds(y, 1), :] = sums[y, 0, 0:1, :]
        return 0

    lax.fori_loop(0, 25, copy, 0, unroll=5)
    for out, y in ((north, 0), (south, 24)):
        for ii in range(3):
            out[8 * ii : 8 * ii + 8, :] = sums[y, ii]
        out[24:32, :] = row8(edge, y)


def place(corner):
    ey = (corner * 874) >> 16
    return 8 * ey + (((corner - 75 * ey) * 21846) >> 16)


def fill_places(nodes, spots):
    def body(e, _):
        spots[e] = place(nodes[0, e])
        return 0

    lax.fori_loop(0, 64, body, 0, unroll=8)


def first_kernel(
    corners, node_rows, x, vel, j_rows, sums, west, east, north, south, t0, u_ref, v_ref, rj_ref, j_ref, rd_ref,
    gathered, winds, jc, spots,
):
    step = pl.program_id(0)
    sub = sublane()
    lane = lax.broadcasted_iota(jnp.int32, (8, 128), 1)

    @pl.when(step == 0)
    def _():
        jc[...] = jnp.zeros_like(jc)
        fill_places(corners, spots)
        to = place(node_rows[0:1, :])
        hit = (lax.broadcasted_iota(jnp.int32, (64, 64), 0) == to).astype(F32)
        jc[:, 0:16] = lax.dot_general(
            hit, j_rows[...], (((1,), (1,)), ((), ())), precision=lax.Precision.HIGHEST, preferred_element_type=F32
        )

        def order(e, _):
            winds[spots[e]] = vel[e]
            return 0

        lax.fori_loop(0, 64, order, 0, unroll=8)
        flat = winds.reshape(1024, 128)

        def coef(ey, _):
            comp = jc[pl.ds(pl.multiple_of(8 * ey, 8), 8), :]
            js = []
            for n in range(16):
                jv = jnp.broadcast_to(comp[:, n : n + 1], (8, 128))
                w = flat[pl.ds(ey * 128 + n, 8, stride=16), :]
                wr = pltpu.roll(w, 64, 1)
                dj = STEP_SIZE * jv
                u_ref[ey, n] = dj * jnp.where(lane < 64, w, wr)
                v_ref[ey, n] = dj * jnp.where(lane < 64, wr, w)
                j_ref[ey, n] = jv
                rj_ref[ey, n] = 1.0 / jv
                js.append(jv)
            rd_ref[ey] = 1.0 / weighted(js)
            return 0

        lax.fori_loop(0, 8, coef, 0)

    def gather(e, _):
        gathered[spots[e]] = x[e]
        return 0

    lax.fori_loop(0, 64, gather, 0, unroll=8)
    flat = gathered.reshape(1024, 128)
    clear_first(sums, east)

    def rows(ey, _):
        f = [flat[pl.ds(ey * 128 + n, 8, stride=16), :] for n in range(16)]
        for n in range(16):
            t0[ey, n] = f[n]
        g = tendency_step(
            f, lambda n: u_ref[ey, n], lambda n: v_ref[ey, n], lambda n: rj_ref[ey, n]
        )
        c = limited(g, [j_ref[ey, n] for n in range(16)], rd_ref[ey])
        add_nodes(sums, east, ey, c, sub)
        return 0

    lax.fori_loop(0, 8, rows, 0, unroll=8)
    thin_messages(sums, east, west, north, south)
    for out in (west, east):
        for half in range(2):
            out[32 + 8 * half : 40 + 8 * half, :] = jc[
                pl.ds(pl.multiple_of(8 * (4 * half + step), 8), 8), :
            ]


def own_geometry_kernel(own, from_e, from_w, inv):
    geometry_rows(own, from_e, from_w, None, None, None, inv, 0, 8)


def geometry_kernel(own, from_e, from_w, from_n, from_s, j_ref, inv):
    geometry_rows(own, from_e, from_w, from_n, from_s, j_ref, inv, -3, 11)


def geometry_rows(own, from_e, from_w, from_n, from_s, j_ref, inv, first, last):
    sub = sublane()

    def tile(ref, base, t):
        return ref[base : base + 8, 128 * t : 128 * t + 128]

    pending = None
    for r in range(first, last):
        if r < 0:
            t = r + 4
            a, b = (tile(from_n, 32, t), tile(from_n, 40, t))
        elif r > 7:
            t = r - 8
            a, b = (tile(from_s, 32, t), tile(from_s, 40, t))
        else:
            base, t = (32 + 8 * (r // 4), r % 4)
            a = tile(own, base, t)
            b = jnp.where(sub < 4, tile(from_e, base, t), tile(from_w, base, t))
        kept = None
        for j in range(4):
            ca = [jnp.broadcast_to(a[:, 4 * j + i : 4 * j + i + 1], (8, 128)) for i in range(4)]
            cb = [jnp.broadcast_to(b[:, 4 * j + i : 4 * j + i + 1], (8, 128)) for i in range(4)]
            if j_ref is not None and -2 <= r <= 9:
                for i in range(4):
                    j_ref[4 * j + i, r + 2, 0:8] = ca[i]
                    j_ref[4 * j + i, r + 2, 8:16] = cb[i]
            ra, rb = (roll(ca[3], 1), roll(cb[3], 1))
            row = [
                ca[0] + jnp.where(sub == 0, rb, ra),
                cb[0] + jnp.where(sub == 0, ra, rb),
                ca[1],
                cb[1],
                ca[2],
                cb[2],
            ]
            if j == 3:
                kept = row
                continue
            if j == 0 and pending is not None:
                row = [p + q for p, q in zip(row, pending)]
            y = 3 * r + j + 6
            if 0 <= y <= 36:
                for ii in range(3):
                    inv[y, ii, 0:8] = 1.0 / row[2 * ii]
                    inv[y, ii, 8:16] = 1.0 / row[2 * ii + 1]
        pending = kept


def node_values(sums, edge, from_e, from_w, inv, whole, side, first, last, sub):
    def body(y, _):
        whole[y, 0] = (sums[y, 0] + jnp.where(sub == 0, row8(from_w, y), 0.0)) * inv[y + 6, 0, 0:8]
        whole[y, 1] = sums[y, 1] * inv[y + 6, 1, 0:8]
        whole[y, 2] = sums[y, 2] * inv[y + 6, 2, 0:8]
        side[pl.ds(y, 1), :] = (edge[pl.ds(y, 1), :] + from_e[pl.ds(y, 1), :]) * inv[y + 6, 0, 8:9]
        return 0

    lax.fori_loop(first, last, body, 0, unroll=4)


def add_row(whole, side, msg, inv, y):
    for ii in range(3):
        whole[y, ii] = whole[y, ii] + msg[8 * ii : 8 * ii + 8, :] * inv[y + 6, ii, 0:8]
    side[y : y + 1, :] = side[y : y + 1, :] + msg[24:25, :] * inv[y + 6, 0, 8:9]


def element_values(whole, side, ey, sub):
    f = []
    for j in range(4):
        y = 3 * ey + j
        p0 = whole[y, 0]
        f += [p0, whole[y, 1], whole[y, 2], jnp.where(sub == 7, row8(side, y), roll(p0, 7))]
    return f


def stage_row(keep, take, whole, side, t0, u_ref, v_ref, rj_ref, j_ref, rd_ref, ey, sub, at=None):
    at = ey if at is None else at
    f = element_values(whole, side, ey, sub)
    h = tendency_step(f, lambda n: u_ref[at, n], lambda n: v_ref[at, n], lambda n: rj_ref[at, n])
    g = [keep * t0[at, n] + take * h[n] for n in range(16)]
    return limited(g, [j_ref[at, n] for n in range(16)], rd_ref[at])


def stage_inner_kernel(
    keep, take, sums, edge, from_e, from_w, inv, t0, u_ref, v_ref, rj_ref, j_ref, rd_ref, out, column, whole, side
):
    sub = sublane()
    node_values(sums, edge, from_e, from_w, inv, whole, side, 3, 22, sub)
    clear_first(out, column, 3)

    def rows(ey, _):
        c = stage_row(keep, take, whole, side, t0, u_ref, v_ref, rj_ref, j_ref, rd_ref, ey, sub)
        add_nodes(out, column, ey, c, sub)
        return 0

    lax.fori_loop(1, 7, rows, 0, unroll=6)


def stage_kernel(
    keep, take, wide, sums, edge, from_e, from_w, from_n, from_s, inv, t0, u0, v0, rj0, j0, rd0, t7, u7, v7, rj7, j7, rd7,
    inner, inner_column, out, west, east, third, fourth, whole, side,
):
    sub = sublane()
    node_values(sums, edge, from_e, from_w, inv, whole, side, 0, 4, sub)
    node_values(sums, edge, from_e, from_w, inv, whole, side, 21, 25, sub)
    add_row(whole, side, from_n, inv, 0)
    add_row(whole, side, from_s, inv, 24)
    column = fourth if wide else east

    def copy(y, _):
        for ii in range(3):
            out[y, ii] = inner[y, ii]
        column[pl.ds(y, 1), :] = inner_column[pl.ds(y, 1), :]
        return 0

    lax.fori_loop(3, 22, copy, 0, unroll=19)
    for ey, joins, coefs in ((0, (3,), (t0, u0, v0, rj0, j0, rd0)), (7, (0,), (t7, u7, v7, rj7, j7, rd7))):
        c = stage_row(keep, take, whole, side, *coefs, ey, sub, 0)
        add_nodes(out, column, ey, c, sub, joins)
    if not wide:
        thin_messages(out, column, west, third, fourth)
        return

    def pack(y, _):
        p0, p1, p2 = (out[y, 0], out[y, 1], out[y, 2])
        west[y] = jnp.where(sub < 3, p0, jnp.where(sub < 5, roll(p1, 3), roll(p2, 5)))
        east[y] = jnp.where(
            sub >= 6,
            p0,
            jnp.where(sub >= 4, roll(p1, -2), jnp.where(sub >= 2, roll(p2, -4), row8(column, y))),
        )
        return 0

    lax.fori_loop(0, 25, pack, 0, unroll=5)


def joined_row(sums, edge, from_e, from_w, y, sub):
    me, mw = (from_e[y], from_w[y])
    a0 = sums[y, 0] + jnp.where(sub == 0, mw, 0.0)
    b0 = jnp.where(sub == 0, row8(edge, y) + me, jnp.where(sub < 4, me, mw))
    b1 = jnp.where(sub < 4, roll(me, -3), roll(mw, 2))
    b2 = jnp.where(sub < 4, roll(me, -5), roll(mw, 4))
    return a0, sums[y, 1], sums[y, 2], b0, b1, b2


def rows_kernel(sums, edge, from_e, from_w, north, south):
    sub = sublane()
    for out, first in ((north, 0), (south, 18)):
        for k in range(7):
            a0, a1, a2, b0, b1, b2 = joined_row(sums, edge, from_e, from_w, first + k, sub)
            out[k, 0:8] = a0
            out[k, 8:16] = a1
            out[k, 16:24] = a2
            out[k, 24:32] = b0
            out[k, 32:40] = jnp.where((sub < 2) | (sub >= 6), b1, roll(b2, 4))


def laplace_core(f, jac):
    out = [None] * 16
    for j in range(4):
        d = line(*[f(4 * j + i) for i in range(4)])
        out[4 * j : 4 * j + 4] = line(*[jac(4 * j + i) * d[i] for i in range(4)])
    for i in range(4):
        d = line(*[f(4 * j + i) for j in range(4)])
        d = line(*[jac(4 * j + i) * d[j] for j in range(4)])
        for j in range(4):
            out[4 * j + i] = out[4 * j + i] + d[j]
    return out


FIRST, JOIN, SKIP = range(3)


def laplace_row(src, j_ref, inv, dst, r, top, bottom, sub, at=(0, 0), narrow=False, only=range(4)):
    fa, fb = ([], [])
    for j in range(4):
        y = 3 * r + j - at[0]
        pa, pb = (src[y, 0, 0:8], src[y, 0, 8:16])
        ra, rb = (roll(pa, 7), roll(pb, 7))
        fa += [pa, src[y, 1, 0:8], src[y, 2, 0:8], jnp.where(sub == 7, rb, ra)]
        fb += [pb, src[y, 1, 8:16], src[y, 2, 8:16], jnp.where(sub == 7, ra, rb)]
    ca = laplace_core(lambda n: fa[n], lambda n: j_ref[n, r, 0:8])
    cb = laplace_core(lambda n: fb[n], lambda n: j_ref[n, r, 8:16])
    for j in range(4):
        what = {0: top, 3: bottom}.get(j)
        if what == SKIP or j not in only:
            continue
        y = 3 * r + j
        ra, rb = (roll(ca[4 * j + 3], 1), roll(cb[4 * j + 3], 1))
        row = [
            (ca[4 * j] + jnp.where(sub == 0, rb, ra), cb[4 * j] + jnp.where(sub == 0, ra, rb)),
            (ca[4 * j + 1], cb[4 * j + 1]),
            (ca[4 * j + 2], cb[4 * j + 2]),
        ]
        z = y - at[1]
        for ii in range(3):
            for part, rows in zip(row[ii], (slice(0, 8), slice(8, 16))):
                if narrow and ii and rows.start:
                    continue
                if what == JOIN:
                    part = part + dst[z, ii, rows]
                if what != FIRST:
                    part = part * inv[y, ii, rows]
                dst[z, ii, rows] = part


def own_rows(sums, edge, from_e, from_w, inv, field, first, last, sub):
    def body(y, _):
        a0, a1, a2, b0, b1, b2 = joined_row(sums, edge, from_e, from_w, y, sub)
        for ii, (a, b) in enumerate(((a0, b0), (a1, b1), (a2, b2))):
            field[y, ii, 0:8] = a * inv[y + 6, ii, 0:8]
            field[y, ii, 8:16] = b * inv[y + 6, ii, 8:16]
        return 0

    lax.fori_loop(first, last, body, 0)


def inner_kernel(sums, edge, from_e, from_w, j_ref, inv, field, one, two):
    sub = sublane()
    own_rows(sums, edge, from_e, from_w, inv, field, 0, 25, sub)
    laplace_row(field, j_ref, inv, one, 3, FIRST, FIRST, sub, (6, 9))

    def rows_one(r, _):
        laplace_row(field, j_ref, inv, one, r, JOIN, FIRST, sub, (6, 9))
        return 0

    lax.fori_loop(4, 9, rows_one, 0, unroll=5)
    laplace_row(one, j_ref, inv, two, 4, FIRST, FIRST, sub, (9, 12), True)

    def rows_two(r, _):
        laplace_row(one, j_ref, inv, two, r, JOIN, FIRST, sub, (9, 12), True)
        return 0

    lax.fori_loop(5, 8, rows_two, 0, unroll=3)


def last_kernel(
    nodes, from_n, from_s, j_ref, inv, field_in, one_in, two_in, out, field, one, two, spread, spots
):
    sub = sublane()

    @pl.when(pl.program_id(0) == 0)
    def _():
        fill_places(nodes, spots)

    def copy_rows(src, dst, first, last):
        def body(y, _):
            for ii in range(3):
                dst[y, ii] = src[y - first, ii]
            return 0

        lax.fori_loop(first, last, body, 0, unroll=4)

    copy_rows(field_in, field, 6, 31)
    for msg, first, shared in ((from_n, 0, 6), (from_s, 30, 0)):
        for k in range(7):
            y = first + k
            c = msg[k, 32:40]
            parts = [msg[k, 0:8], msg[k, 24:32], msg[k, 8:16], c, msg[k, 16:24], roll(c, 4)]
            for ii in range(3):
                a, b = (parts[2 * ii] * inv[y, ii, 0:8], parts[2 * ii + 1] * inv[y, ii, 8:16])
                if k == shared:
                    a, b = (a + field[y, ii, 0:8], b + field[y, ii, 8:16])
                field[y, ii, 0:8] = a
                field[y, ii, 8:16] = b
    copy_rows(one_in, one, 9, 28)
    laplace_row(field, j_ref, inv, one, 0, SKIP, FIRST, sub, only=(3,))
    laplace_row(field, j_ref, inv, one, 1, JOIN, FIRST, sub)
    laplace_row(field, j_ref, inv, one, 2, JOIN, JOIN, sub)
    laplace_row(field, j_ref, inv, one, 9, JOIN, FIRST, sub)
    laplace_row(field, j_ref, inv, one, 10, JOIN, FIRST, sub)
    laplace_row(field, j_ref, inv, one, 11, JOIN, SKIP, sub, only=(0,))
    copy_rows(two_in, two, 12, 25)
    laplace_row(one, j_ref, inv, two, 1, SKIP, FIRST, sub, narrow=True, only=(3,))
    laplace_row(one, j_ref, inv, two, 2, JOIN, FIRST, sub, narrow=True)
    laplace_row(one, j_ref, inv, two, 3, JOIN, JOIN, sub, narrow=True)
    laplace_row(one, j_ref, inv, two, 8, JOIN, FIRST, sub, narrow=True)
    laplace_row(one, j_ref, inv, two, 9, JOIN, FIRST, sub, narrow=True)
    laplace_row(one, j_ref, inv, two, 10, JOIN, SKIP, sub, narrow=True, only=(0,))
    flat = spread.reshape(1024, 128)

    def finish(ey, _):
        for j in range(4):
            y = 3 * ey + j + 6
            p0 = field[y, 0, 0:8] - DIFFUSION * two[y, 0, 0:8]
            q0 = field[y, 0, 8:16] - DIFFUSION * two[y, 0, 8:16]
            vals = [
                p0,
                field[y, 1, 0:8] - DIFFUSION * two[y, 1, 0:8],
                field[y, 2, 0:8] - DIFFUSION * two[y, 2, 0:8],
                jnp.where(sub == 7, roll(q0, 7), roll(p0, 7)),
            ]
            for i in range(4):
                flat[pl.ds(ey * 128 + 4 * j + i, 8, stride=16), :] = vals[i]
        return 0

    lax.fori_loop(0, 8, finish, 0)

    def scatter(e, _):
        out[e] = spread[spots[e]]
        return 0

    lax.fori_loop(0, 64, scatter, 0, unroll=8)


def sds(*shape):
    return jax.ShapeDtypeStruct(shape, F32)


def tiled(*shape):
    zeros = (0,) * (len(shape) - 1)
    return pl.BlockSpec(shape, lambda t: zeros + (t,))


def fixed(*shape):
    zeros = (0,) * len(shape)
    return pl.BlockSpec(shape, lambda t: zeros)


PARAMS = pltpu.CompilerParams(vmem_limit_bytes=VMEM_LIMIT, dimension_semantics=("arbitrary",))
SMEM = pl.BlockSpec(memory_space=pltpu.SMEM)


def swapped(before, after, distance):
    size = lax.axis_size("sfc")
    even = (lax.axis_index("sfc") // distance) % 2 == 0
    up = [(i, (i + distance) % size) for i in range(size) if (i // distance) % 2 == 0]
    over = [(i, (i + distance) % size) for i in range(size) if (i // distance) % 2 == 1]
    one = lax.ppermute(jnp.where(even, after, before), "sfc", up + [(j, i) for i, j in up])
    two = lax.ppermute(jnp.where(even, before, after), "sfc", over + [(j, i) for i, j in over])
    return jnp.where(even, two, one), jnp.where(even, one, two)


def per_device(tracers, velocity, jacobian, elem_nodes):
    nodes = elem_nodes.T
    coef = [sds(8, 16, 8, 128)] * 4 + [sds(8, 8, 128)]
    coef_specs = [fixed(8, 16, 8, 128)] * 4 + [fixed(8, 8, 128)]
    sums_spec = tiled(27, 3, 8, 128)
    first = pl.pallas_call(
        first_kernel,
        grid=(4,),
        in_specs=[SMEM, fixed(16, 64), tiled(64, 16, 128), fixed(64, 16, 128), fixed(16, 64)],
        out_specs=[sums_spec, tiled(48, 128), tiled(48, 128), tiled(32, 128), tiled(32, 128), tiled(8, 16, 8, 128)]
        + coef_specs,
        out_shape=[sds(27, 3, 8, 512), sds(48, 512), sds(48, 512), sds(32, 512), sds(32, 512), sds(8, 16, 8, 512)]
        + coef,
        scratch_shapes=[
            pltpu.VMEM((64, 16, 128), F32),
            pltpu.VMEM((64, 16, 128), F32),
            pltpu.VMEM((64, 128), F32),
            pltpu.SMEM((64,), jnp.int32),
        ],
        compiler_params=pltpu.CompilerParams(vmem_limit_bytes=FIRST_LIMIT, dimension_semantics=("arbitrary",)),
        name="section_one_sums",
    )
    sums, west, east, north, south, t0, *coefs = first(nodes, nodes, tracers, velocity, jacobian.T)

    row = lax.broadcasted_iota(jnp.int32, (32, 1), 0)

    def corrected(own, from_w, from_e, y):
        return own + jnp.where(row == 0, from_w[y : y + 1], 0.0) + jnp.where(row >= 24, from_e[y : y + 1], 0.0)

    from_w, from_e = swapped(west, east, 1)
    low = lax.broadcasted_iota(jnp.int32, (8, 1), 0) < 4
    beside = [jnp.where(low, from_e[k : k + 8], from_w[k : k + 8]) for k in (32, 40)]
    msg_n = jnp.concatenate([corrected(north, from_w, from_e, 0), west[32:40], beside[0]])
    msg_s = jnp.concatenate([corrected(south, from_w, from_e, 24), west[40:48], beside[1]])
    from_n, from_s = swapped(msg_n, msg_s, PX)

    whole = pl.BlockSpec(memory_space=pltpu.VMEM)
    inv_inner = pl.pallas_call(
        own_geometry_kernel,
        in_specs=[whole] * 3,
        out_specs=whole,
        out_shape=sds(37, 3, 16, 128),
        compiler_params=pltpu.CompilerParams(vmem_limit_bytes=VMEM_LIMIT),
        name="inner_geometry",
    )(west, from_e, from_w)
    jac, inv = pl.pallas_call(
        geometry_kernel,
        in_specs=[whole] * 5,
        out_specs=[whole] * 2,
        out_shape=[sds(16, 12, 16, 128), sds(37, 3, 16, 128)],
        compiler_params=pltpu.CompilerParams(vmem_limit_bytes=VMEM_LIMIT),
        name="geometry",
    )(west, from_e, from_w, from_n, from_s)
    jac_spec, inv_spec = (fixed(16, 12, 16, 128), fixed(37, 3, 16, 128))

    def inner_stage(keep, take, sums, edge, from_e, from_w, inv, rows):
        return pl.pallas_call(
            functools.partial(stage_inner_kernel, keep, take),
            grid=(4,),
            in_specs=[sums_spec] + [tiled(rows, 128)] * 3 + [inv_spec, tiled(8, 16, 8, 128)] + coef_specs,
            out_specs=[sums_spec, tiled(32, 128)],
            out_shape=[sds(27, 3, 8, 512), sds(32, 512)],
            scratch_shapes=[pltpu.VMEM((27, 3, 8, 128), F32), pltpu.VMEM((32, 128), F32)],
            compiler_params=PARAMS,
            cost_estimate=pl.CostEstimate(
                flops=64 * 16 * 512 * 60, bytes_accessed=8 * 1024 * 1024, transcendentals=0
            ),
            name="inner_rows",
        )(sums, edge, from_e, from_w, inv, t0, *coefs)

    def one_row(ey):
        return (
            [pl.BlockSpec((1, 16, 8, 128), lambda t: (ey, 0, 0, t))]
            + [pl.BlockSpec((1, 16, 8, 128), lambda t: (ey, 0, 0, 0))] * 4
            + [pl.BlockSpec((1, 8, 128), lambda t: (ey, 0, 0))]
        )

    def stage(keep, take, wide, sums, edge, from_e, from_w, from_n, from_s, rows, inner):
        if wide:
            outs = [sds(25, 8, 512), sds(25, 8, 512), sds(8, 512), sds(32, 512)]
            specs = [tiled(25, 8, 128), tiled(25, 8, 128), tiled(8, 128), tiled(32, 128)]
        else:
            outs = [sds(32, 512)] * 4
            specs = [tiled(32, 128)] * 4
        return pl.pallas_call(
            functools.partial(stage_kernel, keep, take, wide),
            grid=(4,),
            in_specs=[sums_spec]
            + [tiled(rows, 128)] * 5
            + [inv_spec]
            + one_row(0)
            + one_row(7)
            + [sums_spec, tiled(32, 128)],
            out_specs=[sums_spec] + specs,
            out_shape=[sds(27, 3, 8, 512)] + outs,
            scratch_shapes=[pltpu.VMEM((27, 3, 8, 128), F32), pltpu.VMEM((32, 128), F32)],
            compiler_params=PARAMS,
            name="section_three_sums" if wide else "section_two_sums",
        )(sums, edge, from_e, from_w, from_n, from_s, inv, t0, *coefs, t0, *coefs, *inner)

    inner = inner_stage(0.75, 0.25, sums, east, from_e, from_w, inv_inner, 48)
    sums, west, east, north, south = stage(
        0.75, 0.25, False, sums, east, from_e, from_w, from_n, from_s, 48, inner
    )
    from_w, from_e = swapped(west, east, 1)
    msg_n = corrected(north, from_w, from_e, 0)
    msg_s = corrected(south, from_w, from_e, 24)
    from_n, from_s = swapped(msg_n, msg_s, PX)

    inner = inner_stage(1.0 / 3.0, 2.0 / 3.0, sums, east, from_e, from_w, inv, 32)
    sums, west, east, _, edge = stage(
        1.0 / 3.0, 2.0 / 3.0, True, sums, east, from_e, from_w, from_n, from_s, 32, inner
    )
    from_w, from_e = swapped(west, east, 1)
    message = tiled(25, 8, 128)
    band = tiled(7, 40, 128)
    msg_n, msg_s = pl.pallas_call(
        rows_kernel,
        grid=(4,),
        in_specs=[sums_spec, tiled(32, 128), message, message],
        out_specs=[band, band],
        out_shape=[sds(7, 40, 512)] * 2,
        compiler_params=PARAMS,
        name="row_bands",
    )(sums, edge, from_e, from_w)
    from_n, from_s = swapped(msg_n, msg_s, PX)
    grown = [(25, 3, 16), (19, 3, 16), (13, 3, 16)]
    flops = 64 * 16 * 512 * 60
    field, one, two = pl.pallas_call(
        inner_kernel,
        grid=(4,),
        in_specs=[sums_spec, tiled(32, 128), message, message, jac_spec, inv_spec],
        out_specs=[tiled(*g, 128) for g in grown],
        out_shape=[sds(*g, 512) for g in grown],
        compiler_params=PARAMS,
        cost_estimate=pl.CostEstimate(flops=flops, bytes_accessed=16 * 1024 * 1024, transcendentals=0),
        name="biharmonic_inner_rows",
    )(sums, edge, from_e, from_w, jac, inv)
    return pl.pallas_call(
        last_kernel,
        grid=(4,),
        in_specs=[SMEM, band, band, jac_spec, inv_spec] + [tiled(*g, 128) for g in grown],
        out_specs=tiled(64, 16, 128),
        out_shape=sds(64, 16, 512),
        scratch_shapes=[pltpu.VMEM((37, 3, 16, 128), F32)] * 3
        + [pltpu.VMEM((64, 16, 128), F32), pltpu.SMEM((64,), jnp.int32)],
        compiler_params=PARAMS,
        name="biharmonic_outer_rows",
    )(nodes, from_n, from_s, jac, inv, field, one, two)


def solution(mesh):
    in_specs = (P("sfc", None, None), P("sfc", None, None), P("sfc", None), P("sfc", None))
    out_specs = P("sfc", None, None)
    return jax.shard_map(
        per_device, mesh=mesh, in_specs=in_specs, out_specs=out_specs, check_vma=False
    )
```

```python
import functools
import jax
import jax.numpy as jnp
import numpy as np
from jax import lax
from jax.experimental import pallas as pl
from jax.experimental.pallas import tpu as pltpu
from jax.sharding import PartitionSpec as P

TT = 8
PX = 8
STEP_SIZE = 0.04
DIFFUSION = 0.0001
F32 = jnp.float32
VMEM_LIMIT = 36 * 1024 * 1024
FIRST_LIMIT = 52 * 1024 * 1024


def gll_derivative():
    points = np.array([-1.0, -np.sqrt(0.2), np.sqrt(0.2), 1.0])
    bary = np.array(
        [1.0 / np.prod([points[t] - points[p] for p in range(4) if p != t]) for t in range(4)]
    )
    deriv = np.zeros((4, 4))
    for a in range(4):
        for i in range(4):
            if a != i:
                deriv[a, i] = bary[i] / bary[a] / (points[a] - points[i])
        deriv[a, a] = -np.sum(deriv[a])
    return deriv


D = gll_derivative()
ODD_00, ODD_01 = (float(0.5 * (D[0, 0] - D[0, 3])), float(0.5 * (D[0, 1] - D[0, 2])))
ODD_10, ODD_11 = (float(0.5 * (D[1, 0] - D[1, 3])), float(0.5 * (D[1, 1] - D[1, 2])))
EVEN_0, EVEN_1 = (float(0.5 * (D[0, 0] + D[0, 3])), float(0.5 * (D[1, 0] + D[1, 3])))


def line(g0, g1, g2, g3):
    o0, o1 = (g0 - g3, g1 - g2)
    ev = (g0 + g3) - (g1 + g2)
    a = ODD_00 * o0 + ODD_01 * o1
    c = ODD_10 * o0 + ODD_11 * o1
    b = EVEN_0 * ev
    e = EVEN_1 * ev
    return a + b, c + e, c - e, a - b


def roll(x, shift):
    return pltpu.roll(x, shift % 8, 0)


def sublane():
    return lax.broadcasted_iota(jnp.int32, (8, 128), 0)


def row8(ref, y):
    return jnp.broadcast_to(ref[pl.ds(y, 1), :], (8, 128))


def tendency_step(f, u, v, rj):
    dx = [None] * 16
    for j in range(4):
        dx[4 * j : 4 * j + 4] = line(*[u(4 * j + i) * f[4 * j + i] for i in range(4)])
    out = [None] * 16
    for i in range(4):
        de = line(*[v(4 * j + i) * f[4 * j + i] for j in range(4)])
        for j in range(4):
            n = 4 * j + i
            out[n] = f[n] - rj(n) * (dx[n] + de[j])
    return out


def weighted(values):
    corner = (values[0] + values[3]) + (values[12] + values[15])
    edge = ((values[1] + values[2]) + (values[4] + values[7])) + (
        (values[8] + values[11]) + (values[13] + values[14])
    )
    inner = (values[5] + values[6]) + (values[9] + values[10])
    return corner + 5.0 * edge + 25.0 * inner


def limited(g, jac, rden):
    mean = weighted([jac[n] * g[n] for n in range(16)]) * rden
    lows = list(g)
    while len(lows) > 1:
        lows = [jnp.minimum(lows[k], lows[k + 1]) for k in range(0, len(lows), 2)]
    low = lows[0]
    positive = jnp.maximum(mean, 0.0)
    negative = low < 0.0
    denominator = jnp.where(negative, positive - low, 1.0)
    scaling = jnp.where(negative, positive / denominator, 1.0)
    return [jac[n] * (mean + scaling * (g[n] - mean)) for n in range(16)]


def add_nodes(sums, edge, ey, c, sub, joins=(0,)):
    for j in range(4):
        c0, c1, c2, c3 = c[4 * j : 4 * j + 4]
        c0 = c0 + jnp.where(sub == 0, 0.0, roll(c3, 1))
        last = c3[7:8, :]
        y = 3 * ey + j
        if j in joins:
            c0, c1, c2 = (c0 + sums[y, 0], c1 + sums[y, 1], c2 + sums[y, 2])
            last = last + edge[pl.ds(y, 1), :]
        sums[y, 0] = c0
        sums[y, 1] = c1
        sums[y, 2] = c2
        edge[pl.ds(y, 1), :] = last


def clear_first(sums, edge, y=0):
    for ii in range(3):
        sums[y, ii] = jnp.zeros((8, 128), F32)
    edge[y : y + 1, :] = jnp.zeros((1, 128), F32)


def thin_messages(sums, edge, west, north, south):
    def copy(y, _):
        west[pl.ds(y, 1), :] = sums[y, 0, 0:1, :]
        return 0

    lax.fori_loop(0, 25, copy, 0, unroll=5)
    for out, y in ((north, 0), (south, 24)):
        for ii in range(3):
            out[8 * ii : 8 * ii + 8, :] = sums[y, ii]
        out[24:32, :] = row8(edge, y)


def place(corner):
    ey = (corner * 874) >> 16
    return 8 * ey + (((corner - 75 * ey) * 21846) >> 16)


def fill_places(nodes, spots):
    def body(e, _):
        spots[e] = place(nodes[0, e])
        return 0

    lax.fori_loop(0, 64, body, 0, unroll=8)


def first_kernel(
    corners, node_rows, x, vel, j_rows, sums, west, east, north, south, t0, u_ref, v_ref, rj_ref, j_ref, rd_ref,
    gathered, winds, jc, spots,
):
    step = pl.program_id(0)
    sub = sublane()
    lane = lax.broadcasted_iota(jnp.int32, (8, 128), 1)

    @pl.when(step == 0)
    def _():
        jc[...] = jnp.zeros_like(jc)
        fill_places(corners, spots)
        to = place(node_rows[0:1, :])
        hit = (lax.broadcasted_iota(jnp.int32, (64, 64), 0) == to).astype(F32)
        jc[:, 0:16] = lax.dot_general(
            hit, j_rows[...], (((1,), (1,)), ((), ())), precision=lax.Precision.HIGHEST, preferred_element_type=F32
        )

        def order(e, _):
            winds[spots[e]] = vel[e]
            return 0

        lax.fori_loop(0, 64, order, 0, unroll=8)
        flat = winds.reshape(1024, 128)

        def coef(ey, _):
            comp = jc[pl.ds(pl.multiple_of(8 * ey, 8), 8), :]
            js = []
            for n in range(16):
                jv = jnp.broadcast_to(comp[:, n : n + 1], (8, 128))
                w = flat[pl.ds(ey * 128 + n, 8, stride=16), :]
                wr = pltpu.roll(w, 64, 1)
                dj = STEP_SIZE * jv
                u_ref[n, ey] = dj * jnp.where(lane < 64, w, wr)
                v_ref[n, ey] = dj * jnp.where(lane < 64, wr, w)
                j_ref[n, ey] = jv
                rj_ref[n, ey] = 1.0 / jv
                js.append(jv)
            rd_ref[ey] = 1.0 / weighted(js)
            return 0

        lax.fori_loop(0, 8, coef, 0)

    def gather(e, _):
        gathered[spots[e]] = x[e]
        return 0

    lax.fori_loop(0, 64, gather, 0, unroll=8)
    flat = gathered.reshape(1024, 128)
    clear_first(sums, east)

    def rows(ey, _):
        f = [flat[pl.ds(ey * 128 + n, 8, stride=16), :] for n in range(16)]
        for n in range(16):
            t0[n, ey] = f[n]
        g = tendency_step(
            f, lambda n: u_ref[n, ey], lambda n: v_ref[n, ey], lambda n: rj_ref[n, ey]
        )
        c = limited(g, [j_ref[n, ey] for n in range(16)], rd_ref[ey])
        add_nodes(sums, east, ey, c, sub)
        return 0

    lax.fori_loop(0, 8, rows, 0, unroll=8)
    thin_messages(sums, east, west, north, south)
    for out in (west, east):
        for half in range(2):
            out[32 + 8 * half : 40 + 8 * half, :] = jc[
                pl.ds(pl.multiple_of(8 * (4 * half + step), 8), 8), :
            ]


def own_geometry_kernel(own, from_e, from_w, inv):
    geometry_rows(own, from_e, from_w, None, None, None, inv, 0, 8)


def geometry_kernel(own, from_e, from_w, from_n, from_s, j_ref, inv):
    geometry_rows(own, from_e, from_w, from_n, from_s, j_ref, inv, -3, 11)


def geometry_rows(own, from_e, from_w, from_n, from_s, j_ref, inv, first, last):
    sub = sublane()

    def tile(ref, base, t):
        return ref[base : base + 8, 128 * t : 128 * t + 128]

    pending = None
    for r in range(first, last):
        if r < 0:
            t = r + 4
            a, b = (tile(from_n, 32, t), tile(from_n, 40, t))
        elif r > 7:
            t = r - 8
            a, b = (tile(from_s, 32, t), tile(from_s, 40, t))
        else:
            base, t = (32 + 8 * (r // 4), r % 4)
            a = tile(own, base, t)
            b = jnp.where(sub < 4, tile(from_e, base, t), tile(from_w, base, t))
        kept = None
        for j in range(4):
            ca = [jnp.broadcast_to(a[:, 4 * j + i : 4 * j + i + 1], (8, 128)) for i in range(4)]
            cb = [jnp.broadcast_to(b[:, 4 * j + i : 4 * j + i + 1], (8, 128)) for i in range(4)]
            if j_ref is not None and -2 <= r <= 9:
                for i in range(4):
                    j_ref[4 * j + i, r + 2, 0:8] = ca[i]
                    j_ref[4 * j + i, r + 2, 8:16] = cb[i]
            ra, rb = (roll(ca[3], 1), roll(cb[3], 1))
            row = [
                ca[0] + jnp.where(sub == 0, rb, ra),
                cb[0] + jnp.where(sub == 0, ra, rb),
                ca[1],
                cb[1],
                ca[2],
                cb[2],
            ]
            if j == 3:
                kept = row
                continue
            if j == 0 and pending is not None:
                row = [p + q for p, q in zip(row, pending)]
            y = 3 * r + j + 6
            if 0 <= y <= 36:
                for ii in range(3):
                    inv[y, ii, 0:8] = 1.0 / row[2 * ii]
                    inv[y, ii, 8:16] = 1.0 / row[2 * ii + 1]
        pending = kept


def node_values(sums, edge, from_e, from_w, inv, whole, side, first, last, sub):
    def body(y, _):
        whole[y, 0] = (sums[y, 0] + jnp.where(sub == 0, row8(from_w, y), 0.0)) * inv[y + 6, 0, 0:8]
        whole[y, 1] = sums[y, 1] * inv[y + 6, 1, 0:8]
        whole[y, 2] = sums[y, 2] * inv[y + 6, 2, 0:8]
        side[pl.ds(y, 1), :] = (edge[pl.ds(y, 1), :] + from_e[pl.ds(y, 1), :]) * inv[y + 6, 0, 8:9]
        return 0

    lax.fori_loop(first, last, body, 0, unroll=4)


def add_row(whole, side, msg, inv, y):
    for ii in range(3):
        whole[y, ii] = whole[y, ii] + msg[8 * ii : 8 * ii + 8, :] * inv[y + 6, ii, 0:8]
    side[y : y + 1, :] = side[y : y + 1, :] + msg[24:25, :] * inv[y + 6, 0, 8:9]


def element_values(whole, side, ey, sub):
    f = []
    for j in range(4):
        y = 3 * ey + j
        p0 = whole[y, 0]
        f += [p0, whole[y, 1], whole[y, 2], jnp.where(sub == 7, row8(side, y), roll(p0, 7))]
    return f


def stage_row(keep, take, whole, side, t0, u_ref, v_ref, rj_ref, j_ref, rd_ref, ey, sub):
    f = element_values(whole, side, ey, sub)
    h = tendency_step(f, lambda n: u_ref[n, ey], lambda n: v_ref[n, ey], lambda n: rj_ref[n, ey])
    g = [keep * t0[n, ey] + take * h[n] for n in range(16)]
    return limited(g, [j_ref[n, ey] for n in range(16)], rd_ref[ey])


def stage_inner_kernel(
    keep, take, sums, edge, from_e, from_w, inv, t0, u_ref, v_ref, rj_ref, j_ref, rd_ref, out, column, whole, side
):
    sub = sublane()
    node_values(sums, edge, from_e, from_w, inv, whole, side, 3, 22, sub)
    clear_first(out, column, 3)

    def rows(ey, _):
        c = stage_row(keep, take, whole, side, t0, u_ref, v_ref, rj_ref, j_ref, rd_ref, ey, sub)
        add_nodes(out, column, ey, c, sub)
        return 0

    lax.fori_loop(1, 7, rows, 0, unroll=6)


def stage_kernel(
    keep, take, wide, sums, edge, from_e, from_w, from_n, from_s, inv, t0, u_ref, v_ref, rj_ref, j_ref, rd_ref,
    inner, inner_column, out, west, east, third, fourth, whole, side,
):
    sub = sublane()
    node_values(sums, edge, from_e, from_w, inv, whole, side, 0, 4, sub)
    node_values(sums, edge, from_e, from_w, inv, whole, side, 21, 25, sub)
    add_row(whole, side, from_n, inv, 0)
    add_row(whole, side, from_s, inv, 24)
    column = fourth if wide else east

    def copy(y, _):
        for ii in range(3):
            out[y, ii] = inner[y, ii]
        column[pl.ds(y, 1), :] = inner_column[pl.ds(y, 1), :]
        return 0

    lax.fori_loop(3, 22, copy, 0, unroll=19)
    for ey, joins in ((0, (3,)), (7, (0,))):
        c = stage_row(keep, take, whole, side, t0, u_ref, v_ref, rj_ref, j_ref, rd_ref, ey, sub)
        add_nodes(out, column, ey, c, sub, joins)
    if not wide:
        thin_messages(out, column, west, third, fourth)
        return

    def pack(y, _):
        p0, p1, p2 = (out[y, 0], out[y, 1], out[y, 2])
        west[y] = jnp.where(sub < 3, p0, jnp.where(sub < 5, roll(p1, 3), roll(p2, 5)))
        east[y] = jnp.where(
            sub >= 6,
            p0,
            jnp.where(sub >= 4, roll(p1, -2), jnp.where(sub >= 2, roll(p2, -4), row8(column, y))),
        )
        return 0

    lax.fori_loop(0, 25, pack, 0, unroll=5)


def joined_row(sums, edge, from_e, from_w, y, sub):
    me, mw = (from_e[y], from_w[y])
    a0 = sums[y, 0] + jnp.where(sub == 0, mw, 0.0)
    b0 = jnp.where(sub == 0, row8(edge, y) + me, jnp.where(sub < 4, me, mw))
    b1 = jnp.where(sub < 4, roll(me, -3), roll(mw, 2))
    b2 = jnp.where(sub < 4, roll(me, -5), roll(mw, 4))
    return a0, sums[y, 1], sums[y, 2], b0, b1, b2


def rows_kernel(sums, edge, from_e, from_w, north, south):
    sub = sublane()
    for out, first in ((north, 0), (south, 18)):
        for k in range(7):
            a0, a1, a2, b0, b1, b2 = joined_row(sums, edge, from_e, from_w, first + k, sub)
            out[k, 0:8] = a0
            out[k, 8:16] = a1
            out[k, 16:24] = a2
            out[k, 24:32] = b0
            out[k, 32:40] = jnp.where((sub < 2) | (sub >= 6), b1, roll(b2, 4))


def laplace_core(f, jac, nonzero=range(4)):
    out = [None] * 16
    for j in nonzero:
        d = line(*[f(4 * j + i) for i in range(4)])
        out[4 * j : 4 * j + 4] = line(*[jac(4 * j + i) * d[i] for i in range(4)])
    for i in range(4):
        if len(nonzero) == 4:
            d = line(*[f(4 * j + i) for j in range(4)])
        else:
            (k,) = nonzero
            d = [float(D[j, k]) * f(4 * k + i) for j in range(4)]
        d = line(*[jac(4 * j + i) * d[j] for j in range(4)])
        for j in range(4):
            n = 4 * j + i
            out[n] = d[j] if out[n] is None else out[n] + d[j]
    return out


FIRST, JOIN, SKIP = range(3)


def laplace_row(src, j_ref, inv, dst, r, top, bottom, sub, at=(0, 0), narrow=False, only=range(4), nonzero=range(4)):
    fa, fb = ([None] * 16, [None] * 16)
    for j in nonzero:
        y = 3 * r + j - at[0]
        pa, pb = (src[y, 0, 0:8], src[y, 0, 8:16])
        ra, rb = (roll(pa, 7), roll(pb, 7))
        fa[4 * j : 4 * j + 4] = [pa, src[y, 1, 0:8], src[y, 2, 0:8], jnp.where(sub == 7, rb, ra)]
        fb[4 * j : 4 * j + 4] = [pb, src[y, 1, 8:16], src[y, 2, 8:16], jnp.where(sub == 7, ra, rb)]
    ca = laplace_core(lambda n: fa[n], lambda n: j_ref[n, r, 0:8], nonzero)
    cb = laplace_core(lambda n: fb[n], lambda n: j_ref[n, r, 8:16], nonzero)
    for j in range(4):
        what = {0: top, 3: bottom}.get(j)
        if what == SKIP or j not in only:
            continue
        y = 3 * r + j
        ra, rb = (roll(ca[4 * j + 3], 1), roll(cb[4 * j + 3], 1))
        row = [
            (ca[4 * j] + jnp.where(sub == 0, rb, ra), cb[4 * j] + jnp.where(sub == 0, ra, rb)),
            (ca[4 * j + 1], cb[4 * j + 1]),
            (ca[4 * j + 2], cb[4 * j + 2]),
        ]
        z = y - at[1]
        for ii in range(3):
            for part, rows in zip(row[ii], (slice(0, 8), slice(8, 16))):
                if narrow and ii and rows.start:
                    continue
                if what == JOIN:
                    part = part + dst[z, ii, rows]
                if what != FIRST:
                    part = part * inv[y, ii, rows]
                dst[z, ii, rows] = part


def own_rows(sums, edge, from_e, from_w, inv, field, first, last, sub):
    def body(y, _):
        a0, a1, a2, b0, b1, b2 = joined_row(sums, edge, from_e, from_w, y, sub)
        for ii, (a, b) in enumerate(((a0, b0), (a1, b1), (a2, b2))):
            field[y, ii, 0:8] = a * inv[y + 6, ii, 0:8]
            field[y, ii, 8:16] = b * inv[y + 6, ii, 8:16]
        return 0

    lax.fori_loop(first, last, body, 0)


def inner_kernel(sums, edge, from_e, from_w, j_ref, inv, field, ends, two, one):
    sub = sublane()
    own_rows(sums, edge, from_e, from_w, inv, field, 0, 25, sub)
    for src, dst, narrow in ((field, one, False), (one, two, True)):

        def rows(r, _, src=src, dst=dst, narrow=narrow):
            laplace_row(src, j_ref, inv, dst, r, JOIN, FIRST, sub, (6, 6), narrow)
            return 0

        laplace_row(src, j_ref, inv, dst, 2, None, FIRST, sub, (6, 6), narrow)
        lax.fori_loop(3, 9, rows, 0, unroll=3)
        laplace_row(src, j_ref, inv, dst, 9, JOIN, None, sub, (6, 6), narrow)
    for ii in range(3):
        ends[0, ii] = one[0, ii]
        ends[1, ii] = one[24, ii]


def last_kernel(
    nodes, from_n, from_s, j_ref, inv, field_in, ends, two_in, out, field, one, two, beyond, spread, spots
):
    sub = sublane()

    @pl.when(pl.program_id(0) == 0)
    def _():
        fill_places(nodes, spots)

    def copy_rows(src, dst, first, last):
        def body(y, _):
            for ii in range(3):
                dst[y, ii] = src[y - first, ii]
            return 0

        lax.fori_loop(first, last, body, 0, unroll=4)

    copy_rows(field_in, field, 6, 31)
    for msg, first, shared in ((from_n, 0, 6), (from_s, 30, 0)):
        for k in range(7):
            y = first + k
            c = msg[k, 32:40]
            parts = [msg[k, 0:8], msg[k, 24:32], msg[k, 8:16], c, msg[k, 16:24], roll(c, 4)]
            for ii in range(3):
                a, b = (parts[2 * ii] * inv[y, ii, 0:8], parts[2 * ii + 1] * inv[y, ii, 8:16])
                if k == shared:
                    beyond[y // 30, ii, 0:8] = a
                    beyond[y // 30, ii, 8:16] = b
                    a, b = (a + field[y, ii, 0:8], b + field[y, ii, 8:16])
                field[y, ii, 0:8] = a
                field[y, ii, 8:16] = b
    def row(src, dst, r, top, bottom, **more):
        laplace_row(src, j_ref, inv, dst, r, top, bottom, sub, **more)

    row(field, one, 0, SKIP, FIRST, only=(3,))
    row(field, one, 1, JOIN, FIRST)
    row(beyond, one, 2, JOIN, None, at=(6, 0), nonzero=(0,))
    row(beyond, one, 9, None, FIRST, at=(29, 0), nonzero=(3,))
    row(field, one, 10, JOIN, FIRST)
    row(field, one, 11, JOIN, SKIP, only=(0,))
    row(one, two, 2, FIRST, FIRST, narrow=True)
    row(one, two, 3, JOIN, None, narrow=True, nonzero=(0,))
    row(one, two, 8, None, FIRST, narrow=True, nonzero=(3,))
    row(one, two, 9, JOIN, FIRST, narrow=True)
    for ii in range(3):
        one[6, ii] = one[6, ii] + ends[0, ii]
        one[30, ii] = one[30, ii] + ends[1, ii]
    row(one, two, 1, SKIP, JOIN, narrow=True, only=(3,))
    row(one, two, 10, JOIN, SKIP, narrow=True, only=(0,))
    for y in (*range(6, 13), *range(24, 31)):
        two[y, 0] = two[y, 0] + two_in[y - 6, 0]
        for ii in (1, 2):
            two[y, ii, 0:8] = two[y, ii, 0:8] + two_in[y - 6, ii, 0:8]
    for y in range(13, 24):
        two[y, 0] = two_in[y - 6, 0]
        for ii in (1, 2):
            two[y, ii, 0:8] = two_in[y - 6, ii, 0:8]
    flat = spread.reshape(1024, 128)

    def finish(ey, _):
        for j in range(4):
            y = 3 * ey + j + 6
            p0 = field[y, 0, 0:8] - DIFFUSION * two[y, 0, 0:8]
            q0 = field[y, 0, 8:16] - DIFFUSION * two[y, 0, 8:16]
            vals = [
                p0,
                field[y, 1, 0:8] - DIFFUSION * two[y, 1, 0:8],
                field[y, 2, 0:8] - DIFFUSION * two[y, 2, 0:8],
                jnp.where(sub == 7, roll(q0, 7), roll(p0, 7)),
            ]
            for i in range(4):
                flat[pl.ds(ey * 128 + 4 * j + i, 8, stride=16), :] = vals[i]
        return 0

    lax.fori_loop(0, 8, finish, 0)

    def scatter(e, _):
        out[e] = spread[spots[e]]
        return 0

    lax.fori_loop(0, 64, scatter, 0, unroll=8)


def sds(*shape):
    return jax.ShapeDtypeStruct(shape, F32)


def tiled(*shape):
    zeros = (0,) * (len(shape) - 1)
    return pl.BlockSpec(shape, lambda t: zeros + (t,))


def fixed(*shape):
    zeros = (0,) * len(shape)
    return pl.BlockSpec(shape, lambda t: zeros)


PARAMS = pltpu.CompilerParams(vmem_limit_bytes=VMEM_LIMIT, dimension_semantics=("arbitrary",))
SMEM = pl.BlockSpec(memory_space=pltpu.SMEM)


def swapped(before, after, distance):
    size = lax.axis_size("sfc")
    even = (lax.axis_index("sfc") // distance) % 2 == 0
    up = [(i, (i + distance) % size) for i in range(size) if (i // distance) % 2 == 0]
    over = [(i, (i + distance) % size) for i in range(size) if (i // distance) % 2 == 1]
    one = lax.ppermute(jnp.where(even, after, before), "sfc", up + [(j, i) for i, j in up])
    two = lax.ppermute(jnp.where(even, before, after), "sfc", over + [(j, i) for i, j in over])
    return jnp.where(even, two, one), jnp.where(even, one, two)


def per_device(tracers, velocity, jacobian, elem_nodes):
    nodes = elem_nodes.T
    coef = [sds(16, 8, 8, 128)] * 4 + [sds(8, 8, 128)]
    coef_specs = [fixed(16, 8, 8, 128)] * 4 + [fixed(8, 8, 128)]
    sums_spec = tiled(27, 3, 8, 128)
    first = pl.pallas_call(
        first_kernel,
        grid=(4,),
        in_specs=[SMEM, fixed(16, 64), tiled(64, 16, 128), fixed(64, 16, 128), fixed(16, 64)],
        out_specs=[sums_spec, tiled(48, 128), tiled(48, 128), tiled(32, 128), tiled(32, 128), tiled(16, 8, 8, 128)]
        + coef_specs,
        out_shape=[sds(27, 3, 8, 512), sds(48, 512), sds(48, 512), sds(32, 512), sds(32, 512), sds(16, 8, 8, 512)]
        + coef,
        scratch_shapes=[
            pltpu.VMEM((64, 16, 128), F32),
            pltpu.VMEM((64, 16, 128), F32),
            pltpu.VMEM((64, 128), F32),
            pltpu.SMEM((64,), jnp.int32),
        ],
        compiler_params=pltpu.CompilerParams(vmem_limit_bytes=FIRST_LIMIT, dimension_semantics=("arbitrary",)),
        name="section_one_sums",
    )
    sums, west, east, north, south, t0, *coefs = first(nodes, nodes, tracers, velocity, jacobian.T)

    row = lax.broadcasted_iota(jnp.int32, (32, 1), 0)

    def corrected(own, from_w, from_e, y):
        return own + jnp.where(row == 0, from_w[y : y + 1], 0.0) + jnp.where(row >= 24, from_e[y : y + 1], 0.0)

    from_w, from_e = swapped(west, east, 1)
    low = lax.broadcasted_iota(jnp.int32, (8, 1), 0) < 4
    beside = [jnp.where(low, from_e[k : k + 8], from_w[k : k + 8]) for k in (32, 40)]
    msg_n = jnp.concatenate([corrected(north, from_w, from_e, 0), west[32:40], beside[0]])
    msg_s = jnp.concatenate([corrected(south, from_w, from_e, 24), west[40:48], beside[1]])
    from_n, from_s = swapped(msg_n, msg_s, PX)

    whole = pl.BlockSpec(memory_space=pltpu.VMEM)
    inv_inner = pl.pallas_call(
        own_geometry_kernel,
        in_specs=[whole] * 3,
        out_specs=whole,
        out_shape=sds(37, 3, 16, 128),
        compiler_params=pltpu.CompilerParams(vmem_limit_bytes=VMEM_LIMIT),
        name="inner_geometry",
    )(west, from_e, from_w)
    jac, inv = pl.pallas_call(
        geometry_kernel,
        in_specs=[whole] * 5,
        out_specs=[whole] * 2,
        out_shape=[sds(16, 12, 16, 128), sds(37, 3, 16, 128)],
        compiler_params=pltpu.CompilerParams(vmem_limit_bytes=VMEM_LIMIT),
        name="geometry",
    )(west, from_e, from_w, from_n, from_s)
    jac_spec, inv_spec = (fixed(16, 12, 16, 128), fixed(37, 3, 16, 128))

    def inner_stage(keep, take, sums, edge, from_e, from_w, inv, rows):
        return pl.pallas_call(
            functools.partial(stage_inner_kernel, keep, take),
            grid=(4,),
            in_specs=[sums_spec] + [tiled(rows, 128)] * 3 + [inv_spec, tiled(16, 8, 8, 128)] + coef_specs,
            out_specs=[sums_spec, tiled(32, 128)],
            out_shape=[sds(27, 3, 8, 512), sds(32, 512)],
            scratch_shapes=[pltpu.VMEM((27, 3, 8, 128), F32), pltpu.VMEM((32, 128), F32)],
            compiler_params=PARAMS,
            cost_estimate=pl.CostEstimate(
                flops=64 * 16 * 512 * 60, bytes_accessed=8 * 1024 * 1024, transcendentals=0
            ),
            name="inner_rows",
        )(sums, edge, from_e, from_w, inv, t0, *coefs)

    def stage(keep, take, wide, sums, edge, from_e, from_w, from_n, from_s, rows, inner):
        if wide:
            outs = [sds(25, 8, 512), sds(25, 8, 512), sds(8, 512), sds(32, 512)]
            specs = [tiled(25, 8, 128), tiled(25, 8, 128), tiled(8, 128), tiled(32, 128)]
        else:
            outs = [sds(32, 512)] * 4
            specs = [tiled(32, 128)] * 4
        return pl.pallas_call(
            functools.partial(stage_kernel, keep, take, wide),
            grid=(4,),
            in_specs=[sums_spec]
            + [tiled(rows, 128)] * 5
            + [inv_spec, tiled(16, 8, 8, 128)]
            + coef_specs
            + [sums_spec, tiled(32, 128)],
            out_specs=[sums_spec] + specs,
            out_shape=[sds(27, 3, 8, 512)] + outs,
            scratch_shapes=[pltpu.VMEM((27, 3, 8, 128), F32), pltpu.VMEM((32, 128), F32)],
            compiler_params=PARAMS,
            name="section_three_sums" if wide else "section_two_sums",
        )(sums, edge, from_e, from_w, from_n, from_s, inv, t0, *coefs, *inner)

    inner = inner_stage(0.75, 0.25, sums, east, from_e, from_w, inv_inner, 48)
    sums, west, east, north, south = stage(
        0.75, 0.25, False, sums, east, from_e, from_w, from_n, from_s, 48, inner
    )
    from_w, from_e = swapped(west, east, 1)
    msg_n = corrected(north, from_w, from_e, 0)
    msg_s = corrected(south, from_w, from_e, 24)
    from_n, from_s = swapped(msg_n, msg_s, PX)

    inner = inner_stage(1.0 / 3.0, 2.0 / 3.0, sums, east, from_e, from_w, inv, 32)
    sums, west, east, _, edge = stage(
        1.0 / 3.0, 2.0 / 3.0, True, sums, east, from_e, from_w, from_n, from_s, 32, inner
    )
    from_w, from_e = swapped(west, east, 1)
    message = tiled(25, 8, 128)
    band = tiled(7, 40, 128)
    msg_n, msg_s = pl.pallas_call(
        rows_kernel,
        grid=(4,),
        in_specs=[sums_spec, tiled(32, 128), message, message],
        out_specs=[band, band],
        out_shape=[sds(7, 40, 512)] * 2,
        compiler_params=PARAMS,
        name="row_bands",
    )(sums, edge, from_e, from_w)
    from_n, from_s = swapped(msg_n, msg_s, PX)
    grown = [(25, 3, 16), (2, 3, 16), (25, 3, 16)]
    flops = 64 * 16 * 512 * 60
    field, ends, two = pl.pallas_call(
        inner_kernel,
        grid=(4,),
        in_specs=[sums_spec, tiled(32, 128), message, message, jac_spec, inv_spec],
        out_specs=[tiled(*g, 128) for g in grown],
        out_shape=[sds(*g, 512) for g in grown],
        scratch_shapes=[pltpu.VMEM((25, 3, 16, 128), F32)],
        compiler_params=PARAMS,
        cost_estimate=pl.CostEstimate(flops=flops, bytes_accessed=16 * 1024 * 1024, transcendentals=0),
        name="biharmonic_inner_rows",
    )(sums, edge, from_e, from_w, jac, inv)
    return pl.pallas_call(
        last_kernel,
        grid=(4,),
        in_specs=[SMEM, band, band, jac_spec, inv_spec] + [tiled(*g, 128) for g in grown],
        out_specs=tiled(64, 16, 128),
        out_shape=sds(64, 16, 512),
        scratch_shapes=[pltpu.VMEM((37, 3, 16, 128), F32)] * 3
        + [pltpu.VMEM((2, 3, 16, 128), F32), pltpu.VMEM((64, 16, 128), F32), pltpu.SMEM((64,), jnp.int32)],
        compiler_params=PARAMS,
        name="biharmonic_outer_rows",
    )(nodes, from_n, from_s, jac, inv, field, ends, two)


def solution(mesh):
    in_specs = (P("sfc", None, None), P("sfc", None, None), P("sfc", None), P("sfc", None))
    out_specs = P("sfc", None, None)
    return jax.shard_map(
        per_device, mesh=mesh, in_specs=in_specs, out_specs=out_specs, check_vma=False
    )
```

```python
import functools
import jax
import jax.numpy as jnp
import numpy as np
from jax import lax
from jax.experimental import pallas as pl
from jax.experimental.pallas import tpu as pltpu
from jax.sharding import PartitionSpec as P

TT = 8
PX = 8
STEP_SIZE = 0.04
DIFFUSION = 0.0001
F32 = jnp.float32
VMEM_LIMIT = 36 * 1024 * 1024
FIRST_LIMIT = 52 * 1024 * 1024


def gll_derivative():
    points = np.array([-1.0, -np.sqrt(0.2), np.sqrt(0.2), 1.0])
    bary = np.array(
        [1.0 / np.prod([points[t] - points[p] for p in range(4) if p != t]) for t in range(4)]
    )
    deriv = np.zeros((4, 4))
    for a in range(4):
        for i in range(4):
            if a != i:
                deriv[a, i] = bary[i] / bary[a] / (points[a] - points[i])
        deriv[a, a] = -np.sum(deriv[a])
    return deriv


D = gll_derivative()
ODD_00, ODD_01 = (float(0.5 * (D[0, 0] - D[0, 3])), float(0.5 * (D[0, 1] - D[0, 2])))
ODD_10, ODD_11 = (float(0.5 * (D[1, 0] - D[1, 3])), float(0.5 * (D[1, 1] - D[1, 2])))
EVEN_0, EVEN_1 = (float(0.5 * (D[0, 0] + D[0, 3])), float(0.5 * (D[1, 0] + D[1, 3])))


def line(g0, g1, g2, g3):
    o0, o1 = (g0 - g3, g1 - g2)
    ev = (g0 + g3) - (g1 + g2)
    a = ODD_00 * o0 + ODD_01 * o1
    c = ODD_10 * o0 + ODD_11 * o1
    b = EVEN_0 * ev
    e = EVEN_1 * ev
    return a + b, c + e, c - e, a - b


def roll(x, shift):
    return pltpu.roll(x, shift % 8, 0)


def sublane():
    return lax.broadcasted_iota(jnp.int32, (8, 128), 0)


def row8(ref, y):
    return jnp.broadcast_to(ref[pl.ds(y, 1), :], (8, 128))


def tendency_step(f, u, v, rj):
    dx = [None] * 16
    for j in range(4):
        dx[4 * j : 4 * j + 4] = line(*[u(4 * j + i) * f[4 * j + i] for i in range(4)])
    out = [None] * 16
    for i in range(4):
        de = line(*[v(4 * j + i) * f[4 * j + i] for j in range(4)])
        for j in range(4):
            n = 4 * j + i
            out[n] = f[n] - rj(n) * (dx[n] + de[j])
    return out


def weighted(values):
    corner = (values[0] + values[3]) + (values[12] + values[15])
    edge = ((values[1] + values[2]) + (values[4] + values[7])) + (
        (values[8] + values[11]) + (values[13] + values[14])
    )
    inner = (values[5] + values[6]) + (values[9] + values[10])
    return corner + 5.0 * edge + 25.0 * inner


def limited(g, jac, rden):
    mean = weighted([jac[n] * g[n] for n in range(16)]) * rden
    lows = list(g)
    while len(lows) > 1:
        lows = [jnp.minimum(lows[k], lows[k + 1]) for k in range(0, len(lows), 2)]
    low = lows[0]
    positive = jnp.maximum(mean, 0.0)
    negative = low < 0.0
    denominator = jnp.where(negative, positive - low, 1.0)
    scaling = jnp.where(negative, positive / denominator, 1.0)
    return [jac[n] * (mean + scaling * (g[n] - mean)) for n in range(16)]


def add_nodes(sums, edge, ey, c, sub, joins=(0,)):
    for j in range(4):
        c0, c1, c2, c3 = c[4 * j : 4 * j + 4]
        c0 = c0 + jnp.where(sub == 0, 0.0, roll(c3, 1))
        last = c3[7:8, :]
        y = 3 * ey + j
        if j in joins:
            c0, c1, c2 = (c0 + sums[y, 0], c1 + sums[y, 1], c2 + sums[y, 2])
            last = last + edge[pl.ds(y, 1), :]
        sums[y, 0] = c0
        sums[y, 1] = c1
        sums[y, 2] = c2
        edge[pl.ds(y, 1), :] = last


def clear_first(sums, edge, y=0):
    for ii in range(3):
        sums[y, ii] = jnp.zeros((8, 128), F32)
    edge[y : y + 1, :] = jnp.zeros((1, 128), F32)


def thin_messages(sums, edge, west, north, south):
    def copy(y, _):
        west[pl.ds(y, 1), :] = sums[y, 0, 0:1, :]
        return 0

    lax.fori_loop(0, 25, copy, 0, unroll=5)
    for out, y in ((north, 0), (south, 24)):
        for ii in range(3):
            out[8 * ii : 8 * ii + 8, :] = sums[y, ii]
        out[24:32, :] = row8(edge, y)


def place(corner):
    ey = (corner * 874) >> 16
    return 8 * ey + (((corner - 75 * ey) * 21846) >> 16)


def fill_places(nodes, spots):
    def body(e, _):
        spots[e] = place(nodes[0, e])
        return 0

    lax.fori_loop(0, 64, body, 0, unroll=8)


def first_kernel(
    corners, node_rows, x, vel, j_rows, sums, west, east, north, south, t0, send_one, send_two, u_ref, v_ref, rj_ref, j_ref, rd_ref,
    gathered, winds, jc, spots,
):
    step = pl.program_id(0)
    sub = sublane()
    lane = lax.broadcasted_iota(jnp.int32, (8, 128), 1)

    @pl.when(step == 0)
    def _():
        jc[...] = jnp.zeros_like(jc)
        fill_places(corners, spots)
        to = place(node_rows[0:1, :])
        hit = (lax.broadcasted_iota(jnp.int32, (64, 64), 0) == to).astype(F32)
        jc[:, 0:16] = lax.dot_general(
            hit, j_rows[...], (((1,), (1,)), ((), ())), precision=lax.Precision.HIGHEST, preferred_element_type=F32
        )

        def order(e, _):
            winds[spots[e]] = vel[e]
            return 0

        lax.fori_loop(0, 64, order, 0, unroll=8)
        flat = winds.reshape(1024, 128)

        def coef(ey, _):
            comp = jc[pl.ds(pl.multiple_of(8 * ey, 8), 8), :]
            js = []
            for n in range(16):
                jv = jnp.broadcast_to(comp[:, n : n + 1], (8, 128))
                w = flat[pl.ds(ey * 128 + n, 8, stride=16), :]
                wr = pltpu.roll(w, 64, 1)
                dj = STEP_SIZE * jv
                u_ref[n, ey] = dj * jnp.where(lane < 64, w, wr)
                v_ref[n, ey] = dj * jnp.where(lane < 64, wr, w)
                j_ref[n, ey] = jv
                rj_ref[n, ey] = 1.0 / jv
                js.append(jv)
            rd_ref[ey] = 1.0 / weighted(js)
            return 0

        lax.fori_loop(0, 8, coef, 0)

    def gather(e, _):
        gathered[spots[e]] = x[e]
        return 0

    lax.fori_loop(0, 64, gather, 0, unroll=8)
    flat = gathered.reshape(1024, 128)
    clear_first(sums, east)

    def rows(ey, _):
        f = [flat[pl.ds(ey * 128 + n, 8, stride=16), :] for n in range(16)]
        for n in range(16):
            t0[n, ey] = f[n]
        g = tendency_step(
            f, lambda n: u_ref[n, ey], lambda n: v_ref[n, ey], lambda n: rj_ref[n, ey]
        )
        c = limited(g, [j_ref[n, ey] for n in range(16)], rd_ref[ey])
        add_nodes(sums, east, ey, c, sub)
        return 0

    lax.fori_loop(0, 8, rows, 0, unroll=8)
    thin_messages(sums, east, west, north, south)
    for out in (west, east):
        for half in range(2):
            out[32 + 8 * half : 40 + 8 * half, :] = jc[
                pl.ds(pl.multiple_of(8 * (4 * half + step), 8), 8), :
            ]
    even = lax.axis_index("sfc") % 2 == 0
    send_one[...] = jnp.where(even, east[...], west[...])
    send_two[...] = jnp.where(even, west[...], east[...])


def own_geometry_kernel(own, from_e, from_w, inv):
    geometry_rows(own, from_e, from_w, None, None, None, inv, 0, 8)


def geometry_kernel(own, from_e, from_w, from_n, from_s, j_ref, inv):
    geometry_rows(own, from_e, from_w, from_n, from_s, j_ref, inv, -3, 11)


def geometry_rows(own, from_e, from_w, from_n, from_s, j_ref, inv, first, last):
    sub = sublane()

    def tile(ref, base, t):
        return ref[base : base + 8, 128 * t : 128 * t + 128]

    pending = None
    for r in range(first, last):
        if r < 0:
            t = r + 4
            a, b = (tile(from_n, 32, t), tile(from_n, 40, t))
        elif r > 7:
            t = r - 8
            a, b = (tile(from_s, 32, t), tile(from_s, 40, t))
        else:
            base, t = (32 + 8 * (r // 4), r % 4)
            a = tile(own, base, t)
            b = jnp.where(sub < 4, tile(from_e, base, t), tile(from_w, base, t))
        kept = None
        for j in range(4):
            ca = [jnp.broadcast_to(a[:, 4 * j + i : 4 * j + i + 1], (8, 128)) for i in range(4)]
            cb = [jnp.broadcast_to(b[:, 4 * j + i : 4 * j + i + 1], (8, 128)) for i in range(4)]
            if j_ref is not None and -2 <= r <= 9:
                for i in range(4):
                    j_ref[4 * j + i, r + 2, 0:8] = ca[i]
                    j_ref[4 * j + i, r + 2, 8:16] = cb[i]
            ra, rb = (roll(ca[3], 1), roll(cb[3], 1))
            row = [
                ca[0] + jnp.where(sub == 0, rb, ra),
                cb[0] + jnp.where(sub == 0, ra, rb),
                ca[1],
                cb[1],
                ca[2],
                cb[2],
            ]
            if j == 3:
                kept = row
                continue
            if j == 0 and pending is not None:
                row = [p + q for p, q in zip(row, pending)]
            y = 3 * r + j + 6
            if 0 <= y <= 36:
                for ii in range(3):
                    inv[y, ii, 0:8] = 1.0 / row[2 * ii]
                    inv[y, ii, 8:16] = 1.0 / row[2 * ii + 1]
        pending = kept


def node_values(sums, edge, from_e, from_w, inv, whole, side, first, last, sub):
    def body(y, _):
        whole[y, 0] = (sums[y, 0] + jnp.where(sub == 0, row8(from_w, y), 0.0)) * inv[y + 6, 0, 0:8]
        whole[y, 1] = sums[y, 1] * inv[y + 6, 1, 0:8]
        whole[y, 2] = sums[y, 2] * inv[y + 6, 2, 0:8]
        side[pl.ds(y, 1), :] = (edge[pl.ds(y, 1), :] + from_e[pl.ds(y, 1), :]) * inv[y + 6, 0, 8:9]
        return 0

    lax.fori_loop(first, last, body, 0, unroll=4)


def add_row(whole, side, msg, inv, y):
    for ii in range(3):
        whole[y, ii] = whole[y, ii] + msg[8 * ii : 8 * ii + 8, :] * inv[y + 6, ii, 0:8]
    side[y : y + 1, :] = side[y : y + 1, :] + msg[24:25, :] * inv[y + 6, 0, 8:9]


def element_values(whole, side, ey, sub):
    f = []
    for j in range(4):
        y = 3 * ey + j
        p0 = whole[y, 0]
        f += [p0, whole[y, 1], whole[y, 2], jnp.where(sub == 7, row8(side, y), roll(p0, 7))]
    return f


def stage_row(keep, take, whole, side, t0, u_ref, v_ref, rj_ref, j_ref, rd_ref, ey, sub):
    f = element_values(whole, side, ey, sub)
    h = tendency_step(f, lambda n: u_ref[n, ey], lambda n: v_ref[n, ey], lambda n: rj_ref[n, ey])
    g = [keep * t0[n, ey] + take * h[n] for n in range(16)]
    return limited(g, [j_ref[n, ey] for n in range(16)], rd_ref[ey])


def stage_inner_kernel(
    keep, take, sums, edge, from_e, from_w, inv, t0, u_ref, v_ref, rj_ref, j_ref, rd_ref, out, column, whole, side
):
    sub = sublane()
    node_values(sums, edge, from_e, from_w, inv, whole, side, 3, 22, sub)
    clear_first(out, column, 3)

    def rows(ey, _):
        c = stage_row(keep, take, whole, side, t0, u_ref, v_ref, rj_ref, j_ref, rd_ref, ey, sub)
        add_nodes(out, column, ey, c, sub)
        return 0

    lax.fori_loop(1, 7, rows, 0, unroll=6)


def stage_kernel(
    keep, take, wide, sums, edge, from_e, from_w, from_n, from_s, inv, t0, u_ref, v_ref, rj_ref, j_ref, rd_ref,
    inner, inner_column, out, west, east, third, fourth, whole, side,
):
    sub = sublane()
    node_values(sums, edge, from_e, from_w, inv, whole, side, 0, 4, sub)
    node_values(sums, edge, from_e, from_w, inv, whole, side, 21, 25, sub)
    add_row(whole, side, from_n, inv, 0)
    add_row(whole, side, from_s, inv, 24)
    column = fourth if wide else east

    def copy(y, _):
        for ii in range(3):
            out[y, ii] = inner[y, ii]
        column[pl.ds(y, 1), :] = inner_column[pl.ds(y, 1), :]
        return 0

    lax.fori_loop(3, 22, copy, 0, unroll=19)
    for ey, joins in ((0, (3,)), (7, (0,))):
        c = stage_row(keep, take, whole, side, t0, u_ref, v_ref, rj_ref, j_ref, rd_ref, ey, sub)
        add_nodes(out, column, ey, c, sub, joins)
    if not wide:
        thin_messages(out, column, west, third, fourth)
        return

    def pack(y, _):
        p0, p1, p2 = (out[y, 0], out[y, 1], out[y, 2])
        west[y] = jnp.where(sub < 3, p0, jnp.where(sub < 5, roll(p1, 3), roll(p2, 5)))
        east[y] = jnp.where(
            sub >= 6,
            p0,
            jnp.where(sub >= 4, roll(p1, -2), jnp.where(sub >= 2, roll(p2, -4), row8(column, y))),
        )
        return 0

    lax.fori_loop(0, 25, pack, 0, unroll=5)


def joined_row(sums, edge, from_e, from_w, y, sub):
    me, mw = (from_e[y], from_w[y])
    a0 = sums[y, 0] + jnp.where(sub == 0, mw, 0.0)
    b0 = jnp.where(sub == 0, row8(edge, y) + me, jnp.where(sub < 4, me, mw))
    b1 = jnp.where(sub < 4, roll(me, -3), roll(mw, 2))
    b2 = jnp.where(sub < 4, roll(me, -5), roll(mw, 4))
    return a0, sums[y, 1], sums[y, 2], b0, b1, b2


def rows_kernel(sums, edge, from_e, from_w, north, south):
    sub = sublane()
    for out, first in ((north, 0), (south, 18)):
        for k in range(7):
            a0, a1, a2, b0, b1, b2 = joined_row(sums, edge, from_e, from_w, first + k, sub)
            out[k, 0:8] = a0
            out[k, 8:16] = a1
            out[k, 16:24] = a2
            out[k, 24:32] = b0
            out[k, 32:40] = jnp.where((sub < 2) | (sub >= 6), b1, roll(b2, 4))


def laplace_core(f, jac, nonzero=range(4)):
    out = [None] * 16
    for j in nonzero:
        d = line(*[f(4 * j + i) for i in range(4)])
        out[4 * j : 4 * j + 4] = line(*[jac(4 * j + i) * d[i] for i in range(4)])
    for i in range(4):
        if len(nonzero) == 4:
            d = line(*[f(4 * j + i) for j in range(4)])
        else:
            (k,) = nonzero
            d = [float(D[j, k]) * f(4 * k + i) for j in range(4)]
        d = line(*[jac(4 * j + i) * d[j] for j in range(4)])
        for j in range(4):
            n = 4 * j + i
            out[n] = d[j] if out[n] is None else out[n] + d[j]
    return out


FIRST, JOIN, SKIP = range(3)


def laplace_row(src, j_ref, inv, dst, r, top, bottom, sub, at=(0, 0), narrow=False, only=range(4), nonzero=range(4)):
    fa, fb = ([None] * 16, [None] * 16)
    for j in nonzero:
        y = 3 * r + j - at[0]
        pa, pb = (src[y, 0, 0:8], src[y, 0, 8:16])
        ra, rb = (roll(pa, 7), roll(pb, 7))
        fa[4 * j : 4 * j + 4] = [pa, src[y, 1, 0:8], src[y, 2, 0:8], jnp.where(sub == 7, rb, ra)]
        fb[4 * j : 4 * j + 4] = [pb, src[y, 1, 8:16], src[y, 2, 8:16], jnp.where(sub == 7, ra, rb)]
    ca = laplace_core(lambda n: fa[n], lambda n: j_ref[n, r, 0:8], nonzero)
    cb = laplace_core(lambda n: fb[n], lambda n: j_ref[n, r, 8:16], nonzero)
    for j in range(4):
        what = {0: top, 3: bottom}.get(j)
        if what == SKIP or j not in only:
            continue
        y = 3 * r + j
        ra, rb = (roll(ca[4 * j + 3], 1), roll(cb[4 * j + 3], 1))
        row = [
            (ca[4 * j] + jnp.where(sub == 0, rb, ra), cb[4 * j] + jnp.where(sub == 0, ra, rb)),
            (ca[4 * j + 1], cb[4 * j + 1]),
            (ca[4 * j + 2], cb[4 * j + 2]),
        ]
        z = y - at[1]
        for ii in range(3):
            for part, rows in zip(row[ii], (slice(0, 8), slice(8, 16))):
                if narrow and ii and rows.start:
                    continue
                if what == JOIN:
                    part = part + dst[z, ii, rows]
                if what != FIRST:
                    part = part * inv[y, ii, rows]
                dst[z, ii, rows] = part


def own_rows(sums, edge, from_e, from_w, inv, field, first, last, sub):
    def body(y, _):
        a0, a1, a2, b0, b1, b2 = joined_row(sums, edge, from_e, from_w, y, sub)
        for ii, (a, b) in enumerate(((a0, b0), (a1, b1), (a2, b2))):
            field[y, ii, 0:8] = a * inv[y + 6, ii, 0:8]
            field[y, ii, 8:16] = b * inv[y + 6, ii, 8:16]
        return 0

    lax.fori_loop(first, last, body, 0)


def inner_kernel(sums, edge, from_e, from_w, j_ref, inv, field, ends, two, one):
    sub = sublane()
    own_rows(sums, edge, from_e, from_w, inv, field, 0, 25, sub)
    for src, dst, narrow in ((field, one, False), (one, two, True)):

        def rows(r, _, src=src, dst=dst, narrow=narrow):
            laplace_row(src, j_ref, inv, dst, r, JOIN, FIRST, sub, (6, 6), narrow)
            return 0

        laplace_row(src, j_ref, inv, dst, 2, None, FIRST, sub, (6, 6), narrow)
        lax.fori_loop(3, 9, rows, 0, unroll=3)
        laplace_row(src, j_ref, inv, dst, 9, JOIN, None, sub, (6, 6), narrow)
    for ii in range(3):
        ends[0, ii] = one[0, ii]
        ends[1, ii] = one[24, ii]


def last_kernel(
    nodes, from_n, from_s, j_ref, inv, field_in, ends, two_in, out, field, one, two, beyond, spread, spots
):
    sub = sublane()

    @pl.when(pl.program_id(0) == 0)
    def _():
        fill_places(nodes, spots)

    def copy_rows(src, dst, first, last):
        def body(y, _):
            for ii in range(3):
                dst[y, ii] = src[y - first, ii]
            return 0

        lax.fori_loop(first, last, body, 0, unroll=4)

    copy_rows(field_in, field, 6, 31)
    for msg, first, shared in ((from_n, 0, 6), (from_s, 30, 0)):
        for k in range(7):
            y = first + k
            c = msg[k, 32:40]
            parts = [msg[k, 0:8], msg[k, 24:32], msg[k, 8:16], c, msg[k, 16:24], roll(c, 4)]
            for ii in range(3):
                a, b = (parts[2 * ii] * inv[y, ii, 0:8], parts[2 * ii + 1] * inv[y, ii, 8:16])
                if k == shared:
                    beyond[y // 30, ii, 0:8] = a
                    beyond[y // 30, ii, 8:16] = b
                    a, b = (a + field[y, ii, 0:8], b + field[y, ii, 8:16])
                field[y, ii, 0:8] = a
                field[y, ii, 8:16] = b
    def row(src, dst, r, top, bottom, **more):
        laplace_row(src, j_ref, inv, dst, r, top, bottom, sub, **more)

    row(field, one, 0, SKIP, FIRST, only=(3,))
    row(field, one, 1, JOIN, FIRST)
    row(beyond, one, 2, JOIN, None, at=(6, 0), nonzero=(0,))
    row(beyond, one, 9, None, FIRST, at=(29, 0), nonzero=(3,))
    row(field, one, 10, JOIN, FIRST)
    row(field, one, 11, JOIN, SKIP, only=(0,))
    row(one, two, 2, FIRST, FIRST, narrow=True)
    row(one, two, 3, JOIN, None, narrow=True, nonzero=(0,))
    row(one, two, 8, None, FIRST, narrow=True, nonzero=(3,))
    row(one, two, 9, JOIN, FIRST, narrow=True)
    for ii in range(3):
        one[6, ii] = one[6, ii] + ends[0, ii]
        one[30, ii] = one[30, ii] + ends[1, ii]
    row(one, two, 1, SKIP, JOIN, narrow=True, only=(3,))
    row(one, two, 10, JOIN, SKIP, narrow=True, only=(0,))
    for y in (*range(6, 13), *range(24, 31)):
        two[y, 0] = two[y, 0] + two_in[y - 6, 0]
        for ii in (1, 2):
            two[y, ii, 0:8] = two[y, ii, 0:8] + two_in[y - 6, ii, 0:8]
    for y in range(13, 24):
        two[y, 0] = two_in[y - 6, 0]
        for ii in (1, 2):
            two[y, ii, 0:8] = two_in[y - 6, ii, 0:8]
    flat = spread.reshape(1024, 128)

    def finish(ey, _):
        for j in range(4):
            y = 3 * ey + j + 6
            p0 = field[y, 0, 0:8] - DIFFUSION * two[y, 0, 0:8]
            q0 = field[y, 0, 8:16] - DIFFUSION * two[y, 0, 8:16]
            vals = [
                p0,
                field[y, 1, 0:8] - DIFFUSION * two[y, 1, 0:8],
                field[y, 2, 0:8] - DIFFUSION * two[y, 2, 0:8],
                jnp.where(sub == 7, roll(q0, 7), roll(p0, 7)),
            ]
            for i in range(4):
                flat[pl.ds(ey * 128 + 4 * j + i, 8, stride=16), :] = vals[i]
        return 0

    lax.fori_loop(0, 8, finish, 0)

    def scatter(e, _):
        out[e] = spread[spots[e]]
        return 0

    lax.fori_loop(0, 64, scatter, 0, unroll=8)


def sds(*shape):
    return jax.ShapeDtypeStruct(shape, F32)


def tiled(*shape):
    zeros = (0,) * (len(shape) - 1)
    return pl.BlockSpec(shape, lambda t: zeros + (t,))


def fixed(*shape):
    zeros = (0,) * len(shape)
    return pl.BlockSpec(shape, lambda t: zeros)


PARAMS = pltpu.CompilerParams(vmem_limit_bytes=VMEM_LIMIT, dimension_semantics=("arbitrary",))
SMEM = pl.BlockSpec(memory_space=pltpu.SMEM)


def swapped(before, after, distance, sends=None):
    size = lax.axis_size("sfc")
    even = (lax.axis_index("sfc") // distance) % 2 == 0
    up = [(i, (i + distance) % size) for i in range(size) if (i // distance) % 2 == 0]
    over = [(i, (i + distance) % size) for i in range(size) if (i // distance) % 2 == 1]
    if sends is None:
        sends = (jnp.where(even, after, before), jnp.where(even, before, after))
    one = lax.ppermute(sends[0], "sfc", up + [(j, i) for i, j in up])
    two = lax.ppermute(sends[1], "sfc", over + [(j, i) for i, j in over])
    return jnp.where(even, two, one), jnp.where(even, one, two)


def per_device(tracers, velocity, jacobian, elem_nodes):
    nodes = elem_nodes.T
    coef = [sds(16, 8, 8, 128)] * 4 + [sds(8, 8, 128)]
    coef_specs = [fixed(16, 8, 8, 128)] * 4 + [fixed(8, 8, 128)]
    sums_spec = tiled(27, 3, 8, 128)
    first = pl.pallas_call(
        first_kernel,
        grid=(4,),
        in_specs=[SMEM, fixed(16, 64), tiled(64, 16, 128), fixed(64, 16, 128), fixed(16, 64)],
        out_specs=[sums_spec, tiled(48, 128), tiled(48, 128), tiled(32, 128), tiled(32, 128), tiled(16, 8, 8, 128), tiled(48, 128), tiled(48, 128)]
        + coef_specs,
        out_shape=[sds(27, 3, 8, 512), sds(48, 512), sds(48, 512), sds(32, 512), sds(32, 512), sds(16, 8, 8, 512), sds(48, 512), sds(48, 512)]
        + coef,
        scratch_shapes=[
            pltpu.VMEM((64, 16, 128), F32),
            pltpu.VMEM((64, 16, 128), F32),
            pltpu.VMEM((64, 128), F32),
            pltpu.SMEM((64,), jnp.int32),
        ],
        compiler_params=pltpu.CompilerParams(vmem_limit_bytes=FIRST_LIMIT, dimension_semantics=("arbitrary",)),
        name="section_one_sums",
    )
    sums, west, east, north, south, t0, send_one, send_two, *coefs = first(nodes, nodes, tracers, velocity, jacobian.T)

    row = lax.broadcasted_iota(jnp.int32, (32, 1), 0)

    def corrected(own, from_w, from_e, y):
        return own + jnp.where(row == 0, from_w[y : y + 1], 0.0) + jnp.where(row >= 24, from_e[y : y + 1], 0.0)

    from_w, from_e = swapped(west, east, 1, (send_one, send_two))
    low = lax.broadcasted_iota(jnp.int32, (8, 1), 0) < 4
    beside = [jnp.where(low, from_e[k : k + 8], from_w[k : k + 8]) for k in (32, 40)]
    msg_n = jnp.concatenate([corrected(north, from_w, from_e, 0), west[32:40], beside[0]])
    msg_s = jnp.concatenate([corrected(south, from_w, from_e, 24), west[40:48], beside[1]])
    from_n, from_s = swapped(msg_n, msg_s, PX)

    whole = pl.BlockSpec(memory_space=pltpu.VMEM)
    inv_inner = pl.pallas_call(
        own_geometry_kernel,
        in_specs=[whole] * 3,
        out_specs=whole,
        out_shape=sds(37, 3, 16, 128),
        compiler_params=pltpu.CompilerParams(vmem_limit_bytes=VMEM_LIMIT),
        name="inner_geometry",
    )(west, from_e, from_w)
    jac, inv = pl.pallas_call(
        geometry_kernel,
        in_specs=[whole] * 5,
        out_specs=[whole] * 2,
        out_shape=[sds(16, 12, 16, 128), sds(37, 3, 16, 128)],
        compiler_params=pltpu.CompilerParams(vmem_limit_bytes=VMEM_LIMIT),
        name="geometry",
    )(west, from_e, from_w, from_n, from_s)
    jac_spec, inv_spec = (fixed(16, 12, 16, 128), fixed(37, 3, 16, 128))

    def inner_stage(keep, take, sums, edge, from_e, from_w, inv, rows):
        return pl.pallas_call(
            functools.partial(stage_inner_kernel, keep, take),
            grid=(4,),
            in_specs=[sums_spec] + [tiled(rows, 128)] * 3 + [inv_spec, tiled(16, 8, 8, 128)] + coef_specs,
            out_specs=[sums_spec, tiled(32, 128)],
            out_shape=[sds(27, 3, 8, 512), sds(32, 512)],
            scratch_shapes=[pltpu.VMEM((27, 3, 8, 128), F32), pltpu.VMEM((32, 128), F32)],
            compiler_params=PARAMS,
            cost_estimate=pl.CostEstimate(
                flops=64 * 16 * 512 * 60, bytes_accessed=8 * 1024 * 1024, transcendentals=0
            ),
            name="inner_rows",
        )(sums, edge, from_e, from_w, inv, t0, *coefs)

    def stage(keep, take, wide, sums, edge, from_e, from_w, from_n, from_s, rows, inner):
        if wide:
            outs = [sds(25, 8, 512), sds(25, 8, 512), sds(8, 512), sds(32, 512)]
            specs = [tiled(25, 8, 128), tiled(25, 8, 128), tiled(8, 128), tiled(32, 128)]
        else:
            outs = [sds(32, 512)] * 4
            specs = [tiled(32, 128)] * 4
        return pl.pallas_call(
            functools.partial(stage_kernel, keep, take, wide),
            grid=(4,),
            in_specs=[sums_spec]
            + [tiled(rows, 128)] * 5
            + [inv_spec, tiled(16, 8, 8, 128)]
            + coef_specs
            + [sums_spec, tiled(32, 128)],
            out_specs=[sums_spec] + specs,
            out_shape=[sds(27, 3, 8, 512)] + outs,
            scratch_shapes=[pltpu.VMEM((27, 3, 8, 128), F32), pltpu.VMEM((32, 128), F32)],
            compiler_params=PARAMS,
            name="section_three_sums" if wide else "section_two_sums",
        )(sums, edge, from_e, from_w, from_n, from_s, inv, t0, *coefs, *inner)

    inner = inner_stage(0.75, 0.25, sums, east, from_e, from_w, inv_inner, 48)
    sums, west, east, north, south = stage(
        0.75, 0.25, False, sums, east, from_e, from_w, from_n, from_s, 48, inner
    )
    from_w, from_e = swapped(west, east, 1)
    msg_n = corrected(north, from_w, from_e, 0)
    msg_s = corrected(south, from_w, from_e, 24)
    from_n, from_s = swapped(msg_n, msg_s, PX)

    inner = inner_stage(1.0 / 3.0, 2.0 / 3.0, sums, east, from_e, from_w, inv, 32)
    sums, west, east, _, edge = stage(
        1.0 / 3.0, 2.0 / 3.0, True, sums, east, from_e, from_w, from_n, from_s, 32, inner
    )
    from_w, from_e = swapped(west, east, 1)
    message = tiled(25, 8, 128)
    band = tiled(7, 40, 128)
    msg_n, msg_s = pl.pallas_call(
        rows_kernel,
        grid=(4,),
        in_specs=[sums_spec, tiled(32, 128), message, message],
        out_specs=[band, band],
        out_shape=[sds(7, 40, 512)] * 2,
        compiler_params=PARAMS,
        name="row_bands",
    )(sums, edge, from_e, from_w)
    from_n, from_s = swapped(msg_n, msg_s, PX)
    grown = [(25, 3, 16), (2, 3, 16), (25, 3, 16)]
    flops = 64 * 16 * 512 * 60
    field, ends, two = pl.pallas_call(
        inner_kernel,
        grid=(4,),
        in_specs=[sums_spec, tiled(32, 128), message, message, jac_spec, inv_spec],
        out_specs=[tiled(*g, 128) for g in grown],
        out_shape=[sds(*g, 512) for g in grown],
        scratch_shapes=[pltpu.VMEM((25, 3, 16, 128), F32)],
        compiler_params=PARAMS,
        cost_estimate=pl.CostEstimate(flops=flops, bytes_accessed=16 * 1024 * 1024, transcendentals=0),
        name="biharmonic_inner_rows",
    )(sums, edge, from_e, from_w, jac, inv)
    return pl.pallas_call(
        last_kernel,
        grid=(4,),
        in_specs=[SMEM, band, band, jac_spec, inv_spec] + [tiled(*g, 128) for g in grown],
        out_specs=tiled(64, 16, 128),
        out_shape=sds(64, 16, 512),
        scratch_shapes=[pltpu.VMEM((37, 3, 16, 128), F32)] * 3
        + [pltpu.VMEM((2, 3, 16, 128), F32), pltpu.VMEM((64, 16, 128), F32), pltpu.SMEM((64,), jnp.int32)],
        compiler_params=PARAMS,
        name="biharmonic_outer_rows",
    )(nodes, from_n, from_s, jac, inv, field, ends, two)


def solution(mesh):
    in_specs = (P("sfc", None, None), P("sfc", None, None), P("sfc", None), P("sfc", None))
    out_specs = P("sfc", None, None)
    return jax.shard_map(
        per_device, mesh=mesh, in_specs=in_specs, out_specs=out_specs, check_vma=False
    )
```

```python
import functools
import jax
import jax.numpy as jnp
import numpy as np
from jax import lax
from jax.experimental import pallas as pl
from jax.experimental.pallas import tpu as pltpu
from jax.sharding import PartitionSpec as P

TT = 8
PX = 8
STEP_SIZE = 0.04
DIFFUSION = 0.0001
F32 = jnp.float32
VMEM_LIMIT = 36 * 1024 * 1024
FIRST_LIMIT = 52 * 1024 * 1024


def gll_derivative():
    points = np.array([-1.0, -np.sqrt(0.2), np.sqrt(0.2), 1.0])
    bary = np.array(
        [1.0 / np.prod([points[t] - points[p] for p in range(4) if p != t]) for t in range(4)]
    )
    deriv = np.zeros((4, 4))
    for a in range(4):
        for i in range(4):
            if a != i:
                deriv[a, i] = bary[i] / bary[a] / (points[a] - points[i])
        deriv[a, a] = -np.sum(deriv[a])
    return deriv


D = gll_derivative()
ODD_00, ODD_01 = (float(0.5 * (D[0, 0] - D[0, 3])), float(0.5 * (D[0, 1] - D[0, 2])))
ODD_10, ODD_11 = (float(0.5 * (D[1, 0] - D[1, 3])), float(0.5 * (D[1, 1] - D[1, 2])))
EVEN_0, EVEN_1 = (float(0.5 * (D[0, 0] + D[0, 3])), float(0.5 * (D[1, 0] + D[1, 3])))


def line(g0, g1, g2, g3):
    o0, o1 = (g0 - g3, g1 - g2)
    ev = (g0 + g3) - (g1 + g2)
    a = ODD_00 * o0 + ODD_01 * o1
    c = ODD_10 * o0 + ODD_11 * o1
    b = EVEN_0 * ev
    e = EVEN_1 * ev
    return a + b, c + e, c - e, a - b


def roll(x, shift):
    return pltpu.roll(x, shift % 8, 0)


def sublane():
    return lax.broadcasted_iota(jnp.int32, (8, 128), 0)


def row8(ref, y):
    return jnp.broadcast_to(ref[pl.ds(y, 1), :], (8, 128))


def tendency_step(f, u, v, rj):
    dx = [None] * 16
    for j in range(4):
        dx[4 * j : 4 * j + 4] = line(*[u(4 * j + i) * f[4 * j + i] for i in range(4)])
    out = [None] * 16
    for i in range(4):
        de = line(*[v(4 * j + i) * f[4 * j + i] for j in range(4)])
        for j in range(4):
            n = 4 * j + i
            out[n] = f[n] - rj(n) * (dx[n] + de[j])
    return out


def weighted(values):
    corner = (values[0] + values[3]) + (values[12] + values[15])
    edge = ((values[1] + values[2]) + (values[4] + values[7])) + (
        (values[8] + values[11]) + (values[13] + values[14])
    )
    inner = (values[5] + values[6]) + (values[9] + values[10])
    return corner + 5.0 * edge + 25.0 * inner


def limited(g, jac, rden):
    mean = weighted([jac[n] * g[n] for n in range(16)]) * rden
    lows = list(g)
    while len(lows) > 1:
        lows = [jnp.minimum(lows[k], lows[k + 1]) for k in range(0, len(lows), 2)]
    low = lows[0]
    positive = jnp.maximum(mean, 0.0)
    negative = low < 0.0
    denominator = jnp.where(negative, positive - low, 1.0)
    scaling = jnp.where(negative, positive / denominator, 1.0)
    return [jac[n] * (mean + scaling * (g[n] - mean)) for n in range(16)]


def add_nodes(sums, edge, ey, c, sub, joins=(0,)):
    for j in range(4):
        c0, c1, c2, c3 = c[4 * j : 4 * j + 4]
        c0 = c0 + jnp.where(sub == 0, 0.0, roll(c3, 1))
        last = c3[7:8, :]
        y = 3 * ey + j
        if j in joins:
            c0, c1, c2 = (c0 + sums[y, 0], c1 + sums[y, 1], c2 + sums[y, 2])
            last = last + edge[pl.ds(y, 1), :]
        sums[y, 0] = c0
        sums[y, 1] = c1
        sums[y, 2] = c2
        edge[pl.ds(y, 1), :] = last


def clear_first(sums, edge, y=0):
    for ii in range(3):
        sums[y, ii] = jnp.zeros((8, 128), F32)
    edge[y : y + 1, :] = jnp.zeros((1, 128), F32)


def thin_messages(sums, edge, west, north, south):
    def copy(y, _):
        west[pl.ds(y, 1), :] = sums[y, 0, 0:1, :]
        return 0

    lax.fori_loop(0, 25, copy, 0, unroll=5)
    for out, y in ((north, 0), (south, 24)):
        for ii in range(3):
            out[8 * ii : 8 * ii + 8, :] = sums[y, ii]
        out[24:32, :] = row8(edge, y)


def place(corner):
    ey = (corner * 874) >> 16
    return 8 * ey + (((corner - 75 * ey) * 21846) >> 16)


def fill_places(nodes, spots):
    def body(e, _):
        spots[e] = place(nodes[0, e])
        return 0

    lax.fori_loop(0, 64, body, 0, unroll=8)


def first_kernel(
    corners, node_rows, x, vel, j_rows, sums, west, east, north, south, t0, send_one, send_two, u_ref, v_ref, rj_ref, j_ref, rd_ref,
    gathered, winds, jc, spots,
):
    step = pl.program_id(0)
    sub = sublane()
    lane = lax.broadcasted_iota(jnp.int32, (8, 128), 1)

    @pl.when(step == 0)
    def _():
        jc[...] = jnp.zeros_like(jc)
        fill_places(corners, spots)
        to = place(node_rows[0:1, :])
        hit = (lax.broadcasted_iota(jnp.int32, (64, 64), 0) == to).astype(F32)
        jc[:, 0:16] = lax.dot_general(
            hit, j_rows[...], (((1,), (1,)), ((), ())), precision=lax.Precision.HIGHEST, preferred_element_type=F32
        )

        def order(e, _):
            winds[spots[e]] = vel[e]
            return 0

        lax.fori_loop(0, 64, order, 0, unroll=8)
        flat = winds.reshape(1024, 128)

        def coef(ey, _):
            comp = jc[pl.ds(pl.multiple_of(8 * ey, 8), 8), :]
            js = []
            for n in range(16):
                jv = jnp.broadcast_to(comp[:, n : n + 1], (8, 128))
                w = flat[pl.ds(ey * 128 + n, 8, stride=16), :]
                wr = pltpu.roll(w, 64, 1)
                dj = STEP_SIZE * jv
                u_ref[n, ey] = dj * jnp.where(lane < 64, w, wr)
                v_ref[n, ey] = dj * jnp.where(lane < 64, wr, w)
                j_ref[n, ey] = jv
                rj_ref[n, ey] = 1.0 / jv
                js.append(jv)
            rd_ref[ey] = 1.0 / weighted(js)
            return 0

        lax.fori_loop(0, 8, coef, 0, unroll=4)

    def gather(e, _):
        gathered[spots[e]] = x[e]
        return 0

    lax.fori_loop(0, 64, gather, 0, unroll=16)
    flat = gathered.reshape(1024, 128)
    clear_first(sums, east)

    def rows(ey, _):
        f = [flat[pl.ds(ey * 128 + n, 8, stride=16), :] for n in range(16)]
        for n in range(16):
            t0[n, ey] = f[n]
        g = tendency_step(
            f, lambda n: u_ref[n, ey], lambda n: v_ref[n, ey], lambda n: rj_ref[n, ey]
        )
        c = limited(g, [j_ref[n, ey] for n in range(16)], rd_ref[ey])
        add_nodes(sums, east, ey, c, sub)
        return 0

    lax.fori_loop(0, 8, rows, 0, unroll=8)
    thin_messages(sums, east, west, north, south)
    for out in (west, east):
        for half in range(2):
            out[32 + 8 * half : 40 + 8 * half, :] = jc[
                pl.ds(pl.multiple_of(8 * (4 * half + step), 8), 8), :
            ]
    even = lax.axis_index("sfc") % 2 == 0
    send_one[...] = jnp.where(even, east[...], west[...])
    send_two[...] = jnp.where(even, west[...], east[...])


def own_geometry_kernel(own, from_e, from_w, inv):
    geometry_rows(own, from_e, from_w, None, None, None, inv, 0, 8)


def geometry_kernel(own, from_e, from_w, from_n, from_s, j_ref, inv):
    geometry_rows(own, from_e, from_w, from_n, from_s, j_ref, inv, -3, 11)


def geometry_rows(own, from_e, from_w, from_n, from_s, j_ref, inv, first, last):
    sub = sublane()

    def tile(ref, base, t):
        return ref[base : base + 8, 128 * t : 128 * t + 128]

    pending = None
    for r in range(first, last):
        if r < 0:
            t = r + 4
            a, b = (tile(from_n, 32, t), tile(from_n, 40, t))
        elif r > 7:
            t = r - 8
            a, b = (tile(from_s, 32, t), tile(from_s, 40, t))
        else:
            base, t = (32 + 8 * (r // 4), r % 4)
            a = tile(own, base, t)
            b = jnp.where(sub < 4, tile(from_e, base, t), tile(from_w, base, t))
        kept = None
        for j in range(4):
            ca = [jnp.broadcast_to(a[:, 4 * j + i : 4 * j + i + 1], (8, 128)) for i in range(4)]
            cb = [jnp.broadcast_to(b[:, 4 * j + i : 4 * j + i + 1], (8, 128)) for i in range(4)]
            if j_ref is not None and -2 <= r <= 9:
                for i in range(4):
                    j_ref[4 * j + i, r + 2, 0:8] = ca[i]
                    j_ref[4 * j + i, r + 2, 8:16] = cb[i]
            ra, rb = (roll(ca[3], 1), roll(cb[3], 1))
            row = [
                ca[0] + jnp.where(sub == 0, rb, ra),
                cb[0] + jnp.where(sub == 0, ra, rb),
                ca[1],
                cb[1],
                ca[2],
                cb[2],
            ]
            if j == 3:
                kept = row
                continue
            if j == 0 and pending is not None:
                row = [p + q for p, q in zip(row, pending)]
            y = 3 * r + j + 6
            if 0 <= y <= 36:
                for ii in range(3):
                    inv[y, ii, 0:8] = 1.0 / row[2 * ii]
                    inv[y, ii, 8:16] = 1.0 / row[2 * ii + 1]
        pending = kept


def node_values(sums, edge, from_e, from_w, inv, whole, side, first, last, sub):
    def body(y, _):
        whole[y, 0] = (sums[y, 0] + jnp.where(sub == 0, row8(from_w, y), 0.0)) * inv[y + 6, 0, 0:8]
        whole[y, 1] = sums[y, 1] * inv[y + 6, 1, 0:8]
        whole[y, 2] = sums[y, 2] * inv[y + 6, 2, 0:8]
        side[pl.ds(y, 1), :] = (edge[pl.ds(y, 1), :] + from_e[pl.ds(y, 1), :]) * inv[y + 6, 0, 8:9]
        return 0

    lax.fori_loop(first, last, body, 0, unroll=4)


def add_row(whole, side, msg, inv, y):
    for ii in range(3):
        whole[y, ii] = whole[y, ii] + msg[8 * ii : 8 * ii + 8, :] * inv[y + 6, ii, 0:8]
    side[y : y + 1, :] = side[y : y + 1, :] + msg[24:25, :] * inv[y + 6, 0, 8:9]


def element_values(whole, side, ey, sub):
    f = []
    for j in range(4):
        y = 3 * ey + j
        p0 = whole[y, 0]
        f += [p0, whole[y, 1], whole[y, 2], jnp.where(sub == 7, row8(side, y), roll(p0, 7))]
    return f


def stage_row(keep, take, whole, side, t0, u_ref, v_ref, rj_ref, j_ref, rd_ref, ey, sub):
    f = element_values(whole, side, ey, sub)
    h = tendency_step(f, lambda n: u_ref[n, ey], lambda n: v_ref[n, ey], lambda n: rj_ref[n, ey])
    g = [keep * t0[n, ey] + take * h[n] for n in range(16)]
    return limited(g, [j_ref[n, ey] for n in range(16)], rd_ref[ey])


def stage_inner_kernel(
    keep, take, sums, edge, from_e, from_w, inv, t0, u_ref, v_ref, rj_ref, j_ref, rd_ref, out, column, whole, side
):
    sub = sublane()
    node_values(sums, edge, from_e, from_w, inv, whole, side, 3, 22, sub)
    clear_first(out, column, 3)

    def rows(ey, _):
        c = stage_row(keep, take, whole, side, t0, u_ref, v_ref, rj_ref, j_ref, rd_ref, ey, sub)
        add_nodes(out, column, ey, c, sub)
        return 0

    lax.fori_loop(1, 7, rows, 0, unroll=6)


def stage_kernel(
    keep, take, wide, sums, edge, from_e, from_w, from_n, from_s, inv, t0, u_ref, v_ref, rj_ref, j_ref, rd_ref,
    inner, inner_column, out, west, east, third, fourth, whole, side,
):
    sub = sublane()
    node_values(sums, edge, from_e, from_w, inv, whole, side, 0, 4, sub)
    node_values(sums, edge, from_e, from_w, inv, whole, side, 21, 25, sub)
    add_row(whole, side, from_n, inv, 0)
    add_row(whole, side, from_s, inv, 24)
    column = fourth if wide else east

    def copy(y, _):
        for ii in range(3):
            out[y, ii] = inner[y, ii]
        column[pl.ds(y, 1), :] = inner_column[pl.ds(y, 1), :]
        return 0

    lax.fori_loop(3, 22, copy, 0, unroll=19)
    for ey, joins in ((0, (3,)), (7, (0,))):
        c = stage_row(keep, take, whole, side, t0, u_ref, v_ref, rj_ref, j_ref, rd_ref, ey, sub)
        add_nodes(out, column, ey, c, sub, joins)
    if not wide:
        thin_messages(out, column, west, third, fourth)
        return

    def pack(y, _):
        p0, p1, p2 = (out[y, 0], out[y, 1], out[y, 2])
        west[y] = jnp.where(sub < 3, p0, jnp.where(sub < 5, roll(p1, 3), roll(p2, 5)))
        east[y] = jnp.where(
            sub >= 6,
            p0,
            jnp.where(sub >= 4, roll(p1, -2), jnp.where(sub >= 2, roll(p2, -4), row8(column, y))),
        )
        return 0

    lax.fori_loop(0, 25, pack, 0, unroll=5)


def joined_row(sums, edge, from_e, from_w, y, sub):
    me, mw = (from_e[y], from_w[y])
    a0 = sums[y, 0] + jnp.where(sub == 0, mw, 0.0)
    b0 = jnp.where(sub == 0, row8(edge, y) + me, jnp.where(sub < 4, me, mw))
    b1 = jnp.where(sub < 4, roll(me, -3), roll(mw, 2))
    b2 = jnp.where(sub < 4, roll(me, -5), roll(mw, 4))
    return a0, sums[y, 1], sums[y, 2], b0, b1, b2


def rows_kernel(sums, edge, from_e, from_w, north, south):
    sub = sublane()
    for out, first in ((north, 0), (south, 18)):
        for k in range(7):
            a0, a1, a2, b0, b1, b2 = joined_row(sums, edge, from_e, from_w, first + k, sub)
            out[k, 0:8] = a0
            out[k, 8:16] = a1
            out[k, 16:24] = a2
            out[k, 24:32] = b0
            out[k, 32:40] = jnp.where((sub < 2) | (sub >= 6), b1, roll(b2, 4))


def laplace_core(f, jac, nonzero=range(4)):
    out = [None] * 16
    for j in nonzero:
        d = line(*[f(4 * j + i) for i in range(4)])
        out[4 * j : 4 * j + 4] = line(*[jac(4 * j + i) * d[i] for i in range(4)])
    for i in range(4):
        if len(nonzero) == 4:
            d = line(*[f(4 * j + i) for j in range(4)])
        else:
            (k,) = nonzero
            d = [float(D[j, k]) * f(4 * k + i) for j in range(4)]
        d = line(*[jac(4 * j + i) * d[j] for j in range(4)])
        for j in range(4):
            n = 4 * j + i
            out[n] = d[j] if out[n] is None else out[n] + d[j]
    return out


FIRST, JOIN, SKIP = range(3)


def laplace_row(src, j_ref, inv, dst, r, top, bottom, sub, at=(0, 0), narrow=False, only=range(4), nonzero=range(4)):
    fa, fb = ([None] * 16, [None] * 16)
    for j in nonzero:
        y = 3 * r + j - at[0]
        pa, pb = (src[y, 0, 0:8], src[y, 0, 8:16])
        ra, rb = (roll(pa, 7), roll(pb, 7))
        fa[4 * j : 4 * j + 4] = [pa, src[y, 1, 0:8], src[y, 2, 0:8], jnp.where(sub == 7, rb, ra)]
        fb[4 * j : 4 * j + 4] = [pb, src[y, 1, 8:16], src[y, 2, 8:16], jnp.where(sub == 7, ra, rb)]
    ca = laplace_core(lambda n: fa[n], lambda n: j_ref[n, r, 0:8], nonzero)
    cb = laplace_core(lambda n: fb[n], lambda n: j_ref[n, r, 8:16], nonzero)
    for j in range(4):
        what = {0: top, 3: bottom}.get(j)
        if what == SKIP or j not in only:
            continue
        y = 3 * r + j
        ra, rb = (roll(ca[4 * j + 3], 1), roll(cb[4 * j + 3], 1))
        row = [
            (ca[4 * j] + jnp.where(sub == 0, rb, ra), cb[4 * j] + jnp.where(sub == 0, ra, rb)),
            (ca[4 * j + 1], cb[4 * j + 1]),
            (ca[4 * j + 2], cb[4 * j + 2]),
        ]
        z = y - at[1]
        for ii in range(3):
            for part, rows in zip(row[ii], (slice(0, 8), slice(8, 16))):
                if narrow and ii and rows.start:
                    continue
                if what == JOIN:
                    part = part + dst[z, ii, rows]
                if what != FIRST:
                    part = part * inv[y, ii, rows]
                dst[z, ii, rows] = part


def own_rows(sums, edge, from_e, from_w, inv, field, first, last, sub):
    def body(y, _):
        a0, a1, a2, b0, b1, b2 = joined_row(sums, edge, from_e, from_w, y, sub)
        for ii, (a, b) in enumerate(((a0, b0), (a1, b1), (a2, b2))):
            field[y, ii, 0:8] = a * inv[y + 6, ii, 0:8]
            field[y, ii, 8:16] = b * inv[y + 6, ii, 8:16]
        return 0

    lax.fori_loop(first, last, body, 0)


def inner_kernel(sums, edge, from_e, from_w, j_ref, inv, field, ends, two, one):
    sub = sublane()
    own_rows(sums, edge, from_e, from_w, inv, field, 0, 25, sub)
    for src, dst, narrow in ((field, one, False), (one, two, True)):

        def rows(r, _, src=src, dst=dst, narrow=narrow):
            laplace_row(src, j_ref, inv, dst, r, JOIN, FIRST, sub, (6, 6), narrow)
            return 0

        laplace_row(src, j_ref, inv, dst, 2, None, FIRST, sub, (6, 6), narrow)
        lax.fori_loop(3, 9, rows, 0, unroll=3)
        laplace_row(src, j_ref, inv, dst, 9, JOIN, None, sub, (6, 6), narrow)
    for ii in range(3):
        ends[0, ii] = one[0, ii]
        ends[1, ii] = one[24, ii]


def last_kernel(
    nodes, from_n, from_s, j_ref, inv, field_in, ends, two_in, out, field, one, two, beyond, spread, spots
):
    sub = sublane()

    @pl.when(pl.program_id(0) == 0)
    def _():
        fill_places(nodes, spots)

    def copy_rows(src, dst, first, last):
        def body(y, _):
            for ii in range(3):
                dst[y, ii] = src[y - first, ii]
            return 0

        lax.fori_loop(first, last, body, 0, unroll=4)

    copy_rows(field_in, field, 6, 31)
    for msg, first, shared in ((from_n, 0, 6), (from_s, 30, 0)):
        for k in range(7):
            y = first + k
            c = msg[k, 32:40]
            parts = [msg[k, 0:8], msg[k, 24:32], msg[k, 8:16], c, msg[k, 16:24], roll(c, 4)]
            for ii in range(3):
                a, b = (parts[2 * ii] * inv[y, ii, 0:8], parts[2 * ii + 1] * inv[y, ii, 8:16])
                if k == shared:
                    beyond[y // 30, ii, 0:8] = a
                    beyond[y // 30, ii, 8:16] = b
                    a, b = (a + field[y, ii, 0:8], b + field[y, ii, 8:16])
                field[y, ii, 0:8] = a
                field[y, ii, 8:16] = b
    def row(src, dst, r, top, bottom, **more):
        laplace_row(src, j_ref, inv, dst, r, top, bottom, sub, **more)

    row(field, one, 0, SKIP, FIRST, only=(3,))
    row(field, one, 1, JOIN, FIRST)
    row(beyond, one, 2, JOIN, None, at=(6, 0), nonzero=(0,))
    row(beyond, one, 9, None, FIRST, at=(29, 0), nonzero=(3,))
    row(field, one, 10, JOIN, FIRST)
    row(field, one, 11, JOIN, SKIP, only=(0,))
    row(one, two, 2, FIRST, FIRST, narrow=True)
    row(one, two, 3, JOIN, None, narrow=True, nonzero=(0,))
    row(one, two, 8, None, FIRST, narrow=True, nonzero=(3,))
    row(one, two, 9, JOIN, FIRST, narrow=True)
    for ii in range(3):
        one[6, ii] = one[6, ii] + ends[0, ii]
        one[30, ii] = one[30, ii] + ends[1, ii]
    row(one, two, 1, SKIP, JOIN, narrow=True, only=(3,))
    row(one, two, 10, JOIN, SKIP, narrow=True, only=(0,))
    for y in (*range(6, 13), *range(24, 31)):
        two[y, 0] = two[y, 0] + two_in[y - 6, 0]
        for ii in (1, 2):
            two[y, ii, 0:8] = two[y, ii, 0:8] + two_in[y - 6, ii, 0:8]
    for y in range(13, 24):
        two[y, 0] = two_in[y - 6, 0]
        for ii in (1, 2):
            two[y, ii, 0:8] = two_in[y - 6, ii, 0:8]
    flat = spread.reshape(1024, 128)

    def finish(ey, _):
        for j in range(4):
            y = 3 * ey + j + 6
            p0 = field[y, 0, 0:8] - DIFFUSION * two[y, 0, 0:8]
            q0 = field[y, 0, 8:16] - DIFFUSION * two[y, 0, 8:16]
            vals = [
                p0,
                field[y, 1, 0:8] - DIFFUSION * two[y, 1, 0:8],
                field[y, 2, 0:8] - DIFFUSION * two[y, 2, 0:8],
                jnp.where(sub == 7, roll(q0, 7), roll(p0, 7)),
            ]
            for i in range(4):
                flat[pl.ds(ey * 128 + 4 * j + i, 8, stride=16), :] = vals[i]
        return 0

    lax.fori_loop(0, 8, finish, 0, unroll=8)

    def scatter(e, _):
        out[e] = spread[spots[e]]
        return 0

    lax.fori_loop(0, 64, scatter, 0, unroll=16)


def sds(*shape):
    return jax.ShapeDtypeStruct(shape, F32)


def tiled(*shape):
    zeros = (0,) * (len(shape) - 1)
    return pl.BlockSpec(shape, lambda t: zeros + (t,))


def fixed(*shape):
    zeros = (0,) * len(shape)
    return pl.BlockSpec(shape, lambda t: zeros)


PARAMS = pltpu.CompilerParams(vmem_limit_bytes=VMEM_LIMIT, dimension_semantics=("arbitrary",))
SMEM = pl.BlockSpec(memory_space=pltpu.SMEM)


def swapped(before, after, distance, sends=None):
    size = lax.axis_size("sfc")
    even = (lax.axis_index("sfc") // distance) % 2 == 0
    up = [(i, (i + distance) % size) for i in range(size) if (i // distance) % 2 == 0]
    over = [(i, (i + distance) % size) for i in range(size) if (i // distance) % 2 == 1]
    if sends is None:
        sends = (jnp.where(even, after, before), jnp.where(even, before, after))
    one = lax.ppermute(sends[0], "sfc", up + [(j, i) for i, j in up])
    two = lax.ppermute(sends[1], "sfc", over + [(j, i) for i, j in over])
    return jnp.where(even, two, one), jnp.where(even, one, two)


def per_device(tracers, velocity, jacobian, elem_nodes):
    nodes = elem_nodes.T
    coef = [sds(16, 8, 8, 128)] * 4 + [sds(8, 8, 128)]
    coef_specs = [fixed(16, 8, 8, 128)] * 4 + [fixed(8, 8, 128)]
    sums_spec = tiled(27, 3, 8, 128)
    first = pl.pallas_call(
        first_kernel,
        grid=(4,),
        in_specs=[SMEM, fixed(16, 64), tiled(64, 16, 128), fixed(64, 16, 128), fixed(16, 64)],
        out_specs=[sums_spec, tiled(48, 128), tiled(48, 128), tiled(32, 128), tiled(32, 128), tiled(16, 8, 8, 128), tiled(48, 128), tiled(48, 128)]
        + coef_specs,
        out_shape=[sds(27, 3, 8, 512), sds(48, 512), sds(48, 512), sds(32, 512), sds(32, 512), sds(16, 8, 8, 512), sds(48, 512), sds(48, 512)]
        + coef,
        scratch_shapes=[
            pltpu.VMEM((64, 16, 128), F32),
            pltpu.VMEM((64, 16, 128), F32),
            pltpu.VMEM((64, 128), F32),
            pltpu.SMEM((64,), jnp.int32),
        ],
        compiler_params=pltpu.CompilerParams(vmem_limit_bytes=FIRST_LIMIT, dimension_semantics=("arbitrary",)),
        name="section_one_sums",
    )
    sums, west, east, north, south, t0, send_one, send_two, *coefs = first(nodes, nodes, tracers, velocity, jacobian.T)

    row = lax.broadcasted_iota(jnp.int32, (32, 1), 0)

    def corrected(own, from_w, from_e, y):
        return own + jnp.where(row == 0, from_w[y : y + 1], 0.0) + jnp.where(row >= 24, from_e[y : y + 1], 0.0)

    from_w, from_e = swapped(west, east, 1, (send_one, send_two))
    low = lax.broadcasted_iota(jnp.int32, (8, 1), 0) < 4
    beside = [jnp.where(low, from_e[k : k + 8], from_w[k : k + 8]) for k in (32, 40)]
    msg_n = jnp.concatenate([corrected(north, from_w, from_e, 0), west[32:40], beside[0]])
    msg_s = jnp.concatenate([corrected(south, from_w, from_e, 24), west[40:48], beside[1]])
    from_n, from_s = swapped(msg_n, msg_s, PX)

    whole = pl.BlockSpec(memory_space=pltpu.VMEM)
    inv_inner = pl.pallas_call(
        own_geometry_kernel,
        in_specs=[whole] * 3,
        out_specs=whole,
        out_shape=sds(37, 3, 16, 128),
        compiler_params=pltpu.CompilerParams(vmem_limit_bytes=VMEM_LIMIT),
        name="inner_geometry",
    )(west, from_e, from_w)
    jac, inv = pl.pallas_call(
        geometry_kernel,
        in_specs=[whole] * 5,
        out_specs=[whole] * 2,
        out_shape=[sds(16, 12, 16, 128), sds(37, 3, 16, 128)],
        compiler_params=pltpu.CompilerParams(vmem_limit_bytes=VMEM_LIMIT),
        name="geometry",
    )(west, from_e, from_w, from_n, from_s)
    jac_spec, inv_spec = (fixed(16, 12, 16, 128), fixed(37, 3, 16, 128))

    def inner_stage(keep, take, sums, edge, from_e, from_w, inv, rows):
        return pl.pallas_call(
            functools.partial(stage_inner_kernel, keep, take),
            grid=(4,),
            in_specs=[sums_spec] + [tiled(rows, 128)] * 3 + [inv_spec, tiled(16, 8, 8, 128)] + coef_specs,
            out_specs=[sums_spec, tiled(32, 128)],
            out_shape=[sds(27, 3, 8, 512), sds(32, 512)],
            scratch_shapes=[pltpu.VMEM((27, 3, 8, 128), F32), pltpu.VMEM((32, 128), F32)],
            compiler_params=PARAMS,
            cost_estimate=pl.CostEstimate(
                flops=64 * 16 * 512 * 60, bytes_accessed=8 * 1024 * 1024, transcendentals=0
            ),
            name="inner_rows",
        )(sums, edge, from_e, from_w, inv, t0, *coefs)

    def stage(keep, take, wide, sums, edge, from_e, from_w, from_n, from_s, rows, inner):
        if wide:
            outs = [sds(25, 8, 512), sds(25, 8, 512), sds(8, 512), sds(32, 512)]
            specs = [tiled(25, 8, 128), tiled(25, 8, 128), tiled(8, 128), tiled(32, 128)]
        else:
            outs = [sds(32, 512)] * 4
            specs = [tiled(32, 128)] * 4
        return pl.pallas_call(
            functools.partial(stage_kernel, keep, take, wide),
            grid=(4,),
            in_specs=[sums_spec]
            + [tiled(rows, 128)] * 5
            + [inv_spec, tiled(16, 8, 8, 128)]
            + coef_specs
            + [sums_spec, tiled(32, 128)],
            out_specs=[sums_spec] + specs,
            out_shape=[sds(27, 3, 8, 512)] + outs,
            scratch_shapes=[pltpu.VMEM((27, 3, 8, 128), F32), pltpu.VMEM((32, 128), F32)],
            compiler_params=PARAMS,
            name="section_three_sums" if wide else "section_two_sums",
        )(sums, edge, from_e, from_w, from_n, from_s, inv, t0, *coefs, *inner)

    inner = inner_stage(0.75, 0.25, sums, east, from_e, from_w, inv_inner, 48)
    sums, west, east, north, south = stage(
        0.75, 0.25, False, sums, east, from_e, from_w, from_n, from_s, 48, inner
    )
    from_w, from_e = swapped(west, east, 1)
    msg_n = corrected(north, from_w, from_e, 0)
    msg_s = corrected(south, from_w, from_e, 24)
    from_n, from_s = swapped(msg_n, msg_s, PX)

    inner = inner_stage(1.0 / 3.0, 2.0 / 3.0, sums, east, from_e, from_w, inv, 32)
    sums, west, east, _, edge = stage(
        1.0 / 3.0, 2.0 / 3.0, True, sums, east, from_e, from_w, from_n, from_s, 32, inner
    )
    from_w, from_e = swapped(west, east, 1)
    message = tiled(25, 8, 128)
    band = tiled(7, 40, 128)
    msg_n, msg_s = pl.pallas_call(
        rows_kernel,
        grid=(4,),
        in_specs=[sums_spec, tiled(32, 128), message, message],
        out_specs=[band, band],
        out_shape=[sds(7, 40, 512)] * 2,
        compiler_params=PARAMS,
        name="row_bands",
    )(sums, edge, from_e, from_w)
    from_n, from_s = swapped(msg_n, msg_s, PX)
    grown = [(25, 3, 16), (2, 3, 16), (25, 3, 16)]
    flops = 64 * 16 * 512 * 60
    field, ends, two = pl.pallas_call(
        inner_kernel,
        grid=(4,),
        in_specs=[sums_spec, tiled(32, 128), message, message, jac_spec, inv_spec],
        out_specs=[tiled(*g, 128) for g in grown],
        out_shape=[sds(*g, 512) for g in grown],
        scratch_shapes=[pltpu.VMEM((25, 3, 16, 128), F32)],
        compiler_params=PARAMS,
        cost_estimate=pl.CostEstimate(flops=flops, bytes_accessed=16 * 1024 * 1024, transcendentals=0),
        name="biharmonic_inner_rows",
    )(sums, edge, from_e, from_w, jac, inv)
    return pl.pallas_call(
        last_kernel,
        grid=(4,),
        in_specs=[SMEM, band, band, jac_spec, inv_spec] + [tiled(*g, 128) for g in grown],
        out_specs=tiled(64, 16, 128),
        out_shape=sds(64, 16, 512),
        scratch_shapes=[pltpu.VMEM((37, 3, 16, 128), F32)] * 3
        + [pltpu.VMEM((2, 3, 16, 128), F32), pltpu.VMEM((64, 16, 128), F32), pltpu.SMEM((64,), jnp.int32)],
        compiler_params=PARAMS,
        name="biharmonic_outer_rows",
    )(nodes, from_n, from_s, jac, inv, field, ends, two)


def solution(mesh):
    in_specs = (P("sfc", None, None), P("sfc", None, None), P("sfc", None), P("sfc", None))
    out_specs = P("sfc", None, None)
    return jax.shard_map(
        per_device, mesh=mesh, in_specs=in_specs, out_specs=out_specs, check_vma=False
    )
```
